128 devices in a mesh: dp: 8 (over x_hi, y), vocab: 16 (over x_lo, z, core).
Axes of the slice: x: 4 (x_hi: 2, x_lo: 2; x = x_hi * 2 + x_lo), y: 4, z: 4, core: 2. Of those that a mesh axis runs over, the one named last changes fastest.
Arguments:
- hidden: bfloat16 [8192, 4096], P('dp', 'vocab'), may hold values from -6 to 6
- norm_gain: float32 [4096], replicated, may hold values from 0.5 to 3
- head_weight: bfloat16 [4096, 16000], P(None, 'vocab')
- lengths: int32 [64], P('dp'), may hold values from 16 to 128
- positives: int32 [16], P('dp'), may hold values from 0 to 47
- negatives: int32 [16, 2], P('dp'), may hold values from 0 to 47
Outputs:
- losses: float32 [3], replicated
- hidden_grad: bfloat16 [8192, 4096], P('dp', 'vocab')
- head_grad: bfloat16 [4096, 16000], P('dp', 'vocab')
- gain_grad: float32 [4096], P('vocab')
The draws below stay inside these ranges and needn't reach their ends.
All inputs are finite; a program needn't handle non-finite values.
Results may differ from the reference program's by a relative error of at most 0.025.
Values may be sent and summed in bfloat16 or wider, within the bound.
No kernel may reach another device: no remote copies, remote signals or barrier semaphores. Data moves between devices by JAX's collectives and lax.ppermute only.
A program may use at most 128 MiB of HBM per device.

```python
import math
import jax
import jax.numpy as jnp
from jax import lax

D = 4096
VOCAB = 16000
SEQ_LEN = 128
NEG = 2
QRY_DP = 2
PSG_DP = 6
SEQ_DP = 8
NQRY = 16
NPSG = 48
NSEQ = 64
TOKENS = 8192
N_DP = 8
N_VOCAB = 16


def draw_norm_gain(key, part):
    key = jax.random.fold_in(key, 11)
    drawn = jax.random.uniform(key, (D,), jnp.float32, 0.5, 2.0)
    return drawn


def draw_head_weight(key, part):
    key = jax.random.fold_in(key, 37)
    entry_key, column_key = jax.random.split(key, 2)
    place = jnp.arange(VOCAB, dtype=jnp.float32) / VOCAB
    entries = jax.random.truncated_normal(entry_key, -4.0, 4.0, (D, VOCAB), jnp.float32)
    rough = jnp.exp(jax.random.uniform(column_key, (VOCAB,), jnp.float32, -0.35, 0.35))
    column_scale = 0.4 * jnp.exp(1.386 * place) * rough
    drawn = entries * column_scale[None, :] / jnp.sqrt(jnp.float32(D))
    return drawn.astype(jnp.bfloat16)


def draw_lengths(key, part):
    key = jax.random.fold_in(key, 23)
    first_key, second_key, third_key = jax.random.split(key, 3)
    drawn = jax.random.randint(first_key, (NSEQ,), SEQ_LEN // 8, SEQ_LEN + 1)
    longest = jax.random.randint(second_key, (), 0, NSEQ)
    shortest = (longest + 1 + jax.random.randint(third_key, (), 0, NSEQ - 1)) % NSEQ
    places = jnp.arange(NSEQ)
    drawn = jnp.where(places == longest, SEQ_LEN, drawn)
    drawn = jnp.where(places == shortest, SEQ_LEN // 8, drawn)
    return drawn.astype(jnp.int32)


def place_ends(result, key, least, largest):
    longest = result.shape.index(max(result.shape))
    spots = []
    for shift in (0, 1):
        where = [jax.random.randint(jax.random.fold_in(key, axis), (), 0, length) for axis, length in enumerate(result.shape)]
        where[longest] = (where[longest] + shift) % result.shape[longest]
        spots.append(tuple(where))
    return result.at[spots[0]].set(least).at[spots[1]].set(largest)


def steps_of(own_key, dims, shards, least, high):
    loudness, own = 1.0, jax.random.fold_in(own_key, 6)
    for axis_at, parts in shards:
        heights = jnp.exp(jax.random.uniform(jax.random.fold_in(own, axis_at), (parts,), jnp.float32, least / len(shards), high / len(shards)))
        loudness = loudness * jnp.repeat(heights, dims[axis_at] // parts).reshape([-1 if axis == axis_at else 1 for axis in range(len(dims))])
    return loudness


def noise(stream_key, dims, spread, most, cuts=(), kind=jnp.bfloat16):
    loudness = steps_of(stream_key, dims, cuts, -0.22, 0.18) if cuts else 1.0
    values = jax.random.normal(stream_key, dims, jnp.float32) * spread * loudness
    return jnp.minimum(jnp.maximum(values, -most), most).astype(kind)


def setup_inputs(seed: int = 0) -> dict:
    keys = jax.random.split(jax.random.key(seed), 7)
    return {
        "hidden": noise(keys[0], (TOKENS, D), 1.0, 6.0, ((0, 8), (1, 16))),
        "norm_gain": draw_norm_gain(jax.random.fold_in(keys[6], 71), 0),
        "head_weight": draw_head_weight(jax.random.fold_in(keys[6], 71), 0),
        "lengths": draw_lengths(jax.random.fold_in(keys[6], 71), 0),
        "positives": place_ends(jax.random.randint(keys[4], (NQRY,), 0, NPSG), jax.random.fold_in(keys[4], 1), 0, NPSG - 1).astype(jnp.int32),
        "negatives": place_ends(jax.random.randint(keys[5], (NQRY, NEG), 0, NPSG), jax.random.fold_in(keys[5], 1), 0, NPSG - 1).astype(jnp.int32),
    }


epsilon = 1e-05
sharpness = 80.0
flops_weight = 0.01

def contrast(scores, positive_ids, negative_ids):
    query_count = scores.shape[0]
    passage_count = scores.shape[1]
    negative_count = negative_ids.shape[1]
    columns = jnp.arange(passage_count, dtype=jnp.int32)
    positive_hot = (columns[None, :] == positive_ids[:, None]).astype(jnp.float32)
    negative_hot = (columns[None, None, :] == negative_ids[:, :, None]).astype(jnp.float32)
    highest = lax.optimization_barrier(jnp.max(scores, axis=1, keepdims=True))
    shifted = jnp.exp(scores - highest)
    denominator = lax.optimization_barrier(jnp.sum(shifted, axis=1, keepdims=True))
    log_total = highest[:, 0] + jnp.log(denominator[:, 0])
    positive_score = lax.optimization_barrier(jnp.sum(scores * positive_hot, axis=1))
    negative_score = lax.optimization_barrier(jnp.sum(scores[:, None, :] * negative_hot, axis=2))
    margins = negative_score - positive_score[:, None]
    cross_loss = jnp.mean(log_total - positive_score)
    margin_loss = jnp.mean(jax.nn.softplus(margins))
    slopes = jax.nn.sigmoid(margins) / (query_count * negative_count)
    score_grad = (shifted / denominator - positive_hot) / query_count
    score_grad = score_grad + lax.optimization_barrier(jnp.sum(slopes[:, :, None] * negative_hot, axis=1))
    score_grad = score_grad - lax.optimization_barrier(jnp.sum(slopes, axis=1))[:, None] * positive_hot
    return (cross_loss, margin_loss, score_grad)

def pool_block(logits, valid):
    seq_count = valid.shape[0]
    activity = jnp.log1p(jnp.maximum(logits, 0.0))
    per_sequence = activity.reshape(seq_count, -1, logits.shape[1])
    valid_cells = valid[:, :, None]
    peak_value = lax.optimization_barrier(jnp.max(jnp.where(valid_cells, per_sequence, 0.0), axis=1, keepdims=True))
    raised = jnp.where(valid_cells, jnp.exp(sharpness * (per_sequence - peak_value)), 0.0)
    summed = lax.optimization_barrier(jnp.sum(raised, axis=1, keepdims=True))
    pooled = peak_value[:, 0, :] + jnp.log(summed[:, 0, :]) / sharpness
    return (pooled, raised / summed)

def logit_gradient(logits, weights, rep_grad):
    derivative = jnp.where(logits > 0.0, 1.0 / (1.0 + jnp.maximum(logits, 0.0)), 0.0)
    spread_grad = (rep_grad[:, None, :] * weights).reshape(logits.shape)
    return (spread_grad * derivative).astype(jnp.bfloat16)

def reference(hidden, norm_gain, head_weight, lengths, positives, negatives):
    values = hidden.astype(jnp.float32)
    inverse = lax.rsqrt(lax.optimization_barrier(jnp.mean(values * values, axis=1, keepdims=True)) + epsilon)
    unit_rows = values * inverse
    normed = (unit_rows * norm_gain).astype(jnp.bfloat16)
    valid = jnp.arange(SEQ_LEN, dtype=jnp.int32)[None, :] < lengths[:, None]
    block_width = VOCAB // N_VOCAB
    weight_blocks = head_weight.reshape(D, N_VOCAB, block_width).transpose(1, 0, 2)

    def forward_block(block):
        logits = jnp.dot(normed, block, preferred_element_type=jnp.float32)
        return pool_block(logits, valid)[0]
    pooled = lax.map(forward_block, weight_blocks).transpose(1, 0, 2).reshape(NSEQ, VOCAB)
    grouped = pooled.reshape(N_DP, SEQ_DP, VOCAB)
    queries = grouped[:, :QRY_DP].reshape(NQRY, VOCAB)
    passages = grouped[:, QRY_DP:].reshape(NPSG, VOCAB)
    score_scale = 4.0 / math.sqrt(VOCAB)
    scores = score_scale * jnp.dot(queries, passages.T, precision=lax.Precision.HIGHEST)
    mean_rep = lax.optimization_barrier(jnp.mean(pooled, axis=0))
    cross_loss, margin_loss, score_grad = contrast(scores, positives, negatives)
    flops_loss = flops_weight * jnp.sum(mean_rep * mean_rep)
    losses = jnp.stack([cross_loss, margin_loss, flops_loss])
    query_grad = score_scale * jnp.dot(score_grad, passages, precision=lax.Precision.HIGHEST)
    passage_grad = score_scale * jnp.dot(score_grad.T, queries, precision=lax.Precision.HIGHEST)
    rep_grad = jnp.concatenate([query_grad.reshape(N_DP, QRY_DP, VOCAB), passage_grad.reshape(N_DP, PSG_DP, VOCAB)], axis=1).reshape(NSEQ, VOCAB)
    rep_grad = rep_grad + 2.0 * flops_weight / NSEQ * mean_rep[None, :]
    grad_blocks = rep_grad.reshape(NSEQ, N_VOCAB, block_width).transpose(1, 0, 2)

    def backward_block(carried, inputs):
        block, block_grad = inputs
        logits = jnp.dot(normed, block, preferred_element_type=jnp.float32)
        weights = pool_block(logits, valid)[1]
        local_grad = logit_gradient(logits, weights, block_grad)
        head_block = lax.dot_general(normed, local_grad, (((0,), (0,)), ((), ())), preferred_element_type=jnp.float32)
        term_grad = lax.dot_general(local_grad, block, (((1,), (1,)), ((), ())), preferred_element_type=jnp.float32)
        term_rounded = lax.optimization_barrier(term_grad.astype(jnp.bfloat16)).astype(jnp.float32)
        carried = carried + term_rounded
        return (carried, head_block.astype(jnp.bfloat16))
    normed_grad, head_blocks = lax.scan(backward_block, jnp.zeros((TOKENS, D), jnp.float32), (weight_blocks, grad_blocks))
    head_grad = head_blocks.transpose(1, 0, 2).reshape(D, VOCAB)
    scaled_grad = normed_grad * norm_gain
    gain_grad = lax.optimization_barrier(jnp.sum(normed_grad * unit_rows, axis=0))
    row_dot = lax.optimization_barrier(jnp.sum(scaled_grad * unit_rows, axis=1, keepdims=True)) / D
    hidden_grad = (inverse * (scaled_grad - unit_rows * row_dot)).astype(jnp.bfloat16)
    return (losses, hidden_grad, head_grad, gain_grad)
```

```python
import functools
import math

import jax
import jax.numpy as jnp
from jax import lax
from jax.experimental import pallas as pl
from jax.experimental.pallas import tpu as pltpu
from jax.sharding import Mesh, PartitionSpec as P

VOCAB = 16000
D = 4096
epsilon = 1e-05
sharpness = 80.0
flops_weight = 0.01

TOK = 1024
SEQ = 8
LEN = 128
TERMS = 1000
BLK = 256
ROWS_A = 640
ROWS_B = TERMS - ROWS_A
HALF = TOK // 2
PER = 2
SHORT = 8
SCORE_SCALE = 4.0 / math.sqrt(VOCAB)
COLS = ((0, 256), (256, 512), (512, 768), (768, 1000))
SIZES = {"xh": 2, "y": 4, "xl": 2, "z": 4, "c": 2}
VMEM_LIMIT = 56 * 1024 * 1024
HIGHEST = lax.Precision.HIGHEST

f32, bf16 = jnp.float32, jnp.bfloat16


def shift(x, axis, step):
    n = SIZES[axis]
    return lax.ppermute(x, axis, [(i, (i + step) % n) for i in range(n)])


def swap(x, axis, bits=1):
    return lax.ppermute(x, axis, [(i, i ^ bits) for i in range(SIZES[axis])])


def params(**more):
    return pltpu.CompilerParams(vmem_limit_bytes=VMEM_LIMIT, **more)


def cost(flops, moved):
    return pl.CostEstimate(flops=int(flops / SHORT), bytes_accessed=int(moved / SHORT), transcendentals=0)


def tag(ids, pooled_ref):
    lane = lax.broadcasted_iota(jnp.int32, (1, 24), 1)
    for k in range(SEQ):
        tags = jnp.zeros((1, 24), f32)
        if k < 2:
            tags = jnp.where(lane == 0, ids[8 + k].astype(f32), tags)
            tags = jnp.where(lane == 1, ids[10 + 2 * k].astype(f32), tags)
            tags = jnp.where(lane == 2, ids[11 + 2 * k].astype(f32), tags)
        pooled_ref[k : k + 1, TERMS:] = tags


def pool(lengths, first, acc, ssq, inv_ref, weight_ref, pooled_ref):
    for s in range(acc.shape[0] // LEN):
        k = first + s
        rows = slice(s * LEN, (s + 1) * LEN)
        total = jnp.sum(ssq[rows, :], axis=1, keepdims=True)
        inverse = lax.rsqrt(total / D + epsilon)
        inv_ref[rows, :] = inverse
        count = lengths[k]
        for a, b in COLS:
            logits = acc[rows, a:b] * inverse
            valid = lax.broadcasted_iota(jnp.int32, (LEN, b - a), 0) < count
            held = jnp.where(valid, 1.0 + jnp.maximum(logits, 0.0), 1.0)
            top = jnp.max(held, axis=0, keepdims=True)
            down = 1.0 / top
            r1 = held * down
            r2 = r1 * r1
            r4 = r2 * r2
            r8 = r4 * r4
            r16 = r8 * r8
            r32 = r16 * r16
            r79 = (r32 * r32 * r8) * (r4 * (r2 * r1))
            summed = jnp.sum(jnp.where(valid, r79 * r1, 0.0), axis=0, keepdims=True)
            pooled_ref[pl.ds(k, 1), a:b] = jnp.log(top) + jnp.log(summed) / sharpness
            slope = r79 * (down / summed) * inverse
            weight_ref[rows, a:b] = jnp.where(valid & (logits > 0.0), slope, 0.0).astype(bf16)


def chip_of(ids, far_x, step):
    return (ids[2] ^ far_x) * 4 + ((ids[3] + step) & 3)


def block_at(ids, chip, side):
    return pl.ds(pl.multiple_of((chip * 2 + (ids[4] ^ side)) * BLK, BLK), BLK)


def scaled(weights, gain, ids, chip):
    row = jnp.concatenate([gain[:, block_at(ids, chip, side)] for side in range(2)], axis=1)
    return (weights.astype(f32) * row).astype(bf16)


def folded_squares(lefts):
    squares = 0.0
    for left in lefts:
        value = left.astype(f32)
        square = value * value
        squares = squares + square[:, :128] + square[:, 128:]
    return squares


def forward_kernel(places, first, ids, *refs):
    nb = len(places)
    arrays, (weights, gain), refs = refs[: 2 * nb], refs[2 * nb : 2 * nb + 2], refs[2 * nb + 2 :]
    if not first:
        (acc_in, ssq_in, _), refs = refs[:3], refs[3:]
    acc, ssq, kept, held, w_sem, x_sem = refs
    chips = [chip_of(ids, *place) for place in places]
    loads, saves = [], []
    for j in range(nb):
        for side in range(2):
            at = held.at[j, :, side * BLK : (side + 1) * BLK]
            loads.append(pltpu.make_async_copy(weights.at[:, block_at(ids, chips[j], side)], at, w_sem.at[j, side]))
            loads[-1].start()
    for j in range(nb):
        for side in range(2):
            saves.append(pltpu.make_async_copy(arrays[2 * j + side], kept.at[chips[j], side], x_sem.at[j, side]))
            saves[-1].start()
    for j in range(nb):
        loads[2 * j].wait()
        loads[2 * j + 1].wait()
        right = scaled(held[j], gain, ids, chips[j])
        for half in range(2):
            rows = slice(half * HALF, (half + 1) * HALF)
            lefts = [arrays[2 * j + side][rows, :] for side in range(2)]
            squares = folded_squares(lefts)
            product = lax.dot_general(
                jnp.concatenate(lefts, axis=1), right, (((1,), (1,)), ((), ())), preferred_element_type=f32
            )
            if j == 0 and first:
                acc[rows, :] = product
                ssq[rows, :] = squares
            elif j == 0:
                acc[rows, :] = acc_in[rows, :] + product
                ssq[rows, :] = ssq_in[rows, :] + squares
            else:
                acc[rows, :] += product
                ssq[rows, :] += squares
    for copy in saves:
        copy.wait()


SMEM = pl.BlockSpec(memory_space=pltpu.SMEM)
VMEM = pl.BlockSpec(memory_space=pltpu.VMEM)
ANY = pl.BlockSpec(memory_space=pl.ANY)


STATE = [
    jax.ShapeDtypeStruct((TOK, TERMS), f32),
    jax.ShapeDtypeStruct((TOK, 128), f32),
    jax.ShapeDtypeStruct((8, 2, TOK, BLK), bf16),
]


def forward(ids, places, arrays, weights, gain, state=()):
    nb = len(places)
    base = 3 + len(arrays)
    return pl.pallas_call(
        functools.partial(forward_kernel, places, not state),
        out_shape=STATE,
        in_specs=[SMEM] + [VMEM] * len(arrays) + [ANY, VMEM] + [VMEM, VMEM, ANY][: len(state)],
        out_specs=[VMEM, VMEM, ANY],
        scratch_shapes=[
            pltpu.VMEM((nb, TERMS, 2 * BLK), bf16),
            pltpu.SemaphoreType.DMA((nb, 2)),
            pltpu.SemaphoreType.DMA((nb, 2)),
        ],
        input_output_aliases={base + i: i for i in range(len(state))},
        compiler_params=params(),
        cost_estimate=cost(2 * nb * TOK * 512 * TERMS, nb * 3_000_000 + 8_000_000),
        name="forward_part",
    )(ids, *arrays, weights, gain, *state)


STEP = 256


def forward_last_kernel(place, ids, lengths, a0, a1, b0, b1, w0, w1, gain, acc_in, ssq_in, _, *refs):
    product, kept, inv_ref, weight_ref, pooled_ref, acc, right, left, ssq, sem = refs
    k = pl.program_id(0)
    chip = chip_of(ids, *place)

    @pl.when(k == 0)
    def _():
        right[...] = scaled(jnp.concatenate([w0[...], w1[...]], axis=1), gain, ids, chip)
        tag(ids, pooled_ref)

    @pl.when(k < 2)
    def _():
        left[:, :BLK] = a0[...]
        left[:, BLK:] = a1[...]

    @pl.when(k >= 2)
    def _():
        left[:, :BLK] = b0[...]
        left[:, BLK:] = b1[...]

    rows = pl.ds(pl.multiple_of(k * STEP, STEP), STEP)
    saves = []
    for side in range(2):
        source = left.at[:, side * BLK : (side + 1) * BLK]
        saves.append(pltpu.make_async_copy(source, kept.at[chip, side, rows, :], sem.at[side]))
        saves[-1].start()
    ssq[...] = ssq_in[...] + folded_squares([left[:, :BLK], left[:, BLK:]])
    acc[...] = acc_in[...] + lax.dot_general(
        left[...], right[...], (((1,), (1,)), ((), ())), preferred_element_type=f32
    )
    product[...] = acc[...].astype(bf16)
    pool(lengths, k * (STEP // LEN), acc, ssq, inv_ref, weight_ref, pooled_ref)
    for copy in saves:
        copy.wait()


def forward_last(ids, lengths, place, a, b, weights, gain, state):
    whole = lambda k, *s: (0, 0)
    rows = lambda k, *s: (k, 0)
    early = pl.BlockSpec((STEP, BLK), lambda k, *s: (jnp.minimum(k, 1), 0))
    late = pl.BlockSpec((STEP, BLK), lambda k, *s: (jnp.maximum(k - 2, 0), 0))
    sides = [
        pl.BlockSpec((TERMS, BLK), lambda k, s, n, side=side: (0, chip_of(s, *place) * 2 + (s[4] ^ side)))
        for side in range(2)
    ]
    return pl.pallas_call(
        functools.partial(forward_last_kernel, place),
        out_shape=[
            jax.ShapeDtypeStruct((TOK, TERMS), bf16),
            STATE[2],
            jax.ShapeDtypeStruct((TOK, 1), f32),
            jax.ShapeDtypeStruct((TOK, TERMS), bf16),
            jax.ShapeDtypeStruct((SEQ, 1024), f32),
        ],
        grid_spec=pltpu.PrefetchScalarGridSpec(
            num_scalar_prefetch=2,
            grid=(TOK // STEP,),
            in_specs=[early, early, late, late, *sides, pl.BlockSpec((1, D), whole)]
            + [pl.BlockSpec((STEP, TERMS), rows), pl.BlockSpec((STEP, 128), rows), ANY],
            out_specs=[
                pl.BlockSpec((STEP, TERMS), rows),
                ANY,
                pl.BlockSpec((STEP, 1), rows),
                pl.BlockSpec((STEP, TERMS), rows),
                pl.BlockSpec((SEQ, 1024), whole),
            ],
            scratch_shapes=[
                pltpu.VMEM((STEP, TERMS), f32),
                pltpu.VMEM((TERMS, 2 * BLK), bf16),
                pltpu.VMEM((STEP, 2 * BLK), bf16),
                pltpu.VMEM((STEP, 128), f32),
                pltpu.SemaphoreType.DMA((2,)),
            ],
        ),
        input_output_aliases={11: 1},
        compiler_params=params(),
        cost_estimate=cost(2 * TOK * 512 * TERMS, 20_000_000),
        name="forward_last",
    )(ids, lengths, *a, *b, weights, weights, gain, *state)


def touch_kernel(*refs):
    pass


def touch(after, *arrays):
    n = len(arrays)
    return pl.pallas_call(
        touch_kernel,
        out_shape=[jax.ShapeDtypeStruct(a.shape, a.dtype) for a in arrays],
        in_specs=[ANY] * (n + 1),
        out_specs=[ANY] * n,
        input_output_aliases={i + 1: i for i in range(n)},
        compiler_params=params(has_side_effects=True),
        cost_estimate=cost(1000, 1000),
        name="touch",
    )(after, *arrays)


def gram_kernel(ids, p0, p1, p2, p3, all_ref, part_ref):
    xh, y = ids[0], ids[1]
    for j, ref in enumerate((p0, p1, p2, p3)):
        for m in range(2):
            at = (xh ^ m) * 4 + (y ^ j)
            all_ref[pl.ds(pl.multiple_of(at * SEQ, SEQ), SEQ), :] = ref[m]
    every = all_ref[:, :TERMS]
    part = lax.dot_general(every, every, (((1,), (1,)), ((), ())), precision=HIGHEST, preferred_element_type=f32)
    mean = jnp.sum(every, axis=0, keepdims=True) / 64.0
    flops = jnp.sum(mean * mean, axis=1, keepdims=True)
    part_ref[...] = jnp.zeros_like(part_ref)
    part_ref[0:64, 0:64] = part
    part_ref[64:72, :] = jnp.broadcast_to(flops, (8, 128))


def gram(ids, groups):
    whole3 = lambda s: (0, 0, 0)
    return pl.pallas_call(
        gram_kernel,
        out_shape=[jax.ShapeDtypeStruct((64, 1024), f32), jax.ShapeDtypeStruct((72, 128), f32)],
        grid_spec=pltpu.PrefetchScalarGridSpec(
            num_scalar_prefetch=1,
            grid=(),
            in_specs=[pl.BlockSpec(memory_space=pltpu.VMEM)] * 4,
            out_specs=[pl.BlockSpec(memory_space=pltpu.VMEM)] * 2,
        ),
        compiler_params=params(),
        name="gram",
    )(ids, *groups)


def contrast(every, part_a, part_b, scaled_ref, losses_ref):
    sums = part_a[...] + part_b[...]
    scores = sums[0:64, :] * SCORE_SCALE
    row = lax.broadcasted_iota(jnp.int32, (64, 128), 0)
    col = lax.broadcasted_iota(jnp.int32, (64, 128), 1)
    is_query = (row & 7) < 2
    is_passage = ((col & 7) >= 2) & (col < 64)
    tags = every[:, TERMS:]

    def hot(at):
        index = tags[:, at : at + 1]
        group = jnp.floor((index + 0.5) * (1.0 / 6.0))
        place = group * 8.0 + 2.0 + (index - 6.0 * group)
        return (col.astype(f32) == place).astype(f32)

    positive, negatives = hot(0), (hot(1), hot(2))
    highest = jnp.max(jnp.where(is_passage, scores, -3e38), axis=1, keepdims=True)
    shifted = jnp.where(is_passage, jnp.exp(jnp.minimum(scores - highest, 0.0)), 0.0)
    denominator = jnp.sum(shifted, axis=1, keepdims=True)
    log_total = highest + jnp.log(denominator)
    positive_score = jnp.sum(scores * positive, axis=1, keepdims=True)
    query_row = is_query[:, 0:1]
    cross = jnp.sum(jnp.where(query_row, log_total - positive_score, 0.0), axis=0, keepdims=True) / 16.0
    grad = (shifted / denominator - positive) / 16.0
    margin = jnp.zeros((1, 1), f32)
    for negative in negatives:
        gap = jnp.sum(scores * negative, axis=1, keepdims=True) - positive_score
        small = jnp.exp(-jnp.abs(gap))
        soft = jnp.maximum(gap, 0.0) + jnp.log(1.0 + small)
        slope = jnp.where(gap >= 0.0, 1.0, small) / (1.0 + small) / 32.0
        margin = margin + jnp.sum(jnp.where(query_row, soft, 0.0), axis=0, keepdims=True) / 32.0
        grad = grad + slope * negative - slope * positive
    grad = jnp.where(is_query, grad, 0.0)
    square = jnp.concatenate([grad, jnp.zeros((64, 128), f32)], axis=0)
    scaled_ref[...] = (square + square.T) * SCORE_SCALE
    flops = sums[64:65, 0:1] * flops_weight
    lane = lax.broadcasted_iota(jnp.int32, (8, 128), 1)
    losses_ref[...] = jnp.where(lane == 0, cross, jnp.where(lane == 1, margin, flops))


def grad_kernel(
    ids, every, part_a, part_b, weight, acc, h_ref, ht_ref, dots, losses_ref, rep, scaled, padded
):
    k = pl.program_id(0)

    @pl.when(k == 0)
    def _():
        contrast(every, part_a, part_b, scaled, losses_ref)
        padded[0:64, :] = every[:, :TERMS]
        padded[64:128, :] = jnp.zeros((64, TERMS), f32)
        at = pl.multiple_of((ids[0] * 4 + ids[1]) * SEQ, SEQ)
        own = scaled[pl.ds(at, SEQ), :]
        mean = jnp.sum(padded[...], axis=0, keepdims=True) / 64.0
        rep[...] = jnp.dot(own, padded[...], precision=HIGHEST, preferred_element_type=f32) + (
            2.0 * flops_weight / 64.0
        ) * mean

    for s in range(PER):
        rows = slice(s * LEN, (s + 1) * LEN)
        folded = jnp.zeros((LEN, 128), f32)
        for a, b in COLS:
            grad = weight[rows, a:b].astype(f32) * rep[pl.ds(k * PER + s, 1), a:b]
            rounded = grad.astype(bf16)
            h_ref[rows, a:b] = rounded
            turned = grad.T.astype(bf16)
            ht_ref[a:b, rows] = turned
            product = rounded.astype(f32) * acc[rows, a:b].astype(f32)
            wide = b - a
            folded = folded + product[:, :128]
            if wide == 256:
                folded = folded + product[:, 128:]
            else:
                folded = folded + jnp.concatenate([product[:, 128:], jnp.zeros((LEN, 256 - wide), f32)], axis=1)
        dots[pl.ds(k * PER + s, 1), :] = jnp.sum(folded.T, axis=0, keepdims=True)


def grads(ids, every, part_a, part_b, weight, acc):
    whole = lambda k, s: (0, 0)
    rows = lambda k, s: (k, 0)
    cols = lambda k, s: (0, k)
    return pl.pallas_call(
        grad_kernel,
        out_shape=[
            jax.ShapeDtypeStruct((TOK, TERMS), bf16),
            jax.ShapeDtypeStruct((TERMS, TOK), bf16),
            jax.ShapeDtypeStruct((SEQ, LEN), f32),
            jax.ShapeDtypeStruct((8, 128), f32),
        ],
        grid_spec=pltpu.PrefetchScalarGridSpec(
            num_scalar_prefetch=1,
            grid=(SEQ // PER,),
            in_specs=[
                pl.BlockSpec((64, 1024), whole),
                pl.BlockSpec((72, 128), whole),
                pl.BlockSpec((72, 128), whole),
                pl.BlockSpec((PER * LEN, TERMS), rows),
                pl.BlockSpec((PER * LEN, TERMS), rows),
            ],
            out_specs=[
                pl.BlockSpec((PER * LEN, TERMS), rows),
                pl.BlockSpec((TERMS, PER * LEN), cols),
                pl.BlockSpec((SEQ, LEN), whole),
                pl.BlockSpec((8, 128), whole),
            ],
            scratch_shapes=[pltpu.VMEM((SEQ, TERMS), f32), pltpu.VMEM((128, 128), f32), pltpu.VMEM((128, TERMS), f32)],
        ),
        compiler_params=params(),
        cost_estimate=cost(20 * TOK * TERMS, 12_000_000),
        name="logit_grad",
    )(ids, every, part_a, part_b, weight, acc)


def head_kernel(ids, _, ht, x, gain, a00, a01, a10, a11, keep, send):
    n = pl.program_id(0)
    block = jnp.concatenate([x[0, 0], x[0, 1]], axis=1)
    chip = head_chip(ids, n)
    row = jnp.concatenate([gain[:, block_at(ids, chip, side)] for side in range(2)], axis=1)
    total = (jnp.dot(ht[...], block, preferred_element_type=f32) * row).astype(bf16)
    sides = [total[:, :BLK], total[:, BLK:]]
    for when, outs in ((n < 2, (a00, a01)), (n >= 2, (a10, a11))):

        @pl.when(when)
        def _(outs=outs):
            for side in range(2):
                outs[side][0] = sides[side][:ROWS_A]

    for j, out in enumerate((keep, send)):

        @pl.when((n & 1) == j)
        def _(out=out):
            for side in range(2):
                out[0, side] = sides[side][ROWS_A:]


def head_chip(ids, n):
    return (ids[0] ^ (n & 1)) * 4 + ((ids[1] + jnp.where(n < 2, ids[14], ids[15])) & 3)


def head_part(ids, steps, ht, x, gain, after):
    ids = jnp.concatenate([ids, jnp.array(steps, jnp.int32)])
    first = pl.BlockSpec((1, ROWS_A, BLK), lambda n, s: (jnp.minimum(n, 1), 0, 0))
    second = pl.BlockSpec((1, ROWS_A, BLK), lambda n, s: (jnp.maximum(n - 2, 0), 0, 0))
    low = pl.BlockSpec((1, 2, ROWS_B, BLK), lambda n, s: (n // 2, 0, 0, 0))
    return pl.pallas_call(
        head_kernel,
        out_shape=[jax.ShapeDtypeStruct((2, ROWS_A, BLK), bf16)] * 4
        + [jax.ShapeDtypeStruct((2, 2, ROWS_B, BLK), bf16)] * 2,
        grid_spec=pltpu.PrefetchScalarGridSpec(
            num_scalar_prefetch=1,
            grid=(4,),
            in_specs=[
                ANY,
                pl.BlockSpec((TERMS, TOK), lambda n, s: (0, 0)),
                pl.BlockSpec((1, 2, TOK, BLK), lambda n, s: (head_chip(s, n), 0, 0, 0)),
                pl.BlockSpec((1, D), lambda n, s: (0, 0)),
            ],
            out_specs=[first, first, second, second, low, low],
        ),
        compiler_params=params(),
        cost_estimate=cost(2 * TERMS * TOK * 2048, 2 * TERMS * TOK + 4096 * (TOK + TERMS)),
        name="head_part",
    )(ids, after, ht, x, gain)


def join_kernel(ids, r0, r1, a0, a1, got, keep, swapped, b1, b2, b3, out):
    for side, r, a in ((0, r0, a0), (1, r1, a1)):
        cols = pl.ds(pl.multiple_of((ids[4] ^ side) * BLK, BLK), BLK)
        out[0:ROWS_A, cols] = (r[0].astype(f32) + a[0].astype(f32) + got[side].astype(f32)).astype(bf16)
        total = keep[1, side].astype(f32) + swapped[1, side].astype(f32)
        for b in (b1, b2, b3):
            total = total + b[side].astype(f32)
        out[ROWS_A:TERMS, cols] = total.astype(bf16)


def join(ids, *parts):
    return pl.pallas_call(
        join_kernel,
        out_shape=jax.ShapeDtypeStruct((TERMS, 2 * BLK), bf16),
        in_specs=[SMEM] + [VMEM] * len(parts),
        out_specs=VMEM,
        compiler_params=params(),
        cost_estimate=cost(1000, 8_000_000),
        name="join",
    )(ids, *parts)


def term_kernel(n_add, ids, _, h, w0, w1, *refs):
    weights = jnp.concatenate([w0[...], w1[...]], axis=1)
    out = refs[n_add]
    for half in range(2):
        rows = slice(half * HALF, (half + 1) * HALF)
        total = jnp.dot(h[rows, :], weights, preferred_element_type=f32)
        for m in range(2):
            share = total[:, m * BLK : (m + 1) * BLK]
            for ref in refs[:n_add]:
                share = share + ref[0, m, rows, :].astype(f32)
            out[0, m, rows, :] = share.astype(bf16)


def term_part(ids, side, h, wt, after, adds=()):
    block = pl.BlockSpec((1, 2, TOK, BLK), lambda j, s: (j, 0, 0, 0))
    sides = [
        pl.BlockSpec((TERMS, BLK), lambda j, s, m=m: (0, ((s[2] ^ m) * 4 + j) * 2 + (s[4] ^ side))) for m in range(2)
    ]
    return pl.pallas_call(
        functools.partial(term_kernel, len(adds)),
        out_shape=jax.ShapeDtypeStruct((4, 2, TOK, BLK), bf16),
        grid_spec=pltpu.PrefetchScalarGridSpec(
            num_scalar_prefetch=1,
            grid=(4,),
            in_specs=[ANY, pl.BlockSpec((TOK, TERMS), lambda j, s: (0, 0)), *sides] + [block] * len(adds),
            out_specs=block,
        ),
        compiler_params=params(),
        cost_estimate=cost(16 * TOK * BLK * TERMS, 2 * TOK * TERMS + 8 * BLK * (2 * TERMS + 4 * TOK)),
        name="term_part",
    )(ids, after, h, wt, wt, *adds)


def gain_kernel(n, x, x_p, out):
    for m, ref in ((0, x), (1, x_p)):
        sums = jnp.zeros((8, BLK), f32)
        for k in range(SEQ):
            rows = slice(k * LEN, (k + 1) * LEN)
            sums = sums + jnp.sum((n[m, rows, :].astype(f32) * ref[rows, :].astype(f32)).reshape(LEN // 8, 8, BLK), axis=0)
        out[m] = jnp.sum(sums, axis=0, keepdims=True)


def gain_part(n, x, x_p):
    return pl.pallas_call(
        gain_kernel,
        out_shape=jax.ShapeDtypeStruct((2, 1, BLK), f32),
        in_specs=[VMEM] * 3,
        out_specs=VMEM,
        compiler_params=params(),
        cost_estimate=cost(1_000_000, 2_000_000),
        name="gain_part",
    )(n, x, x_p)


def final_kernel(ids, n_ref, got, x_ref, gain, inv_ref, da, db, out):
    g = gain[:, block_at(ids, ids[2] * 4 + ids[3], 0)]
    lines = (da[...] + db[...]) / D
    for k in range(SEQ):
        rows = slice(k * LEN, (k + 1) * LEN)
        grad = n_ref[0, rows, :].astype(f32) + got[rows, :].astype(f32)
        values = x_ref[rows, :].astype(f32)
        column = jnp.broadcast_to(lines[k : k + 1, :], (LEN, LEN)).T[:, 0:1]
        inverse = inv_ref[rows, :]
        out[rows, :] = (grad * g - values * (inverse * inverse * column)).astype(bf16)


def final(ids, n, got, x, gain, inv, da, db):
    return pl.pallas_call(
        final_kernel,
        out_shape=jax.ShapeDtypeStruct((TOK, BLK), bf16),
        in_specs=[SMEM] + [VMEM] * 7,
        out_specs=VMEM,
        compiler_params=params(),
        cost_estimate=cost(1_000_000, 2_000_000),
        name="hidden_grad",
    )(ids, n, got, x, gain, inv, da, db)


def shards(hidden, norm_gain, head_weight, lengths, positives, negatives):
    xh, y, xl, z, c = (lax.axis_index(a).astype(jnp.int32) for a in ("xh", "y", "xl", "z", "c"))
    nil = jnp.int32(0)
    ids = jnp.concatenate([jnp.stack([xh, y, xl, z, c, nil, nil, nil]), positives, negatives.reshape(-1)])
    wt = head_weight.T
    gain = norm_gain.reshape(1, D)

    z_m, z_p, x_p = shift(hidden, "z", 1), shift(hidden, "z", -1), swap(hidden, "xl")
    own_c = swap(hidden, "c")
    z_m_c, z_p_c, x_p_c = (swap(a, "c") for a in (z_m, z_p, x_p))
    far, xz_p, xz_m = shift(z_m, "z", 1), shift(x_p, "z", -1), swap(z_m, "xl")
    state = forward(ids, [(0, 0), (0, -1), (1, 0)], [hidden, own_c, z_m, z_m_c, x_p, x_p_c], wt, gain)
    far, xz_p, xz_m = touch(state[1], far, xz_p, xz_m)
    far_c, xz_p_c, xz_m_c = (swap(a, "c") for a in (far, xz_p, xz_m))
    last_a, last_b = shift(xz_m[:HALF], "z", 1), shift(xz_p[HALF:], "z", -1)
    state = forward(
        ids,
        [(0, 1), (0, 2), (1, 1), (1, -1)],
        [z_p, z_p_c, far, far_c, xz_p, xz_p_c, xz_m, xz_m_c],
        wt,
        gain,
        state,
    )
    last_a, last_b = touch(state[1], last_a, last_b)
    last_a_c, last_b_c = swap(last_a, "c"), swap(last_b, "c")
    acc, x, inv, weight, pooled = forward_last(
        ids, lengths, (1, 2), (last_a, last_a_c), (last_b, last_b_c), wt, gain, state
    )

    pair = jnp.stack([pooled, swap(pooled, "xh")])
    every, part = gram(ids, [pair] + [swap(pair, "y", j) for j in (1, 2, 3)])
    part = part + swap(part, "c")
    part = (part + swap(part, "z", 1)) + (swap(part, "z", 2) + swap(part, "z", 3))
    h, ht, dots, losses = grads(ids, every, part, swap(part, "xl"), weight, acc)

    crossing = term_part(ids, 1, h, wt, ht)
    a3_own, a3_oth, a1_own, a1_oth, keep_31, send_31 = head_part(ids, (3, 1), ht, x, gain, crossing)
    crossed = swap(crossing, "c")
    term = term_part(ids, 0, h, wt, a3_own, (crossed,))
    a2_own, a2_oth, a0_own, a0_oth, keep_20, send_20 = head_part(ids, (2, 0), ht, x, gain, term)
    summed = lax.psum_scatter(term, "z", scatter_dimension=0, tiled=False)
    partial = gain_part(summed, hidden, x_p)
    gain_grad = partial[0] + swap(partial[1], "xl")
    gain_grad = gain_grad + swap(gain_grad, "xh")
    gain_grad = (gain_grad + swap(gain_grad, "y", 1)) + (swap(gain_grad, "y", 2) + swap(gain_grad, "y", 3))
    got_term = swap(summed[1], "xl")

    own, oth = shift(a3_own, "y", 1), shift(a1_oth, "y", -1)
    swapped_31, swapped_20 = swap(send_31, "xh"), swap(send_20, "xh")
    own, oth = shift(own + a2_own, "y", 1), shift(oth + a2_oth, "y", -1)
    a1_own, a3_oth = touch(swapped_31, a1_own, a3_oth)
    own, oth = shift(own + a1_own, "y", 1), shift(oth + a3_oth, "y", -1)
    got = swap(jnp.stack([own[1] + a0_own[1], oth[1] + a0_oth[1]]), "xh")
    low = [
        shift(keep_31[1] + swapped_31[1], "y", 1),
        shift(keep_20[0] + swapped_20[0], "y", 2),
        shift(keep_31[0] + swapped_31[0], "y", 3),
    ]
    head_t = join(ids, own, oth, a0_own, a0_oth, got, keep_20, swapped_20, *low)

    dots = dots + swap(dots, "c")
    dots = (dots + swap(dots, "z", 1)) + (swap(dots, "z", 2) + swap(dots, "z", 3))
    hidden_grad = final(ids, summed, got_term, hidden, gain, inv, dots, swap(dots, "xl"))
    return losses[0, :3], hidden_grad, head_t.T, gain_grad[0]


def solution(mesh):
    fine = Mesh(mesh.devices.reshape(2, 4, 2, 4, 2), ("xh", "y", "xl", "z", "c"))
    dp, vocab = ("xh", "y"), ("xl", "z", "c")
    in_specs = (P(dp, vocab), P(), P(None, vocab), P(dp), P(dp), P(dp, None))
    out_specs = (P(), P(dp, vocab), P(dp, vocab), P(vocab))
    return jax.shard_map(shards, mesh=fine, in_specs=in_specs, out_specs=out_specs, check_vma=False)
```

```python
import functools
import math

import jax
import jax.numpy as jnp
from jax import lax
from jax.experimental import pallas as pl
from jax.experimental.pallas import tpu as pltpu
from jax.sharding import Mesh, PartitionSpec as P

VOCAB = 16000
D = 4096
epsilon = 1e-05
sharpness = 80.0
flops_weight = 0.01

TOK = 1024
SEQ = 8
LEN = 128
TERMS = 1000
BLK = 256
ROWS_A = 640
ROWS_B = TERMS - ROWS_A
HALF = TOK // 2
PER = 2
SCORE_SCALE = 4.0 / math.sqrt(VOCAB)
COLS = ((0, 256), (256, 512), (512, 768), (768, 1000))
SIZES = {"xh": 2, "y": 4, "xl": 2, "z": 4, "c": 2}
VMEM_LIMIT = 67_000_000
HIGHEST = lax.Precision.HIGHEST

f32, bf16 = jnp.float32, jnp.bfloat16


def shift(x, axis, step):
    n = SIZES[axis]
    return lax.ppermute(x, axis, [(i, (i + step) % n) for i in range(n)])


def swap(x, axis, bits=1):
    return lax.ppermute(x, axis, [(i, i ^ bits) for i in range(SIZES[axis])])


def params(**more):
    return pltpu.CompilerParams(vmem_limit_bytes=VMEM_LIMIT, **more)


def cost(flops, moved, weight=0.02):
    return pl.CostEstimate(flops=int(flops * weight), bytes_accessed=int(moved * weight), transcendentals=0)


def tag(ids, pooled_ref):
    lane = lax.broadcasted_iota(jnp.int32, (1, 24), 1)
    for k in range(SEQ):
        tags = jnp.zeros((1, 24), f32)
        if k < 2:
            tags = jnp.where(lane == 0, ids[8 + k].astype(f32), tags)
            tags = jnp.where(lane == 1, ids[10 + 2 * k].astype(f32), tags)
            tags = jnp.where(lane == 2, ids[11 + 2 * k].astype(f32), tags)
        pooled_ref[k : k + 1, TERMS:] = tags


def pool(lengths, first, acc, ssq, inv_ref, weight_ref, pooled_ref):
    for s in range(acc.shape[0] // LEN):
        k = first + s
        rows = slice(s * LEN, (s + 1) * LEN)
        total = jnp.sum(ssq[rows, :], axis=1, keepdims=True)
        inverse = lax.rsqrt(total / D + epsilon)
        inv_ref[rows, :] = inverse
        count = lengths[k]
        for a, b in COLS:
            logits = acc[rows, a:b] * inverse
            valid = lax.broadcasted_iota(jnp.int32, (LEN, b - a), 0) < count
            held = jnp.where(valid, 1.0 + jnp.maximum(logits, 0.0), 1.0)
            top = jnp.max(held, axis=0, keepdims=True)
            down = 1.0 / top
            r1 = held * down
            r2 = r1 * r1
            r4 = r2 * r2
            r8 = r4 * r4
            r16 = r8 * r8
            r32 = r16 * r16
            r79 = (r32 * r32 * r8) * (r4 * (r2 * r1))
            summed = jnp.sum(jnp.where(valid, r79 * r1, 0.0), axis=0, keepdims=True)
            pooled_ref[pl.ds(k, 1), a:b] = jnp.log(top) + jnp.log(summed) / sharpness
            slope = r79 * (down / summed) * inverse
            weight_ref[rows, a:b] = jnp.where(valid & (logits > 0.0), slope, 0.0).astype(bf16)


def chip_of(ids, far_x, step):
    return (ids[2] ^ far_x) * 4 + ((ids[3] + step) & 3)


def block_at(ids, chip, side):
    return pl.ds(pl.multiple_of((chip * 2 + (ids[4] ^ side)) * BLK, BLK), BLK)


def scaled(weights, gain, ids, chip):
    row = jnp.concatenate([gain[:, block_at(ids, chip, side)] for side in range(2)], axis=1)
    return (weights.astype(f32) * row).astype(bf16)


def folded_squares(lefts):
    squares = 0.0
    for left in lefts:
        value = left.astype(f32)
        square = value * value
        squares = squares + square[:, :128] + square[:, 128:]
    return squares


def forward_kernel(places, first, ids, *refs):
    nb = len(places)
    arrays, (weights, gain), refs = refs[: 2 * nb], refs[2 * nb : 2 * nb + 2], refs[2 * nb + 2 :]
    if not first:
        (acc_in, ssq_in, _), refs = refs[:3], refs[3:]
    acc, ssq, kept, held, w_sem, x_sem = refs
    chips = [chip_of(ids, *place) for place in places]
    loads, saves = [], []
    for j in range(nb):
        for side in range(2):
            at = held.at[j, :, side * BLK : (side + 1) * BLK]
            loads.append(pltpu.make_async_copy(weights.at[:, block_at(ids, chips[j], side)], at, w_sem.at[j, side]))
            loads[-1].start()
    for j in range(nb):
        for side in range(2):
            saves.append(pltpu.make_async_copy(arrays[2 * j + side], kept.at[chips[j], side], x_sem.at[j, side]))
            saves[-1].start()
    for j in range(nb):
        loads[2 * j].wait()
        loads[2 * j + 1].wait()
        right = scaled(held[j], gain, ids, chips[j])
        for half in range(2):
            rows = slice(half * HALF, (half + 1) * HALF)
            lefts = [arrays[2 * j + side][rows, :] for side in range(2)]
            squares = folded_squares(lefts)
            product = lax.dot_general(
                jnp.concatenate(lefts, axis=1), right, (((1,), (1,)), ((), ())), preferred_element_type=f32
            )
            if j == 0 and first:
                acc[rows, :] = product
                ssq[rows, :] = squares
            elif j == 0:
                acc[rows, :] = acc_in[rows, :] + product
                ssq[rows, :] = ssq_in[rows, :] + squares
            else:
                acc[rows, :] += product
                ssq[rows, :] += squares
    for copy in saves:
        copy.wait()


SMEM = pl.BlockSpec(memory_space=pltpu.SMEM)
VMEM = pl.BlockSpec(memory_space=pltpu.VMEM)
ANY = pl.BlockSpec(memory_space=pl.ANY)


STATE = [
    jax.ShapeDtypeStruct((TOK, TERMS), f32),
    jax.ShapeDtypeStruct((TOK, 128), f32),
    jax.ShapeDtypeStruct((8, 2, TOK, BLK), bf16),
]


def forward(ids, places, arrays, weights, gain, state=()):
    nb = len(places)
    base = 3 + len(arrays)
    return pl.pallas_call(
        functools.partial(forward_kernel, places, not state),
        out_shape=STATE,
        in_specs=[SMEM] + [VMEM] * len(arrays) + [ANY, VMEM] + [VMEM, VMEM, ANY][: len(state)],
        out_specs=[VMEM, VMEM, ANY],
        scratch_shapes=[
            pltpu.VMEM((nb, TERMS, 2 * BLK), bf16),
            pltpu.SemaphoreType.DMA((nb, 2)),
            pltpu.SemaphoreType.DMA((nb, 2)),
        ],
        input_output_aliases={base + i: i for i in range(len(state))},
        compiler_params=params(),
        cost_estimate=cost(2 * nb * TOK * 512 * TERMS, nb * 3_000_000 + 8_000_000),
        name="forward_part",
    )(ids, *arrays, weights, gain, *state)


STEP = 256


def forward_last_kernel(place, ids, lengths, a0, a1, w0, w1, gain, acc_in, ssq_in, _, *refs):
    product, kept, inv_ref, weight_ref, pooled_ref, acc, right, ssq, sem = refs
    k = pl.program_id(0)
    chip = chip_of(ids, *place)

    @pl.when(k == 0)
    def _():
        right[...] = scaled(jnp.concatenate([w0[...], w1[...]], axis=1), gain, ids, chip)
        tag(ids, pooled_ref)

    rows = pl.ds(pl.multiple_of(k * STEP, STEP), STEP)
    saves = []
    for side, source in enumerate((a0, a1)):
        saves.append(pltpu.make_async_copy(source, kept.at[chip, side, rows, :], sem.at[side]))
        saves[-1].start()
    lefts = [a0[...], a1[...]]
    ssq[...] = ssq_in[...] + folded_squares(lefts)
    acc[...] = acc_in[...] + lax.dot_general(
        jnp.concatenate(lefts, axis=1), right[...], (((1,), (1,)), ((), ())), preferred_element_type=f32
    )
    product[...] = acc[...].astype(bf16)
    pool(lengths, k * (STEP // LEN), acc, ssq, inv_ref, weight_ref, pooled_ref)
    for copy in saves:
        copy.wait()


def forward_last(ids, lengths, place, arrays, weights, gain, state):
    whole = lambda k, *s: (0, 0)
    rows = lambda k, *s: (k, 0)
    sides = [
        pl.BlockSpec((TERMS, BLK), lambda k, s, n, side=side: (0, chip_of(s, *place) * 2 + (s[4] ^ side)))
        for side in range(2)
    ]
    return pl.pallas_call(
        functools.partial(forward_last_kernel, place),
        out_shape=[
            jax.ShapeDtypeStruct((TOK, TERMS), bf16),
            STATE[2],
            jax.ShapeDtypeStruct((TOK, 1), f32),
            jax.ShapeDtypeStruct((TOK, TERMS), bf16),
            jax.ShapeDtypeStruct((SEQ, 1024), f32),
        ],
        grid_spec=pltpu.PrefetchScalarGridSpec(
            num_scalar_prefetch=2,
            grid=(TOK // STEP,),
            in_specs=[pl.BlockSpec((STEP, BLK), rows)] * 2
            + [*sides, pl.BlockSpec((1, D), whole)]
            + [pl.BlockSpec((STEP, TERMS), rows), pl.BlockSpec((STEP, 128), rows), ANY],
            out_specs=[
                pl.BlockSpec((STEP, TERMS), rows),
                ANY,
                pl.BlockSpec((STEP, 1), rows),
                pl.BlockSpec((STEP, TERMS), rows),
                pl.BlockSpec((SEQ, 1024), whole),
            ],
            scratch_shapes=[
                pltpu.VMEM((STEP, TERMS), f32),
                pltpu.VMEM((TERMS, 2 * BLK), bf16),
                pltpu.VMEM((STEP, 128), f32),
                pltpu.SemaphoreType.DMA((2,)),
            ],
        ),
        input_output_aliases={9: 1},
        compiler_params=params(),
        cost_estimate=cost(2 * TOK * 512 * TERMS, 20_000_000),
        name="forward_last",
    )(ids, lengths, *arrays, weights, weights, gain, *state)


def touch_kernel(*refs):
    pass


def touch(after, *arrays):
    n = len(arrays)
    return pl.pallas_call(
        touch_kernel,
        out_shape=[jax.ShapeDtypeStruct(a.shape, a.dtype) for a in arrays],
        in_specs=[ANY] * (n + 1),
        out_specs=[ANY] * n,
        input_output_aliases={i + 1: i for i in range(n)},
        compiler_params=params(has_side_effects=True),
        cost_estimate=cost(1000, 1000),
        name="touch",
    )(after, *arrays)


def gram_kernel(ids, *refs):
    all_ref, part_ref = refs[8:]
    for bits, ref in enumerate(refs[:8]):
        at = (ids[0] * 4 + ids[1]) ^ bits
        all_ref[pl.ds(pl.multiple_of(at * SEQ, SEQ), SEQ), :] = ref[...]
    every = all_ref[:, :TERMS]
    part = lax.dot_general(every, every, (((1,), (1,)), ((), ())), precision=HIGHEST, preferred_element_type=f32)
    mean = jnp.sum(every, axis=0, keepdims=True) / 64.0
    flops = jnp.sum(mean * mean, axis=1, keepdims=True)
    part_ref[...] = jnp.zeros_like(part_ref)
    part_ref[0:64, 0:64] = part
    part_ref[64:72, :] = jnp.broadcast_to(flops, (8, 128))


def gram(ids, groups):
    return pl.pallas_call(
        gram_kernel,
        out_shape=[jax.ShapeDtypeStruct((64, 1024), f32), jax.ShapeDtypeStruct((72, 128), f32)],
        grid_spec=pltpu.PrefetchScalarGridSpec(
            num_scalar_prefetch=1,
            grid=(),
            in_specs=[VMEM] * 8,
            out_specs=[VMEM] * 2,
        ),
        compiler_params=params(),
        name="gram",
    )(ids, *groups)


def contrast(every, parts, scaled_ref, losses_ref):
    sums = (parts[0][...] + parts[1][...]) + (parts[2][...] + parts[3][...])
    scores = sums[0:64, :] * SCORE_SCALE
    row = lax.broadcasted_iota(jnp.int32, (64, 128), 0)
    col = lax.broadcasted_iota(jnp.int32, (64, 128), 1)
    is_query = (row & 7) < 2
    is_passage = ((col & 7) >= 2) & (col < 64)
    tags = every[:, TERMS:]

    def hot(at):
        index = tags[:, at : at + 1]
        group = jnp.floor((index + 0.5) * (1.0 / 6.0))
        place = group * 8.0 + 2.0 + (index - 6.0 * group)
        return (col.astype(f32) == place).astype(f32)

    positive, negatives = hot(0), (hot(1), hot(2))
    highest = jnp.max(jnp.where(is_passage, scores, -3e38), axis=1, keepdims=True)
    shifted = jnp.where(is_passage, jnp.exp(jnp.minimum(scores - highest, 0.0)), 0.0)
    denominator = jnp.sum(shifted, axis=1, keepdims=True)
    log_total = highest + jnp.log(denominator)
    positive_score = jnp.sum(scores * positive, axis=1, keepdims=True)
    query_row = is_query[:, 0:1]
    cross = jnp.sum(jnp.where(query_row, log_total - positive_score, 0.0), axis=0, keepdims=True) / 16.0
    grad = (shifted / denominator - positive) / 16.0
    margin = jnp.zeros((1, 1), f32)
    for negative in negatives:
        gap = jnp.sum(scores * negative, axis=1, keepdims=True) - positive_score
        small = jnp.exp(-jnp.abs(gap))
        soft = jnp.maximum(gap, 0.0) + jnp.log(1.0 + small)
        slope = jnp.where(gap >= 0.0, 1.0, small) / (1.0 + small) / 32.0
        margin = margin + jnp.sum(jnp.where(query_row, soft, 0.0), axis=0, keepdims=True) / 32.0
        grad = grad + slope * negative - slope * positive
    grad = jnp.where(is_query, grad, 0.0)
    square = jnp.concatenate([grad, jnp.zeros((64, 128), f32)], axis=0)
    scaled_ref[...] = (square + square.T) * SCORE_SCALE
    flops = sums[64:65, 0:1] * flops_weight
    lane = lax.broadcasted_iota(jnp.int32, (8, 128), 1)
    losses_ref[...] = jnp.where(lane == 0, cross, jnp.where(lane == 1, margin, flops))


def grad_kernel(
    ids, every, p0, p1, p2, p3, weight, acc, h_ref, ht_ref, dots, losses_ref, rep, scaled, padded
):
    k = pl.program_id(0)

    @pl.when(k == 0)
    def _():
        contrast(every, (p0, p1, p2, p3), scaled, losses_ref)
        dots[...] = jnp.zeros_like(dots)
        padded[0:64, :] = every[:, :TERMS]
        padded[64:128, :] = jnp.zeros((64, TERMS), f32)
        at = pl.multiple_of((ids[0] * 4 + ids[1]) * SEQ, SEQ)
        own = scaled[pl.ds(at, SEQ), :]
        mean = jnp.sum(padded[...], axis=0, keepdims=True) / 64.0
        rep[...] = jnp.dot(own, padded[...], precision=HIGHEST, preferred_element_type=f32) + (
            2.0 * flops_weight / 64.0
        ) * mean

    lines = []
    for s in range(PER):
        rows = slice(s * LEN, (s + 1) * LEN)
        folded = jnp.zeros((LEN, 128), f32)
        for a, b in COLS:
            grad = weight[rows, a:b].astype(f32) * rep[pl.ds(k * PER + s, 1), a:b]
            rounded = grad.astype(bf16)
            h_ref[rows, a:b] = rounded
            turned = grad.T.astype(bf16)
            ht_ref[a:b, rows] = turned
            product = rounded.astype(f32) * acc[rows, a:b].astype(f32)
            wide = b - a
            folded = folded + product[:, :128]
            if wide == 256:
                folded = folded + product[:, 128:]
            else:
                folded = folded + jnp.concatenate([product[:, 128:], jnp.zeros((LEN, 256 - wide), f32)], axis=1)
        lines.append(jnp.sum(folded.T, axis=0, keepdims=True))
    dots[pl.ds((k >> 1) * 8 + (k & 1), 1), :] = jnp.concatenate(lines, axis=1)


def grads(ids, every, parts, weight, acc):
    whole = lambda k, s: (0, 0)
    rows = lambda k, s: (k, 0)
    cols = lambda k, s: (0, k)
    return pl.pallas_call(
        grad_kernel,
        out_shape=[
            jax.ShapeDtypeStruct((TOK, TERMS), bf16),
            jax.ShapeDtypeStruct((TERMS, TOK), bf16),
            jax.ShapeDtypeStruct((16, BLK), f32),
            jax.ShapeDtypeStruct((8, 128), f32),
        ],
        grid_spec=pltpu.PrefetchScalarGridSpec(
            num_scalar_prefetch=1,
            grid=(SEQ // PER,),
            in_specs=[
                pl.BlockSpec((64, 1024), whole),
                *[pl.BlockSpec((72, 128), whole)] * 4,
                pl.BlockSpec((PER * LEN, TERMS), rows),
                pl.BlockSpec((PER * LEN, TERMS), rows),
            ],
            out_specs=[
                pl.BlockSpec((PER * LEN, TERMS), rows),
                pl.BlockSpec((TERMS, PER * LEN), cols),
                pl.BlockSpec((16, BLK), whole),
                pl.BlockSpec((8, 128), whole),
            ],
            scratch_shapes=[pltpu.VMEM((SEQ, TERMS), f32), pltpu.VMEM((128, 128), f32), pltpu.VMEM((128, TERMS), f32)],
        ),
        compiler_params=params(),
        cost_estimate=cost(20 * TOK * TERMS, 12_000_000),
        name="logit_grad",
    )(ids, every, *parts, weight, acc)


def later(count, kernel):
    return lambda ids, *refs: kernel(ids, *refs[count:])


def place_of(steps, n):
    step = steps[0]
    for i in range(1, len(steps)):
        step = jnp.where(n < 2 * i, step, steps[i])
    return step, n & 1


def head_chip(steps, ids, n):
    step, j = place_of(steps, n)
    return (ids[0] ^ j) * 4 + ((ids[1] + step) & 3)


def head_kernel(steps, split, n_add, ids, ht, x, gain, *refs):
    n = pl.program_id(0)
    adds, outs, (keep, send) = refs[:n_add], refs[n_add:-2], refs[-2:]
    block = jnp.concatenate([x[0, 0], x[0, 1]], axis=1)
    chip = head_chip(steps, ids, n)
    row = jnp.concatenate([gain[:, block_at(ids, chip, side)] for side in range(2)], axis=1)
    total = jnp.dot(ht[...], block, preferred_element_type=f32) * row
    sides = [total[:, :BLK], total[:, BLK:]]
    for i in range(len(steps)):

        @pl.when((n >> 1) == i)
        def _(i=i):
            for side in range(2):
                share = sides[side][:ROWS_A]
                if n_add and side == i:
                    share = share + adds[i][0].astype(f32)
                if split:
                    outs[side][0] = share.astype(bf16)
                else:
                    outs[i][0, side] = share.astype(bf16)

    for j, out in enumerate((keep, send)):

        @pl.when((n & 1) == j)
        def _(out=out):
            for side in range(2):
                out[0, side] = sides[side][ROWS_A:].astype(bf16)


def head_part(ids, steps, ht, x, gain, after, split=False, adds=(), weight=0.02):
    count = len(steps)
    at = lambda i: lambda n, s: (jnp.clip(n - 2 * i, 0, 1), 0, 0)
    at4 = lambda i: lambda n, s: (jnp.clip(n - 2 * i, 0, 1), 0, 0, 0)
    one = pl.BlockSpec((1, ROWS_A, BLK), at(0))
    low = pl.BlockSpec((1, 2, ROWS_B, BLK), lambda n, s: (n // 2, 0, 0, 0))
    if split:
        high, specs = [jax.ShapeDtypeStruct((2, ROWS_A, BLK), bf16)] * 2, [one, one]
    else:
        high = [jax.ShapeDtypeStruct((2, 2, ROWS_A, BLK), bf16)] * count
        specs = [pl.BlockSpec((1, 2, ROWS_A, BLK), at4(i)) for i in range(count)]
    return pl.pallas_call(
        later(len(after), functools.partial(head_kernel, steps, split, len(adds))),
        out_shape=high + [jax.ShapeDtypeStruct((count, 2, ROWS_B, BLK), bf16)] * 2,
        grid_spec=pltpu.PrefetchScalarGridSpec(
            num_scalar_prefetch=1,
            grid=(2 * count,),
            in_specs=[ANY] * len(after)
            + [
                pl.BlockSpec((TERMS, TOK), lambda n, s: (0, 0)),
                pl.BlockSpec((1, 2, TOK, BLK), lambda n, s: (head_chip(steps, s, n), 0, 0, 0)),
                pl.BlockSpec((1, D), lambda n, s: (0, 0)),
            ]
            + [pl.BlockSpec((1, ROWS_A, BLK), at(i)) for i in range(len(adds))],
            out_specs=specs + [low, low],
        ),
        compiler_params=params(),
        cost_estimate=cost(2 * TERMS * TOK * 1024 * count, 2 * TERMS * TOK + 2048 * count * (TOK + TERMS), weight),
        name="head_part",
    )(ids, *after, ht, x, gain, *adds)


def join_kernel(ids, _, a0, ra, rb, got, keep, swapped, b1, b2, b3, out):
    for side in range(2):
        cols = pl.ds(pl.multiple_of((ids[4] ^ side) * BLK, BLK), BLK)
        total = a0[0, side].astype(f32) + ra[0, side].astype(f32) + rb[0, side].astype(f32) + got[side].astype(f32)
        out[0:ROWS_A, cols] = total.astype(bf16)
        total = keep[0, side].astype(f32) + swapped[0, side].astype(f32)
        for b in (b1, b2, b3):
            total = total + b[side].astype(f32)
        out[ROWS_A:TERMS, cols] = total.astype(bf16)


def join(ids, after, *parts):
    return pl.pallas_call(
        join_kernel,
        out_shape=jax.ShapeDtypeStruct((TERMS, 2 * BLK), bf16),
        in_specs=[SMEM, ANY] + [VMEM] * len(parts),
        out_specs=VMEM,
        compiler_params=params(),
        cost_estimate=cost(1000, 8_000_000),
        name="join",
    )(ids, after, *parts)


ROWS_T = HALF + 16


def term_step(steps, n):
    step = steps[0]
    for i in range(1, len(steps)):
        step = jnp.where(n < i, step, steps[i])
    return step


def term_kernel(n_steps, split, n_adds, ids, h, w0, w1, dots, *refs):
    n = pl.program_id(0)
    crossed, adds, outs = refs[: n_adds[0]], refs[n_adds[0] : sum(n_adds)], refs[sum(n_adds) :]
    weights = jnp.concatenate([w0[...], w1[...]], axis=1)
    for half in range(2):
        total = jnp.dot(h[half * HALF : (half + 1) * HALF, :], weights, preferred_element_type=f32)
        tail = jnp.concatenate([dots[half * 8 : half * 8 + 8, :], jnp.zeros((8, BLK), f32)], axis=0)
        for m in range(2):
            share = jnp.concatenate([total[:, m * BLK : (m + 1) * BLK], tail], axis=0)
            for ref in crossed:
                share = share + ref[0, half, m].astype(f32)
            if adds:
                got = adds[half][m].astype(f32)
                share = share + jnp.where(n == half, got, 0.0)
            if split:
                outs[half][m] = share.astype(bf16)
            elif len(outs) == 1:
                outs[0][0, half, m] = share.astype(bf16)
            else:
                for i in range(n_steps):

                    @pl.when(n == i)
                    def _(i=i, half=half, m=m, share=share):
                        outs[i][half, m] = share.astype(bf16)


def term_part(ids, steps, side, h, wt, dots, after, split=False, apart=False, crossed=(), adds=(), weight=0.02):
    block = pl.BlockSpec((1, 2, 2, ROWS_T, BLK), lambda n, s: (n, 0, 0, 0, 0))
    part = pl.BlockSpec((2, ROWS_T, BLK), lambda n, s: (0, 0, 0))
    sides = [
        pl.BlockSpec(
            (TERMS, BLK), lambda n, s, m=m: (0, ((s[2] ^ m) * 4 + ((s[3] + term_step(steps, n)) & 3)) * 2 + (s[4] ^ side))
        )
        for m in range(2)
    ]
    count = len(steps)
    outs, specs = [jax.ShapeDtypeStruct((count, 2, 2, ROWS_T, BLK), bf16)], [block]
    if split:
        outs, specs = [jax.ShapeDtypeStruct((2, ROWS_T, BLK), bf16)] * 2, [part] * 2
    elif apart:
        outs = [jax.ShapeDtypeStruct((2, 2, ROWS_T, BLK), bf16)] * count
        specs = [pl.BlockSpec((2, 2, ROWS_T, BLK), lambda n, s: (0, 0, 0, 0))] * count
    return pl.pallas_call(
        later(len(after), functools.partial(term_kernel, count, split, (len(crossed), len(adds)))),
        out_shape=outs,
        grid_spec=pltpu.PrefetchScalarGridSpec(
            num_scalar_prefetch=1,
            grid=(count,),
            in_specs=[ANY] * len(after)
            + [pl.BlockSpec((TOK, TERMS), lambda n, s: (0, 0)), *sides]
            + [pl.BlockSpec((16, BLK), lambda n, s: (0, 0))]
            + [block] * len(crossed)
            + [part] * len(adds),
            out_specs=specs,
        ),
        compiler_params=params(),
        cost_estimate=cost(
            4 * count * TOK * BLK * TERMS, 2 * TOK * TERMS + 2 * count * BLK * (2 * TERMS + 4 * TOK), weight
        ),
        name="term_part",
    )(ids, *after, h, wt, wt, dots, *crossed, *adds)


def term_sum_kernel(own, ra, rb, x, x_p, keep, send, dots, gain):
    sums = [jnp.zeros((8, BLK), f32) for _ in range(2)]
    for half in range(2):
        for m, values in ((0, x), (1, x_p)):
            for first in range(0, ROWS_T, 128):
                rows = slice(first, min(first + 128, ROWS_T))
                total = own[half, m, rows, :].astype(f32)
                for ref in (ra, rb):
                    total = total + ref[half, m, rows, :].astype(f32)
                if m:
                    send[half, rows, :] = total.astype(bf16)
                elif first < HALF:
                    keep[half * HALF + first : half * HALF + first + 128, :] = total.astype(bf16)
                else:
                    dots[half * 8 : half * 8 + 8, :] = total[:8]
                if first < HALF:
                    at = half * HALF + first
                    product = total * values[at : at + 128, :].astype(f32)
                    sums[m] = sums[m] + jnp.sum(product.reshape(16, 8, BLK), axis=0)
    for m in range(2):
        gain[m] = jnp.sum(sums[m], axis=0, keepdims=True)


def term_sum(after, own, ra, rb, x, x_p):
    count = len(after)
    return pl.pallas_call(
        lambda *refs: term_sum_kernel(*refs[count:]),
        out_shape=[
            jax.ShapeDtypeStruct((TOK, BLK), bf16),
            jax.ShapeDtypeStruct((2, ROWS_T, BLK), bf16),
            jax.ShapeDtypeStruct((16, BLK), f32),
            jax.ShapeDtypeStruct((2, 1, BLK), f32),
        ],
        in_specs=[ANY] * count + [VMEM] * 5,
        out_specs=[VMEM] * 4,
        compiler_params=params(),
        cost_estimate=cost(1_000_000, 5_000_000),
        name="term_sum",
    )(*after, own, ra, rb, x, x_p)


def final_kernel(ids, n_ref, got, x_ref, gain, inv_ref, dots, sums, out, sums_out):
    sums_out[...] = sums[...]
    g = gain[:, block_at(ids, ids[2] * 4 + ids[3], 0)]
    for half in range(2):
        lines = (dots[half * 8 : half * 8 + 8, :] + got[half, HALF:, :].astype(f32)[:8]) / D
        for k in range(4):
            local = slice(k * LEN, (k + 1) * LEN)
            rows = slice(half * HALF + k * LEN, half * HALF + (k + 1) * LEN)
            grad = n_ref[rows, :].astype(f32) + got[half, local, :].astype(f32)
            values = x_ref[rows, :].astype(f32)
            line = lines[k // 2 : k // 2 + 1, (k % 2) * LEN : (k % 2 + 1) * LEN]
            column = jnp.broadcast_to(line, (LEN, LEN)).T[:, 0:1]
            inverse = inv_ref[rows, :]
            out[rows, :] = (grad * g - values * (inverse * inverse * column)).astype(bf16)


def final(ids, after, n, got, x, gain, inv, dots, sums):
    return pl.pallas_call(
        later(len(after), final_kernel),
        out_shape=[jax.ShapeDtypeStruct((TOK, BLK), bf16), jax.ShapeDtypeStruct((1, BLK), f32)],
        in_specs=[SMEM] + [ANY] * len(after) + [VMEM] * 7,
        out_specs=[VMEM] * 2,
        compiler_params=params(),
        cost_estimate=cost(1_000_000, 2_000_000),
        name="hidden_grad",
    )(ids, *after, n, got, x, gain, inv, dots, sums)


def shards(hidden, norm_gain, head_weight, lengths, positives, negatives):
    xh, y, xl, z, c = (lax.axis_index(a).astype(jnp.int32) for a in ("xh", "y", "xl", "z", "c"))
    nil = jnp.int32(0)
    ids = jnp.concatenate([jnp.stack([xh, y, xl, z, c, nil, nil, nil]), positives, negatives.reshape(-1)])
    wt = head_weight.T
    gain = norm_gain.reshape(1, D)

    z_m, z_p, x_p = shift(hidden, "z", 1), shift(hidden, "z", -1), swap(hidden, "xl")
    own_c = swap(hidden, "c")
    z_m_c, z_p_c, x_p_c = (swap(a, "c") for a in (z_m, z_p, x_p))
    far, xz_p, xz_m = shift(z_m, "z", 1), shift(x_p, "z", -1), swap(z_m, "xl")
    state = forward(ids, [(0, 0), (0, -1), (1, 0)], [hidden, own_c, z_m, z_m_c, x_p, x_p_c], wt, gain)
    far, xz_p, xz_m = touch(state[1], far, xz_p, xz_m)
    last = swap(far, "xl")
    far_c, xz_p_c, xz_m_c = (swap(a, "c") for a in (far, xz_p, xz_m))
    state = forward(
        ids,
        [(0, 1), (0, 2), (1, 1), (1, -1)],
        [z_p, z_p_c, far, far_c, xz_p, xz_p_c, xz_m, xz_m_c],
        wt,
        gain,
        state,
    )
    (last,) = touch(state[1], last)
    last_c = swap(last, "c")
    acc, x, inv, weight, pooled = forward_last(ids, lengths, (1, 2), (last, last_c), wt, gain, state)

    others = [lax.ppermute(pooled, ("xh", "y"), [(i, i ^ bits) for i in range(8)]) for bits in range(1, 8)]
    every, part = gram(ids, [pooled, *others])
    part = (part + swap(part, "z", 1)) + (swap(part, "z", 2) + swap(part, "z", 3))
    both = lax.ppermute(part, ("xl", "c"), [(i, i ^ 3) for i in range(4)])
    parts = (part, swap(part, "c"), swap(part, "xl"), both)
    h, ht, dots, losses = grads(ids, every, parts, weight, acc)

    (crossing_2,) = term_part(ids, (2,), 1, h, wt, dots, ())
    (crossing,) = term_part(ids, (1, 3, 0), 1, h, wt, dots, (crossing_2,), weight=20)
    far_0, far_1, keep_2, send_2 = head_part(ids, (2,), ht, x, gain, (crossing,), split=True)
    crossed_2, crossed = swap(crossing_2, "c"), swap(crossing, "c")
    term_0, term_1 = term_part(ids, (2,), 0, h, wt, dots, (far_0, crossed), split=True, crossed=(crossed_2,))
    adds = (shift(far_0, "y", 1), shift(far_1, "y", -1))
    swap_2 = swap(send_2, "xh")
    a_1, a_3, keep_13, send_13 = head_part(ids, (1, 3), ht, x, gain, (term_0, swap_2), adds=adds, weight=20)
    swap_13 = swap(send_13, "xh")
    ra, rb = shift(a_1, "y", 1), shift(a_3, "y", -1)
    adds = (shift(term_0, "z", 1), shift(term_1, "z", -1))
    t_1, t_3, t_0 = term_part(
        ids, (1, 3, 0), 0, h, wt, dots, (a_1,), apart=True, crossed=(crossed,), adds=adds, weight=20
    )
    a_0, keep_0, send_0 = head_part(ids, (0,), ht, x, gain, (t_0,))
    swap_0 = swap(send_0, "xh")
    got = swap(a_0[1] + ra[1] + rb[1], "xh")
    low = [
        shift(keep_13[0] + swap_13[0], "y", 1),
        shift(keep_2[0] + swap_2[0], "y", 2),
        shift(keep_13[1] + swap_13[1], "y", 3),
    ]
    after = (keep_0, ra, rb, swap_13)
    keep, send, dots, partial = term_sum(after, t_0, shift(t_1, "z", 1), shift(t_3, "z", -1), hidden, x_p)
    gain_grad = partial[0] + swap(partial[1], "xl")
    gain_grad = gain_grad + swap(gain_grad, "xh")
    after = (*low, got)
    hidden_grad, gain_grad = final(ids, after, keep, swap(send, "xl"), hidden, gain, inv, dots, gain_grad)
    gain_grad = (gain_grad + swap(gain_grad, "y", 1)) + (swap(gain_grad, "y", 2) + swap(gain_grad, "y", 3))
    head_t = join(ids, hidden_grad, a_0, ra, rb, got, keep_0, swap_0, *low)
    return losses[0, :3], hidden_grad, head_t.T, gain_grad[0]


def solution(mesh):
    fine = Mesh(mesh.devices.reshape(2, 4, 2, 4, 2), ("xh", "y", "xl", "z", "c"))
    dp, vocab = ("xh", "y"), ("xl", "z", "c")
    in_specs = (P(dp, vocab), P(), P(None, vocab), P(dp), P(dp), P(dp, None))
    out_specs = (P(), P(dp, vocab), P(dp, vocab), P(vocab))
    return jax.shard_map(shards, mesh=fine, in_specs=in_specs, out_specs=out_specs, check_vma=False)
```

```python
import functools
import math

import jax
import jax.numpy as jnp
from jax import lax
from jax.experimental import pallas as pl
from jax.experimental.pallas import tpu as pltpu
from jax.sharding import Mesh, PartitionSpec as P

VOCAB = 16000
D = 4096
epsilon = 1e-05
sharpness = 80.0
flops_weight = 0.01

TOK = 1024
SEQ = 8
LEN = 128
TERMS = 1000
BLK = 256
ROWS_A = 560
ROWS_B = TERMS - ROWS_A
HALF = TOK // 2
PER = 2
SCORE_SCALE = 4.0 / math.sqrt(VOCAB)
COLS = ((0, 256), (256, 512), (512, 768), (768, 1000))
SIZES = {"xh": 2, "y": 4, "xl": 2, "z": 4, "c": 2}
VMEM_LIMIT = 67_000_000
HIGHEST = lax.Precision.HIGHEST

f32, bf16 = jnp.float32, jnp.bfloat16


def shift(x, axis, step):
    n = SIZES[axis]
    return lax.ppermute(x, axis, [(i, (i + step) % n) for i in range(n)])


def swap(x, axis, bits=1):
    return lax.ppermute(x, axis, [(i, i ^ bits) for i in range(SIZES[axis])])


def params(**more):
    return pltpu.CompilerParams(vmem_limit_bytes=VMEM_LIMIT, **more)


def cost(flops, moved, weight=0.02):
    return pl.CostEstimate(flops=int(flops * weight), bytes_accessed=int(moved * weight), transcendentals=0)


def tag(ids, pooled_ref):
    lane = lax.broadcasted_iota(jnp.int32, (1, 24), 1)
    for k in range(SEQ):
        tags = jnp.zeros((1, 24), f32)
        if k < 2:
            tags = jnp.where(lane == 0, ids[8 + k].astype(f32), tags)
            tags = jnp.where(lane == 1, ids[10 + 2 * k].astype(f32), tags)
            tags = jnp.where(lane == 2, ids[11 + 2 * k].astype(f32), tags)
        pooled_ref[k : k + 1, TERMS:] = tags


def pool(lengths, first, acc, ssq, inv_ref, weight_ref, pooled_ref):
    for s in range(acc.shape[0] // LEN):
        k = first + s
        rows = slice(s * LEN, (s + 1) * LEN)
        total = jnp.sum(ssq[rows, :], axis=1, keepdims=True)
        inverse = lax.rsqrt(total / D + epsilon)
        inv_ref[rows, :] = inverse
        count = lengths[k]
        for a, b in COLS:
            logits = acc[rows, a:b] * inverse
            valid = lax.broadcasted_iota(jnp.int32, (LEN, b - a), 0) < count
            held = jnp.where(valid, 1.0 + jnp.maximum(logits, 0.0), 1.0)
            top = jnp.max(held, axis=0, keepdims=True)
            down = 1.0 / top
            r1 = held * down
            r2 = r1 * r1
            r4 = r2 * r2
            r8 = r4 * r4
            r16 = r8 * r8
            r32 = r16 * r16
            r79 = (r32 * r32 * r8) * (r4 * (r2 * r1))
            summed = jnp.sum(jnp.where(valid, r79 * r1, 0.0), axis=0, keepdims=True)
            pooled_ref[pl.ds(k, 1), a:b] = jnp.log(top) + jnp.log(summed) / sharpness
            slope = r79 * (down / summed) * inverse
            weight_ref[rows, a:b] = jnp.where(valid & (logits > 0.0), slope, 0.0).astype(bf16)


def chip_of(ids, far_x, step):
    return (ids[2] ^ far_x) * 4 + ((ids[3] + step) & 3)


def block_at(ids, chip, side):
    return pl.ds(pl.multiple_of((chip * 2 + (ids[4] ^ side)) * BLK, BLK), BLK)


def scaled(weights, gain, ids, chip):
    row = jnp.concatenate([gain[:, block_at(ids, chip, side)] for side in range(2)], axis=1)
    return (weights.astype(f32) * row).astype(bf16)


def folded_squares(lefts):
    squares = 0.0
    for left in lefts:
        value = left.astype(f32)
        square = value * value
        squares = squares + square[:, :128] + square[:, 128:]
    return squares


def forward_kernel(places, first, ids, *refs):
    nb = len(places)
    arrays, (weights, gain), refs = refs[: 2 * nb], refs[2 * nb : 2 * nb + 2], refs[2 * nb + 2 :]
    if not first:
        (acc_in, ssq_in, _), refs = refs[:3], refs[3:]
    acc, ssq, kept, held, w_sem, x_sem = refs
    chips = [chip_of(ids, *place) for place in places]
    loads, saves = [], []
    for j in range(nb):
        for side in range(2):
            at = held.at[j, :, side * BLK : (side + 1) * BLK]
            loads.append(pltpu.make_async_copy(weights.at[:, block_at(ids, chips[j], side)], at, w_sem.at[j, side]))
            loads[-1].start()
    for j in range(nb):
        for side in range(2):
            saves.append(pltpu.make_async_copy(arrays[2 * j + side], kept.at[chips[j], side], x_sem.at[j, side]))
            saves[-1].start()
    for j in range(nb):
        loads[2 * j].wait()
        loads[2 * j + 1].wait()
        right = scaled(held[j], gain, ids, chips[j])
        for half in range(2):
            rows = slice(half * HALF, (half + 1) * HALF)
            lefts = [arrays[2 * j + side][rows, :] for side in range(2)]
            squares = folded_squares(lefts)
            product = lax.dot_general(
                jnp.concatenate(lefts, axis=1), right, (((1,), (1,)), ((), ())), preferred_element_type=f32
            )
            if j == 0 and first:
                acc[rows, :] = product
                ssq[rows, :] = squares
            elif j == 0:
                acc[rows, :] = acc_in[rows, :] + product
                ssq[rows, :] = ssq_in[rows, :] + squares
            else:
                acc[rows, :] += product
                ssq[rows, :] += squares
    for copy in saves:
        copy.wait()


SMEM = pl.BlockSpec(memory_space=pltpu.SMEM)
VMEM = pl.BlockSpec(memory_space=pltpu.VMEM)
ANY = pl.BlockSpec(memory_space=pl.ANY)


STATE = [
    jax.ShapeDtypeStruct((TOK, TERMS), f32),
    jax.ShapeDtypeStruct((TOK, 128), f32),
    jax.ShapeDtypeStruct((8, 2, TOK, BLK), bf16),
]


def forward(ids, places, arrays, weights, gain, state=()):
    nb = len(places)
    base = 3 + len(arrays)
    return pl.pallas_call(
        functools.partial(forward_kernel, places, not state),
        out_shape=STATE,
        in_specs=[SMEM] + [VMEM] * len(arrays) + [ANY, VMEM] + [VMEM, VMEM, ANY][: len(state)],
        out_specs=[VMEM, VMEM, ANY],
        scratch_shapes=[
            pltpu.VMEM((nb, TERMS, 2 * BLK), bf16),
            pltpu.SemaphoreType.DMA((nb, 2)),
            pltpu.SemaphoreType.DMA((nb, 2)),
        ],
        input_output_aliases={base + i: i for i in range(len(state))},
        compiler_params=params(),
        cost_estimate=cost(2 * nb * TOK * 512 * TERMS, nb * 3_000_000 + 8_000_000),
        name="forward_part",
    )(ids, *arrays, weights, gain, *state)


STEP = 256


def forward_last_kernel(place, ids, lengths, a0, a1, w0, w1, gain, acc_in, ssq_in, _, *refs):
    product, kept, inv_ref, weight_ref, pooled_ref, acc, right, ssq, sem = refs
    k = pl.program_id(0)
    chip = chip_of(ids, *place)

    @pl.when(k == 0)
    def _():
        right[...] = scaled(jnp.concatenate([w0[...], w1[...]], axis=1), gain, ids, chip)
        tag(ids, pooled_ref)

    rows = pl.ds(pl.multiple_of(k * STEP, STEP), STEP)
    saves = []
    for side, source in enumerate((a0, a1)):
        saves.append(pltpu.make_async_copy(source, kept.at[chip, side, rows, :], sem.at[side]))
        saves[-1].start()
    lefts = [a0[...], a1[...]]
    ssq[...] = ssq_in[...] + folded_squares(lefts)
    acc[...] = acc_in[...] + lax.dot_general(
        jnp.concatenate(lefts, axis=1), right[...], (((1,), (1,)), ((), ())), preferred_element_type=f32
    )
    product[...] = acc[...].astype(bf16)
    pool(lengths, k * (STEP // LEN), acc, ssq, inv_ref, weight_ref, pooled_ref)
    for copy in saves:
        copy.wait()


def forward_last(ids, lengths, place, arrays, weights, gain, state):
    whole = lambda k, *s: (0, 0)
    rows = lambda k, *s: (k, 0)
    sides = [
        pl.BlockSpec((TERMS, BLK), lambda k, s, n, side=side: (0, chip_of(s, *place) * 2 + (s[4] ^ side)))
        for side in range(2)
    ]
    return pl.pallas_call(
        functools.partial(forward_last_kernel, place),
        out_shape=[
            jax.ShapeDtypeStruct((TOK, TERMS), bf16),
            STATE[2],
            jax.ShapeDtypeStruct((TOK, 1), f32),
            jax.ShapeDtypeStruct((TOK, TERMS), bf16),
            jax.ShapeDtypeStruct((SEQ, 1024), f32),
        ],
        grid_spec=pltpu.PrefetchScalarGridSpec(
            num_scalar_prefetch=2,
            grid=(TOK // STEP,),
            in_specs=[pl.BlockSpec((STEP, BLK), rows)] * 2
            + [*sides, pl.BlockSpec((1, D), whole)]
            + [pl.BlockSpec((STEP, TERMS), rows), pl.BlockSpec((STEP, 128), rows), ANY],
            out_specs=[
                pl.BlockSpec((STEP, TERMS), rows),
                ANY,
                pl.BlockSpec((STEP, 1), rows),
                pl.BlockSpec((STEP, TERMS), rows),
                pl.BlockSpec((SEQ, 1024), whole),
            ],
            scratch_shapes=[
                pltpu.VMEM((STEP, TERMS), f32),
                pltpu.VMEM((TERMS, 2 * BLK), bf16),
                pltpu.VMEM((STEP, 128), f32),
                pltpu.SemaphoreType.DMA((2,)),
            ],
        ),
        input_output_aliases={9: 1},
        compiler_params=params(),
        cost_estimate=cost(2 * TOK * 512 * TERMS, 20_000_000),
        name="forward_last",
    )(ids, lengths, *arrays, weights, weights, gain, *state)


def touch_kernel(*refs):
    pass


def touch(after, *arrays):
    n = len(arrays)
    return pl.pallas_call(
        touch_kernel,
        out_shape=[jax.ShapeDtypeStruct(a.shape, a.dtype) for a in arrays],
        in_specs=[ANY] * (n + 1),
        out_specs=[ANY] * n,
        input_output_aliases={i + 1: i for i in range(n)},
        compiler_params=params(has_side_effects=True),
        cost_estimate=cost(1000, 1000),
        name="touch",
    )(after, *arrays)


def gram_kernel(ids, *refs):
    all_ref, part_ref = refs[4:]
    for bits, ref in enumerate(refs[:4]):
        for m in range(2):
            at = (ids[0] * 4 + ids[1]) ^ (4 * m + bits)
            all_ref[pl.ds(pl.multiple_of(at * SEQ, SEQ), SEQ), :] = ref[m]
    every = all_ref[:, :TERMS]
    part = lax.dot_general(every, every, (((1,), (1,)), ((), ())), precision=HIGHEST, preferred_element_type=f32)
    mean = jnp.sum(every, axis=0, keepdims=True) / 64.0
    flops = jnp.sum(mean * mean, axis=1, keepdims=True)
    part_ref[...] = jnp.zeros_like(part_ref)
    part_ref[0:64, 0:64] = part
    part_ref[64:72, :] = jnp.broadcast_to(flops, (8, 128))


def gram(ids, groups):
    return pl.pallas_call(
        gram_kernel,
        out_shape=[jax.ShapeDtypeStruct((64, 1024), f32), jax.ShapeDtypeStruct((72, 128), f32)],
        grid_spec=pltpu.PrefetchScalarGridSpec(
            num_scalar_prefetch=1,
            grid=(),
            in_specs=[VMEM] * 4,
            out_specs=[VMEM] * 2,
        ),
        compiler_params=params(),
        name="gram",
    )(ids, *groups)


def contrast(every, parts, scaled_ref, losses_ref):
    sums = (parts[0][...] + parts[1][...]) + (parts[2][...] + parts[3][...])
    scores = sums[0:64, :] * SCORE_SCALE
    row = lax.broadcasted_iota(jnp.int32, (64, 128), 0)
    col = lax.broadcasted_iota(jnp.int32, (64, 128), 1)
    is_query = (row & 7) < 2
    is_passage = ((col & 7) >= 2) & (col < 64)
    tags = every[:, TERMS:]

    def hot(at):
        index = tags[:, at : at + 1]
        group = jnp.floor((index + 0.5) * (1.0 / 6.0))
        place = group * 8.0 + 2.0 + (index - 6.0 * group)
        return (col.astype(f32) == place).astype(f32)

    positive, negatives = hot(0), (hot(1), hot(2))
    highest = jnp.max(jnp.where(is_passage, scores, -3e38), axis=1, keepdims=True)
    shifted = jnp.where(is_passage, jnp.exp(jnp.minimum(scores - highest, 0.0)), 0.0)
    denominator = jnp.sum(shifted, axis=1, keepdims=True)
    log_total = highest + jnp.log(denominator)
    positive_score = jnp.sum(scores * positive, axis=1, keepdims=True)
    query_row = is_query[:, 0:1]
    cross = jnp.sum(jnp.where(query_row, log_total - positive_score, 0.0), axis=0, keepdims=True) / 16.0
    grad = (shifted / denominator - positive) / 16.0
    margin = jnp.zeros((1, 1), f32)
    for negative in negatives:
        gap = jnp.sum(scores * negative, axis=1, keepdims=True) - positive_score
        small = jnp.exp(-jnp.abs(gap))
        soft = jnp.maximum(gap, 0.0) + jnp.log(1.0 + small)
        slope = jnp.where(gap >= 0.0, 1.0, small) / (1.0 + small) / 32.0
        margin = margin + jnp.sum(jnp.where(query_row, soft, 0.0), axis=0, keepdims=True) / 32.0
        grad = grad + slope * negative - slope * positive
    grad = jnp.where(is_query, grad, 0.0)
    square = jnp.concatenate([grad, jnp.zeros((64, 128), f32)], axis=0)
    scaled_ref[...] = (square + square.T) * SCORE_SCALE
    flops = sums[64:65, 0:1] * flops_weight
    lane = lax.broadcasted_iota(jnp.int32, (8, 128), 1)
    losses_ref[...] = jnp.where(lane == 0, cross, jnp.where(lane == 1, margin, flops))


def grad_kernel(
    ids, every, p0, p1, p2, p3, weight, acc, h_ref, ht_ref, dots, losses_ref, rep, scaled, padded
):
    k = pl.program_id(0)

    @pl.when(k == 0)
    def _():
        contrast(every, (p0, p1, p2, p3), scaled, losses_ref)
        dots[...] = jnp.zeros_like(dots)
        padded[0:64, :] = every[:, :TERMS]
        padded[64:128, :] = jnp.zeros((64, TERMS), f32)
        at = pl.multiple_of((ids[0] * 4 + ids[1]) * SEQ, SEQ)
        own = scaled[pl.ds(at, SEQ), :]
        mean = jnp.sum(padded[...], axis=0, keepdims=True) / 64.0
        rep[...] = jnp.dot(own, padded[...], precision=HIGHEST, preferred_element_type=f32) + (
            2.0 * flops_weight / 64.0
        ) * mean

    lines = []
    for s in range(PER):
        rows = slice(s * LEN, (s + 1) * LEN)
        folded = jnp.zeros((LEN, 128), f32)
        for a, b in COLS:
            grad = weight[rows, a:b].astype(f32) * rep[pl.ds(k * PER + s, 1), a:b]
            rounded = grad.astype(bf16)
            h_ref[rows, a:b] = rounded
            turned = grad.T.astype(bf16)
            ht_ref[a:b, rows] = turned
            product = rounded.astype(f32) * acc[rows, a:b].astype(f32)
            wide = b - a
            folded = folded + product[:, :128]
            if wide == 256:
                folded = folded + product[:, 128:]
            else:
                folded = folded + jnp.concatenate([product[:, 128:], jnp.zeros((LEN, 256 - wide), f32)], axis=1)
        lines.append(jnp.sum(folded.T, axis=0, keepdims=True))
    dots[pl.ds((k >> 1) * 8 + (k & 1), 1), :] = jnp.concatenate(lines, axis=1)


def grads(ids, every, parts, weight, acc):
    whole = lambda k, s: (0, 0)
    rows = lambda k, s: (k, 0)
    cols = lambda k, s: (0, k)
    return pl.pallas_call(
        grad_kernel,
        out_shape=[
            jax.ShapeDtypeStruct((TOK, TERMS), bf16),
            jax.ShapeDtypeStruct((TERMS, TOK), bf16),
            jax.ShapeDtypeStruct((16, BLK), f32),
            jax.ShapeDtypeStruct((8, 128), f32),
        ],
        grid_spec=pltpu.PrefetchScalarGridSpec(
            num_scalar_prefetch=1,
            grid=(SEQ // PER,),
            in_specs=[
                pl.BlockSpec((64, 1024), whole),
                *[pl.BlockSpec((72, 128), whole)] * 4,
                pl.BlockSpec((PER * LEN, TERMS), rows),
                pl.BlockSpec((PER * LEN, TERMS), rows),
            ],
            out_specs=[
                pl.BlockSpec((PER * LEN, TERMS), rows),
                pl.BlockSpec((TERMS, PER * LEN), cols),
                pl.BlockSpec((16, BLK), whole),
                pl.BlockSpec((8, 128), whole),
            ],
            scratch_shapes=[pltpu.VMEM((SEQ, TERMS), f32), pltpu.VMEM((128, 128), f32), pltpu.VMEM((128, TERMS), f32)],
        ),
        compiler_params=params(),
        cost_estimate=cost(20 * TOK * TERMS, 12_000_000),
        name="logit_grad",
    )(ids, every, *parts, weight, acc)


def later(count, kernel):
    return lambda ids, *refs: kernel(ids, *refs[count:])


def place_of(steps, n):
    step = steps[0]
    for i in range(1, len(steps)):
        step = jnp.where(n < 2 * i, step, steps[i])
    return step, n & 1


def head_chip(steps, ids, n):
    step, j = place_of(steps, n)
    return (ids[0] ^ j) * 4 + ((ids[1] + step) & 3)


def head_kernel(steps, split, n_add, ids, ht, x, gain, *refs):
    n = pl.program_id(0)
    adds, outs, (keep, send) = refs[:n_add], refs[n_add:-2], refs[-2:]
    block = jnp.concatenate([x[0, 0], x[0, 1]], axis=1)
    chip = head_chip(steps, ids, n)
    row = jnp.concatenate([gain[:, block_at(ids, chip, side)] for side in range(2)], axis=1)
    total = jnp.dot(ht[...], block, preferred_element_type=f32) * row
    sides = [total[:, :BLK], total[:, BLK:]]
    for i in range(len(steps)):

        @pl.when((n >> 1) == i)
        def _(i=i):
            for side in range(2):
                share = sides[side][:ROWS_A]
                if n_add and side == i:
                    share = share + adds[i][0].astype(f32)
                if split:
                    outs[side][0] = share.astype(bf16)
                else:
                    outs[i][0, side] = share.astype(bf16)

    for j, out in enumerate((keep, send)):

        @pl.when((n & 1) == j)
        def _(out=out):
            for side in range(2):
                out[0, side] = sides[side][ROWS_A:].astype(bf16)


def head_part(ids, steps, ht, x, gain, after, split=False, adds=(), weight=0.02):
    count = len(steps)
    at = lambda i: lambda n, s: (jnp.clip(n - 2 * i, 0, 1), 0, 0)
    at4 = lambda i: lambda n, s: (jnp.clip(n - 2 * i, 0, 1), 0, 0, 0)
    one = pl.BlockSpec((1, ROWS_A, BLK), at(0))
    low = pl.BlockSpec((1, 2, ROWS_B, BLK), lambda n, s: (n // 2, 0, 0, 0))
    if split:
        high, specs = [jax.ShapeDtypeStruct((2, ROWS_A, BLK), bf16)] * 2, [one, one]
    else:
        high = [jax.ShapeDtypeStruct((2, 2, ROWS_A, BLK), bf16)] * count
        specs = [pl.BlockSpec((1, 2, ROWS_A, BLK), at4(i)) for i in range(count)]
    return pl.pallas_call(
        later(len(after), functools.partial(head_kernel, steps, split, len(adds))),
        out_shape=high + [jax.ShapeDtypeStruct((count, 2, ROWS_B, BLK), bf16)] * 2,
        grid_spec=pltpu.PrefetchScalarGridSpec(
            num_scalar_prefetch=1,
            grid=(2 * count,),
            in_specs=[ANY] * len(after)
            + [
                pl.BlockSpec((TERMS, TOK), lambda n, s: (0, 0)),
                pl.BlockSpec((1, 2, TOK, BLK), lambda n, s: (head_chip(steps, s, n), 0, 0, 0)),
                pl.BlockSpec((1, D), lambda n, s: (0, 0)),
            ]
            + [pl.BlockSpec((1, ROWS_A, BLK), at(i)) for i in range(len(adds))],
            out_specs=specs + [low, low],
        ),
        compiler_params=params(),
        cost_estimate=cost(2 * TERMS * TOK * 1024 * count, 2 * TERMS * TOK + 2048 * count * (TOK + TERMS), weight),
        name="head_part",
    )(ids, *after, ht, x, gain, *adds)


def low_sum_kernel(_, a, b, *outs):
    for i, out in enumerate(outs):
        out[...] = (a[i].astype(f32) + b[i].astype(f32)).astype(bf16)


def low_sum(after, a, b):
    return pl.pallas_call(
        low_sum_kernel,
        out_shape=[jax.ShapeDtypeStruct((2, ROWS_B, BLK), bf16)] * a.shape[0],
        in_specs=[ANY, VMEM, VMEM],
        out_specs=[VMEM] * a.shape[0],
        compiler_params=params(),
        cost_estimate=cost(1000, 3_000_000),
        name="low_sum",
    )(after, a, b)


def join_kernel(ids, _, a0, ra, rb, got, keep, swapped, b1, b2, b3, out):
    for side in range(2):
        cols = pl.ds(pl.multiple_of((ids[4] ^ side) * BLK, BLK), BLK)
        total = a0[0, side].astype(f32) + ra[0, side].astype(f32) + rb[0, side].astype(f32) + got[side].astype(f32)
        out[0:ROWS_A, cols] = total.astype(bf16)
        total = keep[0, side].astype(f32) + swapped[0, side].astype(f32)
        for b in (b1, b2, b3):
            total = total + b[side].astype(f32)
        out[ROWS_A:TERMS, cols] = total.astype(bf16)


def join(ids, after, *parts):
    return pl.pallas_call(
        join_kernel,
        out_shape=jax.ShapeDtypeStruct((TERMS, 2 * BLK), bf16),
        in_specs=[SMEM, ANY] + [VMEM] * len(parts),
        out_specs=VMEM,
        compiler_params=params(),
        cost_estimate=cost(1000, 8_000_000),
        name="join",
    )(ids, after, *parts)


ROWS_T = HALF + 16


def term_step(steps, n):
    step = steps[0]
    for i in range(1, len(steps)):
        step = jnp.where(n < i, step, steps[i])
    return step


def term_kernel(n_steps, split, n_adds, ids, h, w0, w1, dots, *refs):
    n = pl.program_id(0)
    crossed, adds, outs = refs[: n_adds[0]], refs[n_adds[0] : sum(n_adds)], refs[sum(n_adds) :]
    weights = jnp.concatenate([w0[...], w1[...]], axis=1)
    for half in range(2):
        total = jnp.dot(h[half * HALF : (half + 1) * HALF, :], weights, preferred_element_type=f32)
        tail = jnp.concatenate([dots[half * 8 : half * 8 + 8, :], jnp.zeros((8, BLK), f32)], axis=0)
        for m in range(2):
            share = jnp.concatenate([total[:, m * BLK : (m + 1) * BLK], tail], axis=0)
            for ref in crossed:
                share = share + ref[0, half, m].astype(f32)
            if adds:
                got = adds[half][m].astype(f32)
                share = share + jnp.where(n == half, got, 0.0)
            if split:
                outs[half][m] = share.astype(bf16)
            elif len(outs) == 1:
                outs[0][0, half, m] = share.astype(bf16)
            else:
                for i in range(n_steps):

                    @pl.when(n == i)
                    def _(i=i, half=half, m=m, share=share):
                        outs[i][half, m] = share.astype(bf16)


def term_part(ids, steps, side, h, wt, dots, after, split=False, apart=False, crossed=(), adds=(), weight=0.02):
    block = pl.BlockSpec((1, 2, 2, ROWS_T, BLK), lambda n, s: (n, 0, 0, 0, 0))
    part = pl.BlockSpec((2, ROWS_T, BLK), lambda n, s: (0, 0, 0))
    sides = [
        pl.BlockSpec(
            (TERMS, BLK), lambda n, s, m=m: (0, ((s[2] ^ m) * 4 + ((s[3] + term_step(steps, n)) & 3)) * 2 + (s[4] ^ side))
        )
        for m in range(2)
    ]
    count = len(steps)
    outs, specs = [jax.ShapeDtypeStruct((count, 2, 2, ROWS_T, BLK), bf16)], [block]
    if split:
        outs, specs = [jax.ShapeDtypeStruct((2, ROWS_T, BLK), bf16)] * 2, [part] * 2
    elif apart:
        outs = [jax.ShapeDtypeStruct((2, 2, ROWS_T, BLK), bf16)] * count
        specs = [pl.BlockSpec((2, 2, ROWS_T, BLK), lambda n, s: (0, 0, 0, 0))] * count
    return pl.pallas_call(
        later(len(after), functools.partial(term_kernel, count, split, (len(crossed), len(adds)))),
        out_shape=outs,
        grid_spec=pltpu.PrefetchScalarGridSpec(
            num_scalar_prefetch=1,
            grid=(count,),
            in_specs=[ANY] * len(after)
            + [pl.BlockSpec((TOK, TERMS), lambda n, s: (0, 0)), *sides]
            + [pl.BlockSpec((16, BLK), lambda n, s: (0, 0))]
            + [block] * len(crossed)
            + [part] * len(adds),
            out_specs=specs,
        ),
        compiler_params=params(),
        cost_estimate=cost(
            4 * count * TOK * BLK * TERMS, 2 * TOK * TERMS + 2 * count * BLK * (2 * TERMS + 4 * TOK), weight
        ),
        name="term_part",
    )(ids, *after, h, wt, wt, dots, *crossed, *adds)


def term_sum_kernel(own, ra, rb, x, x_p, keep, send, dots, gain):
    sums = [jnp.zeros((8, BLK), f32) for _ in range(2)]
    for half in range(2):
        for m, values in ((0, x), (1, x_p)):
            for first in range(0, ROWS_T, 128):
                rows = slice(first, min(first + 128, ROWS_T))
                total = own[half, m, rows, :].astype(f32)
                for ref in (ra, rb):
                    total = total + ref[half, m, rows, :].astype(f32)
                if m:
                    send[half, rows, :] = total.astype(bf16)
                elif first < HALF:
                    keep[half * HALF + first : half * HALF + first + 128, :] = total.astype(bf16)
                else:
                    dots[half * 8 : half * 8 + 8, :] = total[:8]
                if first < HALF:
                    at = half * HALF + first
                    product = total * values[at : at + 128, :].astype(f32)
                    sums[m] = sums[m] + jnp.sum(product.reshape(16, 8, BLK), axis=0)
    gain[...] = jnp.sum(sums[0], axis=0, keepdims=True)
    other = jnp.sum(sums[1], axis=0, keepdims=True)
    high = other.astype(bf16).astype(f32)
    row = lax.broadcasted_iota(jnp.int32, (16, 1), 0)
    tail = send[0, HALF:, :].astype(f32)
    tail = jnp.where(row == 2, high, jnp.where(row == 3, other - high, tail))
    send[0, HALF:, :] = tail.astype(bf16)


def term_sum(after, own, ra, rb, x, x_p):
    count = len(after)
    return pl.pallas_call(
        lambda *refs: term_sum_kernel(*refs[count:]),
        out_shape=[
            jax.ShapeDtypeStruct((TOK, BLK), bf16),
            jax.ShapeDtypeStruct((2, ROWS_T, BLK), bf16),
            jax.ShapeDtypeStruct((16, BLK), f32),
            jax.ShapeDtypeStruct((1, BLK), f32),
        ],
        in_specs=[ANY] * count + [VMEM] * 5,
        out_specs=[VMEM] * 4,
        compiler_params=params(),
        cost_estimate=cost(1_000_000, 5_000_000),
        name="term_sum",
    )(*after, own, ra, rb, x, x_p)


def final_kernel(ids, n_ref, got, x_ref, gain, inv_ref, dots, sums, out, sums_out):
    tail = got[0, HALF:, :].astype(f32)
    sums_out[...] = sums[...] + tail[2:3] + tail[3:4]
    g = gain[:, block_at(ids, ids[2] * 4 + ids[3], 0)]
    for half in range(2):
        lines = (dots[half * 8 : half * 8 + 8, :] + got[half, HALF:, :].astype(f32)[:8]) / D
        for k in range(4):
            local = slice(k * LEN, (k + 1) * LEN)
            rows = slice(half * HALF + k * LEN, half * HALF + (k + 1) * LEN)
            grad = n_ref[rows, :].astype(f32) + got[half, local, :].astype(f32)
            values = x_ref[rows, :].astype(f32)
            line = lines[k // 2 : k // 2 + 1, (k % 2) * LEN : (k % 2 + 1) * LEN]
            column = jnp.broadcast_to(line, (LEN, LEN)).T[:, 0:1]
            inverse = inv_ref[rows, :]
            out[rows, :] = (grad * g - values * (inverse * inverse * column)).astype(bf16)


def final(ids, after, n, got, x, gain, inv, dots, sums):
    return pl.pallas_call(
        later(len(after), final_kernel),
        out_shape=[jax.ShapeDtypeStruct((TOK, BLK), bf16), jax.ShapeDtypeStruct((1, BLK), f32)],
        in_specs=[SMEM] + [ANY] * len(after) + [VMEM] * 7,
        out_specs=[VMEM] * 2,
        compiler_params=params(),
        cost_estimate=cost(1_000_000, 2_000_000),
        name="hidden_grad",
    )(ids, *after, n, got, x, gain, inv, dots, sums)


def gain_sum_kernel(_, a, b, out):
    out[...] = a[...] + b[...]


def gain_sum(after, a, b):
    return pl.pallas_call(
        gain_sum_kernel,
        out_shape=jax.ShapeDtypeStruct((1, BLK), f32),
        in_specs=[ANY] + [VMEM] * 2,
        out_specs=VMEM,
        compiler_params=params(),
        cost_estimate=cost(1000, 5000),
        name="gain_sum",
    )(after, a, b)


def shards(hidden, norm_gain, head_weight, lengths, positives, negatives):
    xh, y, xl, z, c = (lax.axis_index(a).astype(jnp.int32) for a in ("xh", "y", "xl", "z", "c"))
    nil = jnp.int32(0)
    ids = jnp.concatenate([jnp.stack([xh, y, xl, z, c, nil, nil, nil]), positives, negatives.reshape(-1)])
    wt = head_weight.T
    gain = norm_gain.reshape(1, D)

    z_m, z_p, x_p = shift(hidden, "z", 1), shift(hidden, "z", -1), swap(hidden, "xl")
    own_c = swap(hidden, "c")
    z_m_c, z_p_c, x_p_c = (swap(a, "c") for a in (z_m, z_p, x_p))
    far, xz_p, xz_m = shift(z_m, "z", 1), shift(x_p, "z", -1), swap(z_m, "xl")
    state = forward(ids, [(0, 0), (0, -1), (1, 0)], [hidden, own_c, z_m, z_m_c, x_p, x_p_c], wt, gain)
    far, xz_p, xz_m = touch(state[1], far, xz_p, xz_m)
    last = swap(far, "xl")
    far_c, xz_p_c, xz_m_c = (swap(a, "c") for a in (far, xz_p, xz_m))
    state = forward(
        ids,
        [(0, 1), (0, 2), (1, 1), (1, -1)],
        [z_p, z_p_c, far, far_c, xz_p, xz_p_c, xz_m, xz_m_c],
        wt,
        gain,
        state,
    )
    (last,) = touch(state[1], last)
    last_c = swap(last, "c")
    acc, x, inv, weight, pooled = forward_last(ids, lengths, (1, 2), (last, last_c), wt, gain, state)

    pair = jnp.stack([pooled, swap(pooled, "xh")])
    every, part = gram(ids, [pair] + [swap(pair, "y", bits) for bits in (1, 2, 3)])
    part = (part + swap(part, "z", 1)) + (swap(part, "z", 2) + swap(part, "z", 3))
    both = lax.ppermute(part, ("xl", "c"), [(i, i ^ 3) for i in range(4)])
    parts = (part, swap(part, "c"), swap(part, "xl"), both)
    h, ht, dots, losses = grads(ids, every, parts, weight, acc)

    (crossing_2,) = term_part(ids, (2,), 1, h, wt, dots, ())
    (crossing,) = term_part(ids, (1, 3, 0), 1, h, wt, dots, (crossing_2,), weight=20)
    crossed_2, crossed = swap(crossing_2, "c"), swap(crossing, "c")
    term_0, term_1 = term_part(ids, (2,), 0, h, wt, dots, (crossing,), split=True, crossed=(crossed_2,))
    far_0, far_1, keep_2, send_2 = head_part(ids, (2,), ht, x, gain, (term_0,), split=True, weight=20)
    swap_2 = swap(send_2, "xh")
    adds = (shift(term_0, "z", 1), shift(term_1, "z", -1))
    t_1, t_3, t_0 = term_part(
        ids, (1, 3, 0), 0, h, wt, dots, (far_0,), apart=True, crossed=(crossed,), adds=adds, weight=20
    )
    adds = (shift(far_0, "y", 1), shift(far_1, "y", -1))
    a_1, a_3, keep_13, send_13 = head_part(ids, (1, 3), ht, x, gain, (t_0, swap_2), adds=adds, weight=20)
    swap_13 = swap(send_13, "xh")
    ra, rb = shift(a_1, "y", 1), shift(a_3, "y", -1)
    a_0, keep_0, send_0 = head_part(ids, (0,), ht, x, gain, (a_1,))
    keep, send, dots, partial = term_sum((keep_0,), t_0, shift(t_1, "z", 1), shift(t_3, "z", -1), hidden, x_p)
    swap_0 = swap(send_0, "xh")
    got = swap(a_0[1] + ra[1] + rb[1], "xh")
    low_1, low_3 = low_sum(keep, keep_13, swap_13)
    low = [shift(low_1, "y", 1), shift(keep_2[0] + swap_2[0], "y", 2), shift(low_3, "y", 3)]
    hidden_grad, gain_grad = final(ids, low, keep, swap(send, "xl"), hidden, gain, inv, dots, partial)
    gain_grad = (gain_grad + swap(gain_grad, "y", 1)) + (swap(gain_grad, "y", 2) + swap(gain_grad, "y", 3))
    head_t = join(ids, hidden_grad, a_0, ra, rb, got, keep_0, swap_0, *low)
    return losses[0, :3], hidden_grad, head_t.T, gain_sum(head_t, gain_grad, swap(gain_grad, "xh"))[0]


def solution(mesh):
    fine = Mesh(mesh.devices.reshape(2, 4, 2, 4, 2), ("xh", "y", "xl", "z", "c"))
    dp, vocab = ("xh", "y"), ("xl", "z", "c")
    in_specs = (P(dp, vocab), P(), P(None, vocab), P(dp), P(dp), P(dp, None))
    out_specs = (P(), P(dp, vocab), P(dp, vocab), P(vocab))
    return jax.shard_map(shards, mesh=fine, in_specs=in_specs, out_specs=out_specs, check_vma=False)
```

```python
import functools
import math

import jax
import jax.numpy as jnp
from jax import lax
from jax.experimental import pallas as pl
from jax.experimental.pallas import tpu as pltpu
from jax.sharding import Mesh, PartitionSpec as P

VOCAB = 16000
D = 4096
epsilon = 1e-05
sharpness = 80.0
flops_weight = 0.01

TOK = 1024
SEQ = 8
LEN = 128
TERMS = 1000
BLK = 256
ROWS_A = 560
ROWS_B = TERMS - ROWS_A
HALF = TOK // 2
PER = 2
SCORE_SCALE = 4.0 / math.sqrt(VOCAB)
COLS = ((0, 256), (256, 512), (512, 768), (768, 1000))
SIZES = {"xh": 2, "y": 4, "xl": 2, "z": 4, "c": 2}
VMEM_LIMIT = 67_000_000
HIGHEST = lax.Precision.HIGHEST

f32, bf16 = jnp.float32, jnp.bfloat16


def shift(x, axis, step):
    n = SIZES[axis]
    return lax.ppermute(x, axis, [(i, (i + step) % n) for i in range(n)])


def swap(x, axis, bits=1):
    return lax.ppermute(x, axis, [(i, i ^ bits) for i in range(SIZES[axis])])


def params(**more):
    return pltpu.CompilerParams(vmem_limit_bytes=VMEM_LIMIT, **more)


def cost(flops, moved, weight=0.02):
    return pl.CostEstimate(flops=int(flops * weight), bytes_accessed=int(moved * weight), transcendentals=0)


def tag(ids, pooled_ref):
    lane = lax.broadcasted_iota(jnp.int32, (1, 24), 1)
    for k in range(SEQ):
        tags = jnp.zeros((1, 24), f32)
        if k < 2:
            tags = jnp.where(lane == 0, ids[8 + k].astype(f32), tags)
            tags = jnp.where(lane == 1, ids[10 + 2 * k].astype(f32), tags)
            tags = jnp.where(lane == 2, ids[11 + 2 * k].astype(f32), tags)
        pooled_ref[k : k + 1, TERMS:] = tags


def pool(lengths, first, acc, ssq, inv_ref, weight_ref, pooled_ref):
    for s in range(acc.shape[0] // LEN):
        k = first + s
        rows = slice(s * LEN, (s + 1) * LEN)
        total = jnp.sum(ssq[rows, :], axis=1, keepdims=True)
        inverse = lax.rsqrt(total / D + epsilon)
        inv_ref[rows, :] = inverse
        count = lengths[k]
        for a, b in COLS:
            logits = acc[rows, a:b] * inverse
            valid = lax.broadcasted_iota(jnp.int32, (LEN, b - a), 0) < count
            held = jnp.where(valid, 1.0 + jnp.maximum(logits, 0.0), 1.0)
            top = jnp.max(held, axis=0, keepdims=True)
            down = 1.0 / top
            r1 = held * down
            r2 = r1 * r1
            r4 = r2 * r2
            r8 = r4 * r4
            r16 = r8 * r8
            r32 = r16 * r16
            r79 = (r32 * r32 * r8) * (r4 * (r2 * r1))
            summed = jnp.sum(jnp.where(valid, r79 * r1, 0.0), axis=0, keepdims=True)
            pooled_ref[pl.ds(k, 1), a:b] = jnp.log(top) + jnp.log(summed) / sharpness
            slope = r79 * (down / summed) * inverse
            weight_ref[rows, a:b] = jnp.where(valid & (logits > 0.0), slope, 0.0).astype(bf16)


def chip_of(ids, far_x, step):
    return (ids[2] ^ far_x) * 4 + ((ids[3] + step) & 3)


def block_at(ids, chip, side):
    return pl.ds(pl.multiple_of((chip * 2 + (ids[4] ^ side)) * BLK, BLK), BLK)


def scaled(weights, gain, ids, chip):
    row = jnp.concatenate([gain[:, block_at(ids, chip, side)] for side in range(2)], axis=1)
    return (weights.astype(f32) * row).astype(bf16)


def folded_squares(lefts):
    squares = 0.0
    for left in lefts:
        value = left.astype(f32)
        square = value * value
        squares = squares + square[:, :128] + square[:, 128:]
    return squares


def forward_kernel(places, first, ids, *refs):
    nb = len(places)
    arrays, (weights, gain), refs = refs[: 2 * nb], refs[2 * nb : 2 * nb + 2], refs[2 * nb + 2 :]
    if not first:
        (acc_in, ssq_in, _), refs = refs[:3], refs[3:]
    acc, ssq, kept, held, w_sem, x_sem = refs
    chips = [chip_of(ids, *place) for place in places]
    loads, saves = [], []
    for j in range(nb):
        for side in range(2):
            at = held.at[j, :, side * BLK : (side + 1) * BLK]
            loads.append(pltpu.make_async_copy(weights.at[:, block_at(ids, chips[j], side)], at, w_sem.at[j, side]))
            loads[-1].start()
    for j in range(nb):
        for side in range(2):
            saves.append(pltpu.make_async_copy(arrays[2 * j + side], kept.at[chips[j], side], x_sem.at[j, side]))
            saves[-1].start()
    for j in range(nb):
        loads[2 * j].wait()
        loads[2 * j + 1].wait()
        right = scaled(held[j], gain, ids, chips[j])
        for half in range(2):
            rows = slice(half * HALF, (half + 1) * HALF)
            lefts = [arrays[2 * j + side][rows, :] for side in range(2)]
            squares = folded_squares(lefts)
            product = lax.dot_general(
                jnp.concatenate(lefts, axis=1), right, (((1,), (1,)), ((), ())), preferred_element_type=f32
            )
            if j == 0 and first:
                acc[rows, :] = product
                ssq[rows, :] = squares
            elif j == 0:
                acc[rows, :] = acc_in[rows, :] + product
                ssq[rows, :] = ssq_in[rows, :] + squares
            else:
                acc[rows, :] += product
                ssq[rows, :] += squares
    for copy in saves:
        copy.wait()


SMEM = pl.BlockSpec(memory_space=pltpu.SMEM)
VMEM = pl.BlockSpec(memory_space=pltpu.VMEM)
ANY = pl.BlockSpec(memory_space=pl.ANY)


STATE = [
    jax.ShapeDtypeStruct((TOK, TERMS), f32),
    jax.ShapeDtypeStruct((TOK, 128), f32),
    jax.ShapeDtypeStruct((8, 2, TOK, BLK), bf16),
]


def forward(ids, places, arrays, weights, gain, state=()):
    nb = len(places)
    base = 3 + len(arrays)
    return pl.pallas_call(
        functools.partial(forward_kernel, places, not state),
        out_shape=STATE,
        in_specs=[SMEM] + [VMEM] * len(arrays) + [ANY, VMEM] + [VMEM, VMEM, ANY][: len(state)],
        out_specs=[VMEM, VMEM, ANY],
        scratch_shapes=[
            pltpu.VMEM((nb, TERMS, 2 * BLK), bf16),
            pltpu.SemaphoreType.DMA((nb, 2)),
            pltpu.SemaphoreType.DMA((nb, 2)),
        ],
        input_output_aliases={base + i: i for i in range(len(state))},
        compiler_params=params(),
        cost_estimate=cost(2 * nb * TOK * 512 * TERMS, nb * 3_000_000 + 8_000_000),
        name="forward_part",
    )(ids, *arrays, weights, gain, *state)


STEP = 256


def forward_last_kernel(place, ids, lengths, a0, a1, w0, w1, gain, acc_in, ssq_in, _, *refs):
    product, kept, inv_ref, weight_ref, pooled_ref, acc, right, ssq, sem = refs
    k = pl.program_id(0)
    chip = chip_of(ids, *place)

    @pl.when(k == 0)
    def _():
        right[...] = scaled(jnp.concatenate([w0[...], w1[...]], axis=1), gain, ids, chip)
        tag(ids, pooled_ref)

    rows = pl.ds(pl.multiple_of(k * STEP, STEP), STEP)
    saves = []
    for side, source in enumerate((a0, a1)):
        saves.append(pltpu.make_async_copy(source, kept.at[chip, side, rows, :], sem.at[side]))
        saves[-1].start()
    lefts = [a0[...], a1[...]]
    ssq[...] = ssq_in[...] + folded_squares(lefts)
    acc[...] = acc_in[...] + lax.dot_general(
        jnp.concatenate(lefts, axis=1), right[...], (((1,), (1,)), ((), ())), preferred_element_type=f32
    )
    product[...] = acc[...].astype(bf16)
    pool(lengths, k * (STEP // LEN), acc, ssq, inv_ref, weight_ref, pooled_ref)
    for copy in saves:
        copy.wait()


def forward_last(ids, lengths, place, arrays, weights, gain, state):
    whole = lambda k, *s: (0, 0)
    rows = lambda k, *s: (k, 0)
    sides = [
        pl.BlockSpec((TERMS, BLK), lambda k, s, n, side=side: (0, chip_of(s, *place) * 2 + (s[4] ^ side)))
        for side in range(2)
    ]
    return pl.pallas_call(
        functools.partial(forward_last_kernel, place),
        out_shape=[
            jax.ShapeDtypeStruct((TOK, TERMS), bf16),
            STATE[2],
            jax.ShapeDtypeStruct((TOK, 1), f32),
            jax.ShapeDtypeStruct((TOK, TERMS), bf16),
            jax.ShapeDtypeStruct((SEQ, 1024), f32),
        ],
        grid_spec=pltpu.PrefetchScalarGridSpec(
            num_scalar_prefetch=2,
            grid=(TOK // STEP,),
            in_specs=[pl.BlockSpec((STEP, BLK), rows)] * 2
            + [*sides, pl.BlockSpec((1, D), whole)]
            + [pl.BlockSpec((STEP, TERMS), rows), pl.BlockSpec((STEP, 128), rows), ANY],
            out_specs=[
                pl.BlockSpec((STEP, TERMS), rows),
                ANY,
                pl.BlockSpec((STEP, 1), rows),
                pl.BlockSpec((STEP, TERMS), rows),
                pl.BlockSpec((SEQ, 1024), whole),
            ],
            scratch_shapes=[
                pltpu.VMEM((STEP, TERMS), f32),
                pltpu.VMEM((TERMS, 2 * BLK), bf16),
                pltpu.VMEM((STEP, 128), f32),
                pltpu.SemaphoreType.DMA((2,)),
            ],
        ),
        input_output_aliases={9: 1},
        compiler_params=params(),
        cost_estimate=cost(2 * TOK * 512 * TERMS, 20_000_000),
        name="forward_last",
    )(ids, lengths, *arrays, weights, weights, gain, *state)


def touch_kernel(*refs):
    pass


def touch(after, *arrays):
    n = len(arrays)
    return pl.pallas_call(
        touch_kernel,
        out_shape=[jax.ShapeDtypeStruct(a.shape, a.dtype) for a in arrays],
        in_specs=[ANY] * (n + 1),
        out_specs=[ANY] * n,
        input_output_aliases={i + 1: i for i in range(n)},
        compiler_params=params(has_side_effects=True),
        cost_estimate=cost(1000, 1000),
        name="touch",
    )(after, *arrays)


def gram_kernel(ids, *refs):
    all_ref, part_ref = refs[4:]
    for bits, ref in enumerate(refs[:4]):
        for m in range(2):
            at = (ids[0] * 4 + ids[1]) ^ (4 * m + bits)
            all_ref[pl.ds(pl.multiple_of(at * SEQ, SEQ), SEQ), :] = ref[m]
    every = all_ref[:, :TERMS]
    part = lax.dot_general(every, every, (((1,), (1,)), ((), ())), precision=HIGHEST, preferred_element_type=f32)
    mean = jnp.sum(every, axis=0, keepdims=True) / 64.0
    flops = jnp.sum(mean * mean, axis=1, keepdims=True)
    part_ref[...] = jnp.zeros_like(part_ref)
    part_ref[0:64, 0:64] = part
    part_ref[64:72, :] = jnp.broadcast_to(flops, (8, 128))


def gram(ids, groups):
    return pl.pallas_call(
        gram_kernel,
        out_shape=[jax.ShapeDtypeStruct((64, 1024), f32), jax.ShapeDtypeStruct((72, 128), f32)],
        grid_spec=pltpu.PrefetchScalarGridSpec(
            num_scalar_prefetch=1,
            grid=(),
            in_specs=[VMEM] * 4,
            out_specs=[VMEM] * 2,
        ),
        compiler_params=params(),
        name="gram",
    )(ids, *groups)


def contrast(every, parts, scaled_ref, losses_ref):
    sums = (parts[0][...] + parts[1][...]) + (parts[2][...] + parts[3][...])
    scores = sums[0:64, :] * SCORE_SCALE
    row = lax.broadcasted_iota(jnp.int32, (64, 128), 0)
    col = lax.broadcasted_iota(jnp.int32, (64, 128), 1)
    is_query = (row & 7) < 2
    is_passage = ((col & 7) >= 2) & (col < 64)
    tags = every[:, TERMS:]

    def hot(at):
        index = tags[:, at : at + 1]
        group = jnp.floor((index + 0.5) * (1.0 / 6.0))
        place = group * 8.0 + 2.0 + (index - 6.0 * group)
        return (col.astype(f32) == place).astype(f32)

    positive, negatives = hot(0), (hot(1), hot(2))
    highest = jnp.max(jnp.where(is_passage, scores, -3e38), axis=1, keepdims=True)
    shifted = jnp.where(is_passage, jnp.exp(jnp.minimum(scores - highest, 0.0)), 0.0)
    denominator = jnp.sum(shifted, axis=1, keepdims=True)
    log_total = highest + jnp.log(denominator)
    positive_score = jnp.sum(scores * positive, axis=1, keepdims=True)
    query_row = is_query[:, 0:1]
    cross = jnp.sum(jnp.where(query_row, log_total - positive_score, 0.0), axis=0, keepdims=True) / 16.0
    grad = (shifted / denominator - positive) / 16.0
    margin = jnp.zeros((1, 1), f32)
    for negative in negatives:
        gap = jnp.sum(scores * negative, axis=1, keepdims=True) - positive_score
        small = jnp.exp(-jnp.abs(gap))
        soft = jnp.maximum(gap, 0.0) + jnp.log(1.0 + small)
        slope = jnp.where(gap >= 0.0, 1.0, small) / (1.0 + small) / 32.0
        margin = margin + jnp.sum(jnp.where(query_row, soft, 0.0), axis=0, keepdims=True) / 32.0
        grad = grad + slope * negative - slope * positive
    grad = jnp.where(is_query, grad, 0.0)
    square = jnp.concatenate([grad, jnp.zeros((64, 128), f32)], axis=0)
    scaled_ref[...] = (square + square.T) * SCORE_SCALE
    flops = sums[64:65, 0:1] * flops_weight
    lane = lax.broadcasted_iota(jnp.int32, (8, 128), 1)
    losses_ref[...] = jnp.where(lane == 0, cross, jnp.where(lane == 1, margin, flops))


def grad_kernel(
    ids, every, p0, p1, p2, p3, weight, acc, h_ref, ht_ref, dots, losses_ref, rep, scaled, padded
):
    k = pl.program_id(0)

    @pl.when(k == 0)
    def _():
        contrast(every, (p0, p1, p2, p3), scaled, losses_ref)
        dots[...] = jnp.zeros_like(dots)
        padded[0:64, :] = every[:, :TERMS]
        padded[64:128, :] = jnp.zeros((64, TERMS), f32)
        at = pl.multiple_of((ids[0] * 4 + ids[1]) * SEQ, SEQ)
        own = scaled[pl.ds(at, SEQ), :]
        mean = jnp.sum(padded[...], axis=0, keepdims=True) / 64.0
        rep[...] = jnp.dot(own, padded[...], precision=HIGHEST, preferred_element_type=f32) + (
            2.0 * flops_weight / 64.0
        ) * mean

    lines = []
    for s in range(PER):
        rows = slice(s * LEN, (s + 1) * LEN)
        folded = jnp.zeros((LEN, 128), f32)
        for a, b in COLS:
            grad = weight[rows, a:b].astype(f32) * rep[pl.ds(k * PER + s, 1), a:b]
            rounded = grad.astype(bf16)
            h_ref[rows, a:b] = rounded
            turned = grad.T.astype(bf16)
            ht_ref[a:b, rows] = turned
            product = rounded.astype(f32) * acc[rows, a:b].astype(f32)
            wide = b - a
            folded = folded + product[:, :128]
            if wide == 256:
                folded = folded + product[:, 128:]
            else:
                folded = folded + jnp.concatenate([product[:, 128:], jnp.zeros((LEN, 256 - wide), f32)], axis=1)
        lines.append(jnp.sum(folded.T, axis=0, keepdims=True))
    dots[pl.ds((k >> 1) * 8 + (k & 1), 1), :] = jnp.concatenate(lines, axis=1)


def grads(ids, every, parts, weight, acc):
    whole = lambda k, s: (0, 0)
    rows = lambda k, s: (k, 0)
    cols = lambda k, s: (0, k)
    return pl.pallas_call(
        grad_kernel,
        out_shape=[
            jax.ShapeDtypeStruct((TOK, TERMS), bf16),
            jax.ShapeDtypeStruct((TERMS, TOK), bf16),
            jax.ShapeDtypeStruct((16, BLK), f32),
            jax.ShapeDtypeStruct((8, 128), f32),
        ],
        grid_spec=pltpu.PrefetchScalarGridSpec(
            num_scalar_prefetch=1,
            grid=(SEQ // PER,),
            in_specs=[
                pl.BlockSpec((64, 1024), whole),
                *[pl.BlockSpec((72, 128), whole)] * 4,
                pl.BlockSpec((PER * LEN, TERMS), rows),
                pl.BlockSpec((PER * LEN, TERMS), rows),
            ],
            out_specs=[
                pl.BlockSpec((PER * LEN, TERMS), rows),
                pl.BlockSpec((TERMS, PER * LEN), cols),
                pl.BlockSpec((16, BLK), whole),
                pl.BlockSpec((8, 128), whole),
            ],
            scratch_shapes=[pltpu.VMEM((SEQ, TERMS), f32), pltpu.VMEM((128, 128), f32), pltpu.VMEM((128, TERMS), f32)],
        ),
        compiler_params=params(),
        cost_estimate=cost(20 * TOK * TERMS, 12_000_000),
        name="logit_grad",
    )(ids, every, *parts, weight, acc)


def later(count, kernel):
    return lambda ids, *refs: kernel(ids, *refs[count:])


def place_of(steps, n):
    step = steps[0]
    for i in range(1, len(steps)):
        step = jnp.where(n < 2 * i, step, steps[i])
    return step, n & 1


def head_chip(steps, ids, n):
    step, j = place_of(steps, n)
    return (ids[0] ^ j) * 4 + ((ids[1] + step) & 3)


def head_kernel(steps, split, n_add, ids, ht, x, gain, *refs):
    n = pl.program_id(0)
    adds, outs, (keep, send) = refs[:n_add], refs[n_add:-2], refs[-2:]
    block = jnp.concatenate([x[0, 0], x[0, 1]], axis=1)
    chip = head_chip(steps, ids, n)
    row = jnp.concatenate([gain[:, block_at(ids, chip, side)] for side in range(2)], axis=1)
    total = jnp.dot(ht[...], block, preferred_element_type=f32) * row
    sides = [total[:, :BLK], total[:, BLK:]]
    for i in range(len(steps)):

        @pl.when((n >> 1) == i)
        def _(i=i):
            for side in range(2):
                share = sides[side][:ROWS_A]
                if n_add and side == i:
                    share = share + adds[i][0].astype(f32)
                if split:
                    outs[side][0] = share.astype(bf16)
                else:
                    outs[i][0, side] = share.astype(bf16)

    for j, out in enumerate((keep, send)):

        @pl.when((n & 1) == j)
        def _(out=out):
            for side in range(2):
                out[0, side] = sides[side][ROWS_A:].astype(bf16)


def head_part(ids, steps, ht, x, gain, after, split=False, adds=(), weight=0.02):
    count = len(steps)
    at = lambda i: lambda n, s: (jnp.clip(n - 2 * i, 0, 1), 0, 0)
    at4 = lambda i: lambda n, s: (jnp.clip(n - 2 * i, 0, 1), 0, 0, 0)
    one = pl.BlockSpec((1, ROWS_A, BLK), at(0))
    low = pl.BlockSpec((1, 2, ROWS_B, BLK), lambda n, s: (n // 2, 0, 0, 0))
    if split:
        high, specs = [jax.ShapeDtypeStruct((2, ROWS_A, BLK), bf16)] * 2, [one, one]
    else:
        high = [jax.ShapeDtypeStruct((2, 2, ROWS_A, BLK), bf16)] * count
        specs = [pl.BlockSpec((1, 2, ROWS_A, BLK), at4(i)) for i in range(count)]
    return pl.pallas_call(
        later(len(after), functools.partial(head_kernel, steps, split, len(adds))),
        out_shape=high + [jax.ShapeDtypeStruct((count, 2, ROWS_B, BLK), bf16)] * 2,
        grid_spec=pltpu.PrefetchScalarGridSpec(
            num_scalar_prefetch=1,
            grid=(2 * count,),
            in_specs=[ANY] * len(after)
            + [
                pl.BlockSpec((TERMS, TOK), lambda n, s: (0, 0)),
                pl.BlockSpec((1, 2, TOK, BLK), lambda n, s: (head_chip(steps, s, n), 0, 0, 0)),
                pl.BlockSpec((1, D), lambda n, s: (0, 0)),
            ]
            + [pl.BlockSpec((1, ROWS_A, BLK), at(i)) for i in range(len(adds))],
            out_specs=specs + [low, low],
        ),
        compiler_params=params(),
        cost_estimate=cost(2 * TERMS * TOK * 1024 * count, 2 * TERMS * TOK + 2048 * count * (TOK + TERMS), weight),
        name="head_part",
    )(ids, *after, ht, x, gain, *adds)


def low_sum_kernel(_, a13, b13, a2, b2, out_1, out_3, out_2):
    for a, b, i, out in ((a13, b13, 0, out_1), (a13, b13, 1, out_3), (a2, b2, 0, out_2)):
        out[...] = (a[i].astype(f32) + b[i].astype(f32)).astype(bf16)


def low_sum(after, *parts):
    return pl.pallas_call(
        low_sum_kernel,
        out_shape=[jax.ShapeDtypeStruct((2, ROWS_B, BLK), bf16)] * 3,
        in_specs=[ANY] + [VMEM] * 4,
        out_specs=[VMEM] * 3,
        compiler_params=params(),
        cost_estimate=cost(1000, 4_000_000),
        name="low_sum",
    )(after, *parts)


def join_kernel(ids, _, a0, ra, rb, got, keep, swapped, b1, b2, b3, out):
    for side in range(2):
        cols = pl.ds(pl.multiple_of((ids[4] ^ side) * BLK, BLK), BLK)
        total = a0[0, side].astype(f32) + ra[0, side].astype(f32) + rb[0, side].astype(f32) + got[side].astype(f32)
        out[0:ROWS_A, cols] = total.astype(bf16)
        total = keep[0, side].astype(f32) + swapped[0, side].astype(f32)
        for b in (b1, b2, b3):
            total = total + b[side].astype(f32)
        out[ROWS_A:TERMS, cols] = total.astype(bf16)


def join(ids, after, *parts):
    return pl.pallas_call(
        join_kernel,
        out_shape=jax.ShapeDtypeStruct((TERMS, 2 * BLK), bf16),
        in_specs=[SMEM, ANY] + [VMEM] * len(parts),
        out_specs=VMEM,
        compiler_params=params(),
        cost_estimate=cost(1000, 8_000_000),
        name="join",
    )(ids, after, *parts)


ROWS_T = HALF + 16


def term_step(steps, n):
    step = steps[0]
    for i in range(1, len(steps)):
        step = jnp.where(n < i, step, steps[i])
    return step


def term_kernel(n_steps, split, n_adds, ids, h, w0, w1, dots, *refs):
    n = pl.program_id(0)
    crossed, adds, outs = refs[: n_adds[0]], refs[n_adds[0] : sum(n_adds)], refs[sum(n_adds) :]
    weights = jnp.concatenate([w0[...], w1[...]], axis=1)
    for half in range(2):
        total = jnp.dot(h[half * HALF : (half + 1) * HALF, :], weights, preferred_element_type=f32)
        tail = jnp.concatenate([dots[half * 8 : half * 8 + 8, :], jnp.zeros((8, BLK), f32)], axis=0)
        for m in range(2):
            share = jnp.concatenate([total[:, m * BLK : (m + 1) * BLK], tail], axis=0)
            for ref in crossed:
                share = share + ref[0, half, m].astype(f32)
            if adds:
                got = adds[half][m].astype(f32)
                share = share + jnp.where(n == half, got, 0.0)
            if split:
                outs[half][m] = share.astype(bf16)
            elif len(outs) == 1:
                outs[0][0, half, m] = share.astype(bf16)
            else:
                for i in range(n_steps):

                    @pl.when(n == i)
                    def _(i=i, half=half, m=m, share=share):
                        outs[i][half, m] = share.astype(bf16)


def term_part(ids, steps, side, h, wt, dots, after, split=False, apart=False, crossed=(), adds=(), weight=0.02):
    block = pl.BlockSpec((1, 2, 2, ROWS_T, BLK), lambda n, s: (n, 0, 0, 0, 0))
    part = pl.BlockSpec((2, ROWS_T, BLK), lambda n, s: (0, 0, 0))
    sides = [
        pl.BlockSpec(
            (TERMS, BLK), lambda n, s, m=m: (0, ((s[2] ^ m) * 4 + ((s[3] + term_step(steps, n)) & 3)) * 2 + (s[4] ^ side))
        )
        for m in range(2)
    ]
    count = len(steps)
    outs, specs = [jax.ShapeDtypeStruct((count, 2, 2, ROWS_T, BLK), bf16)], [block]
    if split:
        outs, specs = [jax.ShapeDtypeStruct((2, ROWS_T, BLK), bf16)] * 2, [part] * 2
    elif apart:
        outs = [jax.ShapeDtypeStruct((2, 2, ROWS_T, BLK), bf16)] * count
        specs = [pl.BlockSpec((2, 2, ROWS_T, BLK), lambda n, s: (0, 0, 0, 0))] * count
    return pl.pallas_call(
        later(len(after), functools.partial(term_kernel, count, split, (len(crossed), len(adds)))),
        out_shape=outs,
        grid_spec=pltpu.PrefetchScalarGridSpec(
            num_scalar_prefetch=1,
            grid=(count,),
            in_specs=[ANY] * len(after)
            + [pl.BlockSpec((TOK, TERMS), lambda n, s: (0, 0)), *sides]
            + [pl.BlockSpec((16, BLK), lambda n, s: (0, 0))]
            + [block] * len(crossed)
            + [part] * len(adds),
            out_specs=specs,
        ),
        compiler_params=params(),
        cost_estimate=cost(
            4 * count * TOK * BLK * TERMS, 2 * TOK * TERMS + 2 * count * BLK * (2 * TERMS + 4 * TOK), weight
        ),
        name="term_part",
    )(ids, *after, h, wt, wt, dots, *crossed, *adds)


def term_sum_kernel(own, ra, rb, x, x_p, keep, send, dots, gain):
    sums = [jnp.zeros((8, BLK), f32) for _ in range(2)]
    for half in range(2):
        for m, values in ((0, x), (1, x_p)):
            for first in range(0, ROWS_T, 128):
                rows = slice(first, min(first + 128, ROWS_T))
                total = own[half, m, rows, :].astype(f32)
                for ref in (ra, rb):
                    total = total + ref[half, m, rows, :].astype(f32)
                if m:
                    send[half, rows, :] = total.astype(bf16)
                elif first < HALF:
                    keep[half * HALF + first : half * HALF + first + 128, :] = total.astype(bf16)
                else:
                    dots[half * 8 : half * 8 + 8, :] = total[:8]
                if first < HALF:
                    at = half * HALF + first
                    product = total * values[at : at + 128, :].astype(f32)
                    sums[m] = sums[m] + jnp.sum(product.reshape(16, 8, BLK), axis=0)
    gain[...] = jnp.sum(sums[0], axis=0, keepdims=True)
    other = jnp.sum(sums[1], axis=0, keepdims=True)
    high = other.astype(bf16).astype(f32)
    row = lax.broadcasted_iota(jnp.int32, (16, 1), 0)
    tail = send[0, HALF:, :].astype(f32)
    tail = jnp.where(row == 2, high, jnp.where(row == 3, other - high, tail))
    send[0, HALF:, :] = tail.astype(bf16)


def term_sum(after, own, ra, rb, x, x_p):
    count = len(after)
    return pl.pallas_call(
        lambda *refs: term_sum_kernel(*refs[count:]),
        out_shape=[
            jax.ShapeDtypeStruct((TOK, BLK), bf16),
            jax.ShapeDtypeStruct((2, ROWS_T, BLK), bf16),
            jax.ShapeDtypeStruct((16, BLK), f32),
            jax.ShapeDtypeStruct((1, BLK), f32),
        ],
        in_specs=[ANY] * count + [VMEM] * 5,
        out_specs=[VMEM] * 4,
        compiler_params=params(),
        cost_estimate=cost(1_000_000, 5_000_000),
        name="term_sum",
    )(*after, own, ra, rb, x, x_p)


def final_kernel(ids, n_ref, got, x_ref, gain, inv_ref, dots, out):
    g = gain[:, block_at(ids, ids[2] * 4 + ids[3], 0)]
    for half in range(2):
        lines = (dots[half * 8 : half * 8 + 8, :] + got[half, HALF:, :].astype(f32)[:8]) / D
        for k in range(4):
            local = slice(k * LEN, (k + 1) * LEN)
            rows = slice(half * HALF + k * LEN, half * HALF + (k + 1) * LEN)
            grad = n_ref[rows, :].astype(f32) + got[half, local, :].astype(f32)
            values = x_ref[rows, :].astype(f32)
            line = lines[k // 2 : k // 2 + 1, (k % 2) * LEN : (k % 2 + 1) * LEN]
            column = jnp.broadcast_to(line, (LEN, LEN)).T[:, 0:1]
            inverse = inv_ref[rows, :]
            out[rows, :] = (grad * g - values * (inverse * inverse * column)).astype(bf16)


def final(ids, after, n, got, x, gain, inv, dots):
    return pl.pallas_call(
        later(len(after), final_kernel),
        out_shape=jax.ShapeDtypeStruct((TOK, BLK), bf16),
        in_specs=[SMEM] + [ANY] * len(after) + [VMEM] * 6,
        out_specs=VMEM,
        compiler_params=params(),
        cost_estimate=cost(1_000_000, 2_000_000),
        name="hidden_grad",
    )(ids, *after, n, got, x, gain, inv, dots)


def gain_vocab(after, partial, got):
    count = len(after)

    def kernel(*refs):
        sums, tail, out = refs[count:]
        rows = tail[0].astype(f32)
        out[...] = sums[...] + rows[2:3] + rows[3:4]

    return pl.pallas_call(
        kernel,
        grid=(1,),
        out_shape=jax.ShapeDtypeStruct((1, BLK), f32),
        in_specs=[ANY] * count
        + [pl.BlockSpec((1, BLK), lambda k: (0, 0)), pl.BlockSpec((1, 16, BLK), lambda k: (0, HALF // 16, 0))],
        out_specs=pl.BlockSpec((1, BLK), lambda k: (0, 0)),
        compiler_params=params(),
        cost_estimate=cost(1000, 5000),
        name="gain_vocab",
    )(*after, partial, got)


def gain_sum_kernel(_, a, b, out):
    out[...] = a[...] + b[...]


def gain_sum(after, a, b):
    return pl.pallas_call(
        gain_sum_kernel,
        out_shape=jax.ShapeDtypeStruct((1, BLK), f32),
        in_specs=[ANY] + [VMEM] * 2,
        out_specs=VMEM,
        compiler_params=params(),
        cost_estimate=cost(1000, 5000),
        name="gain_sum",
    )(after, a, b)


def shards(hidden, norm_gain, head_weight, lengths, positives, negatives):
    xh, y, xl, z, c = (lax.axis_index(a).astype(jnp.int32) for a in ("xh", "y", "xl", "z", "c"))
    nil = jnp.int32(0)
    ids = jnp.concatenate([jnp.stack([xh, y, xl, z, c, nil, nil, nil]), positives, negatives.reshape(-1)])
    wt = head_weight.T
    gain = norm_gain.reshape(1, D)

    z_m, z_p, x_p = shift(hidden, "z", 1), shift(hidden, "z", -1), swap(hidden, "xl")
    own_c = swap(hidden, "c")
    z_m_c, z_p_c, x_p_c = (swap(a, "c") for a in (z_m, z_p, x_p))
    far, xz_p, xz_m = shift(z_m, "z", 1), shift(x_p, "z", -1), swap(z_m, "xl")
    state = forward(ids, [(0, 0), (0, -1), (1, 0)], [hidden, own_c, z_m, z_m_c, x_p, x_p_c], wt, gain)
    far, xz_p, xz_m = touch(state[1], far, xz_p, xz_m)
    last = swap(far, "xl")
    far_c, xz_p_c, xz_m_c = (swap(a, "c") for a in (far, xz_p, xz_m))
    state = forward(
        ids,
        [(0, 1), (0, 2), (1, 1), (1, -1)],
        [z_p, z_p_c, far, far_c, xz_p, xz_p_c, xz_m, xz_m_c],
        wt,
        gain,
        state,
    )
    (last,) = touch(state[1], last)
    last_c = swap(last, "c")
    acc, x, inv, weight, pooled = forward_last(ids, lengths, (1, 2), (last, last_c), wt, gain, state)

    pair = jnp.stack([pooled, swap(pooled, "xh")])
    every, part = gram(ids, [pair] + [swap(pair, "y", bits) for bits in (1, 2, 3)])
    part = (part + swap(part, "z", 1)) + (swap(part, "z", 2) + swap(part, "z", 3))
    both = lax.ppermute(part, ("xl", "c"), [(i, i ^ 3) for i in range(4)])
    parts = (part, swap(part, "c"), swap(part, "xl"), both)
    h, ht, dots, losses = grads(ids, every, parts, weight, acc)

    (crossing_2,) = term_part(ids, (2,), 1, h, wt, dots, ())
    (crossing,) = term_part(ids, (1, 3, 0), 1, h, wt, dots, (crossing_2,), weight=20)
    crossed_2, crossed = swap(crossing_2, "c"), swap(crossing, "c")
    term_0, term_1 = term_part(ids, (2,), 0, h, wt, dots, (crossing,), split=True, crossed=(crossed_2,))
    far_0, far_1, keep_2, send_2 = head_part(ids, (2,), ht, x, gain, (term_0,), split=True, weight=20)
    swap_2 = swap(send_2, "xh")
    adds = (shift(term_0, "z", 1), shift(term_1, "z", -1))
    t_1, t_3, t_0 = term_part(
        ids, (1, 3, 0), 0, h, wt, dots, (far_0,), apart=True, crossed=(crossed,), adds=adds, weight=20
    )
    adds = (shift(far_0, "y", 1), shift(far_1, "y", -1))
    a_1, a_3, keep_13, send_13 = head_part(ids, (1, 3), ht, x, gain, (t_0, swap_2), adds=adds, weight=20)
    swap_13 = swap(send_13, "xh")
    ra, rb = shift(a_1, "y", 1), shift(a_3, "y", -1)
    a_0, keep_0, send_0 = head_part(ids, (0,), ht, x, gain, (a_1,))
    keep, send, dots, partial = term_sum((keep_0,), t_0, shift(t_1, "z", 1), shift(t_3, "z", -1), hidden, x_p)
    swap_0 = swap(send_0, "xh")
    got = swap(a_0[1] + ra[1] + rb[1], "xh")
    low_1, low_3, low_2 = low_sum(keep, keep_13, swap_13, keep_2, swap_2)
    low = [shift(low_1, "y", 1), shift(low_2, "y", 2), shift(low_3, "y", 3)]
    got_term = swap(send, "xl")
    hidden_grad = final(ids, (swap_0,), keep, got_term, hidden, gain, inv, dots)
    gain_grad = gain_vocab((hidden_grad, *low), partial, got_term)
    gain_grad = (gain_grad + swap(gain_grad, "y", 1)) + (swap(gain_grad, "y", 2) + swap(gain_grad, "y", 3))
    head_t = join(ids, hidden_grad, a_0, ra, rb, got, keep_0, swap_0, *low)
    return losses[0, :3], hidden_grad, head_t.T, gain_sum(head_t, gain_grad, swap(gain_grad, "xh"))[0]


def solution(mesh):
    fine = Mesh(mesh.devices.reshape(2, 4, 2, 4, 2), ("xh", "y", "xl", "z", "c"))
    dp, vocab = ("xh", "y"), ("xl", "z", "c")
    in_specs = (P(dp, vocab), P(), P(None, vocab), P(dp), P(dp), P(dp, None))
    out_specs = (P(), P(dp, vocab), P(dp, vocab), P(vocab))
    return jax.shard_map(shards, mesh=fine, in_specs=in_specs, out_specs=out_specs, check_vma=False)
```

```python
import functools
import math

import jax
import jax.numpy as jnp
from jax import lax
from jax.experimental import pallas as pl
from jax.experimental.pallas import tpu as pltpu
from jax.sharding import Mesh, PartitionSpec as P

VOCAB = 16000
D = 4096
epsilon = 1e-05
sharpness = 80.0
flops_weight = 0.01

TOK = 1024
SEQ = 8
LEN = 128
TERMS = 1000
BLK = 256
ROWS_A = 688
ROWS_B = TERMS - ROWS_A
HALF = TOK // 2
PER = 2
SCORE_SCALE = 4.0 / math.sqrt(VOCAB)
COLS = ((0, 256), (256, 512), (512, 768), (768, 1000))
SIZES = {"xh": 2, "y": 4, "xl": 2, "z": 4, "c": 2}
VMEM_LIMIT = 67_000_000
HIGHEST = lax.Precision.HIGHEST

f32, bf16 = jnp.float32, jnp.bfloat16


def shift(x, axis, step):
    n = SIZES[axis]
    return lax.ppermute(x, axis, [(i, (i + step) % n) for i in range(n)])


def swap(x, axis, bits=1):
    return lax.ppermute(x, axis, [(i, i ^ bits) for i in range(SIZES[axis])])


def params(**more):
    return pltpu.CompilerParams(vmem_limit_bytes=VMEM_LIMIT, **more)


def cost(flops, moved, weight=0.02):
    return pl.CostEstimate(flops=int(flops * weight), bytes_accessed=int(moved * weight), transcendentals=0)


def tag(ids, pooled_ref):
    lane = lax.broadcasted_iota(jnp.int32, (1, 24), 1)
    for k in range(SEQ):
        tags = jnp.zeros((1, 24), f32)
        if k < 2:
            tags = jnp.where(lane == 0, ids[8 + k].astype(f32), tags)
            tags = jnp.where(lane == 1, ids[10 + 2 * k].astype(f32), tags)
            tags = jnp.where(lane == 2, ids[11 + 2 * k].astype(f32), tags)
        pooled_ref[k : k + 1, TERMS:] = tags


def pool(lengths, first, acc, ssq, inv_ref, weight_ref, pooled_ref):
    for s in range(acc.shape[0] // LEN):
        k = first + s
        rows = slice(s * LEN, (s + 1) * LEN)
        total = jnp.sum(ssq[rows, :], axis=1, keepdims=True)
        inverse = lax.rsqrt(total / D + epsilon)
        inv_ref[rows, :] = inverse
        count = lengths[k]
        for a, b in COLS:
            logits = acc[rows, a:b] * inverse
            valid = lax.broadcasted_iota(jnp.int32, (LEN, b - a), 0) < count
            held = jnp.where(valid, 1.0 + jnp.maximum(logits, 0.0), 1.0)
            top = jnp.max(held, axis=0, keepdims=True)
            down = 1.0 / top
            r1 = held * down
            r2 = r1 * r1
            r4 = r2 * r2
            r8 = r4 * r4
            r16 = r8 * r8
            r32 = r16 * r16
            r79 = (r32 * r32 * r8) * (r4 * (r2 * r1))
            summed = jnp.sum(jnp.where(valid, r79 * r1, 0.0), axis=0, keepdims=True)
            pooled_ref[pl.ds(k, 1), a:b] = jnp.log(top) + jnp.log(summed) / sharpness
            slope = r79 * (down / summed) * inverse
            weight_ref[rows, a:b] = jnp.where(valid & (logits > 0.0), slope, 0.0).astype(bf16)


def chip_of(ids, far_x, step):
    return (ids[2] ^ far_x) * 4 + ((ids[3] + step) & 3)


def block_at(ids, chip, side):
    return pl.ds(pl.multiple_of((chip * 2 + (ids[4] ^ side)) * BLK, BLK), BLK)


def scaled(weights, gain, ids, chip):
    row = jnp.concatenate([gain[:, block_at(ids, chip, side)] for side in range(2)], axis=1)
    return (weights.astype(f32) * row).astype(bf16)


def folded_squares(lefts):
    squares = 0.0
    for left in lefts:
        value = left.astype(f32)
        square = value * value
        squares = squares + square[:, :128] + square[:, 128:]
    return squares


def forward_kernel(places, first, ids, *refs):
    nb = len(places)
    arrays, (weights, gain), refs = refs[: 2 * nb], refs[2 * nb : 2 * nb + 2], refs[2 * nb + 2 :]
    if not first:
        (acc_in, ssq_in, _), refs = refs[:3], refs[3:]
    acc, ssq, kept, held, w_sem, x_sem = refs
    chips = [chip_of(ids, *place) for place in places]
    loads, saves = [], []
    for j in range(nb):
        for side in range(2):
            at = held.at[j, :, side * BLK : (side + 1) * BLK]
            loads.append(pltpu.make_async_copy(weights.at[:, block_at(ids, chips[j], side)], at, w_sem.at[j, side]))
            loads[-1].start()
    for j in range(nb):
        for side in range(2):
            saves.append(pltpu.make_async_copy(arrays[2 * j + side], kept.at[chips[j], side], x_sem.at[j, side]))
            saves[-1].start()
    for j in range(nb):
        loads[2 * j].wait()
        loads[2 * j + 1].wait()
        right = scaled(held[j], gain, ids, chips[j])
        for half in range(2):
            rows = slice(half * HALF, (half + 1) * HALF)
            lefts = [arrays[2 * j + side][rows, :] for side in range(2)]
            squares = folded_squares(lefts)
            product = lax.dot_general(
                jnp.concatenate(lefts, axis=1), right, (((1,), (1,)), ((), ())), preferred_element_type=f32
            )
            if j == 0 and first:
                acc[rows, :] = product
                ssq[rows, :] = squares
            elif j == 0:
                acc[rows, :] = acc_in[rows, :] + product
                ssq[rows, :] = ssq_in[rows, :] + squares
            else:
                acc[rows, :] += product
                ssq[rows, :] += squares
    for copy in saves:
        copy.wait()


SMEM = pl.BlockSpec(memory_space=pltpu.SMEM)
VMEM = pl.BlockSpec(memory_space=pltpu.VMEM)
ANY = pl.BlockSpec(memory_space=pl.ANY)


STATE = [
    jax.ShapeDtypeStruct((TOK, TERMS), f32),
    jax.ShapeDtypeStruct((TOK, 128), f32),
    jax.ShapeDtypeStruct((8, 2, TOK, BLK), bf16),
]


def forward(ids, places, arrays, weights, gain, state=()):
    nb = len(places)
    base = 3 + len(arrays)
    return pl.pallas_call(
        functools.partial(forward_kernel, places, not state),
        out_shape=STATE,
        in_specs=[SMEM] + [VMEM] * len(arrays) + [ANY, VMEM] + [VMEM, VMEM, ANY][: len(state)],
        out_specs=[VMEM, VMEM, ANY],
        scratch_shapes=[
            pltpu.VMEM((nb, TERMS, 2 * BLK), bf16),
            pltpu.SemaphoreType.DMA((nb, 2)),
            pltpu.SemaphoreType.DMA((nb, 2)),
        ],
        input_output_aliases={base + i: i for i in range(len(state))},
        compiler_params=params(),
        cost_estimate=cost(2 * nb * TOK * 512 * TERMS, nb * 3_000_000 + 8_000_000),
        name="forward_part",
    )(ids, *arrays, weights, gain, *state)


STEP = 256


def forward_last_kernel(place, ids, lengths, a0, a1, w0, w1, gain, acc_in, ssq_in, _, *refs):
    product, kept, inv_ref, weight_ref, pooled_ref, acc, right, ssq, sem = refs
    k = pl.program_id(0)
    chip = chip_of(ids, *place)

    @pl.when(k == 0)
    def _():
        right[...] = scaled(jnp.concatenate([w0[...], w1[...]], axis=1), gain, ids, chip)
        tag(ids, pooled_ref)

    rows = pl.ds(pl.multiple_of(k * STEP, STEP), STEP)
    saves = []
    for side, source in enumerate((a0, a1)):
        saves.append(pltpu.make_async_copy(source, kept.at[chip, side, rows, :], sem.at[side]))
        saves[-1].start()
    lefts = [a0[...], a1[...]]
    ssq[...] = ssq_in[...] + folded_squares(lefts)
    acc[...] = acc_in[...] + lax.dot_general(
        jnp.concatenate(lefts, axis=1), right[...], (((1,), (1,)), ((), ())), preferred_element_type=f32
    )
    product[...] = acc[...].astype(bf16)
    pool(lengths, k * (STEP // LEN), acc, ssq, inv_ref, weight_ref, pooled_ref)
    for copy in saves:
        copy.wait()


def forward_last(ids, lengths, place, arrays, weights, gain, state):
    whole = lambda k, *s: (0, 0)
    rows = lambda k, *s: (k, 0)
    sides = [
        pl.BlockSpec((TERMS, BLK), lambda k, s, n, side=side: (0, chip_of(s, *place) * 2 + (s[4] ^ side)))
        for side in range(2)
    ]
    return pl.pallas_call(
        functools.partial(forward_last_kernel, place),
        out_shape=[
            jax.ShapeDtypeStruct((TOK, TERMS), bf16),
            STATE[2],
            jax.ShapeDtypeStruct((TOK, 1), f32),
            jax.ShapeDtypeStruct((TOK, TERMS), bf16),
            jax.ShapeDtypeStruct((SEQ, 1024), f32),
        ],
        grid_spec=pltpu.PrefetchScalarGridSpec(
            num_scalar_prefetch=2,
            grid=(TOK // STEP,),
            in_specs=[pl.BlockSpec((STEP, BLK), rows)] * 2
            + [*sides, pl.BlockSpec((1, D), whole)]
            + [pl.BlockSpec((STEP, TERMS), rows), pl.BlockSpec((STEP, 128), rows), ANY],
            out_specs=[
                pl.BlockSpec((STEP, TERMS), rows),
                ANY,
                pl.BlockSpec((STEP, 1), rows),
                pl.BlockSpec((STEP, TERMS), rows),
                pl.BlockSpec((SEQ, 1024), whole),
            ],
            scratch_shapes=[
                pltpu.VMEM((STEP, TERMS), f32),
                pltpu.VMEM((TERMS, 2 * BLK), bf16),
                pltpu.VMEM((STEP, 128), f32),
                pltpu.SemaphoreType.DMA((2,)),
            ],
        ),
        input_output_aliases={9: 1},
        compiler_params=params(),
        cost_estimate=cost(2 * TOK * 512 * TERMS, 20_000_000),
        name="forward_last",
    )(ids, lengths, *arrays, weights, weights, gain, *state)


def touch_kernel(*refs):
    pass


def touch(after, *arrays):
    n = len(arrays)
    return pl.pallas_call(
        touch_kernel,
        out_shape=[jax.ShapeDtypeStruct(a.shape, a.dtype) for a in arrays],
        in_specs=[ANY] * (n + 1),
        out_specs=[ANY] * n,
        input_output_aliases={i + 1: i for i in range(n)},
        compiler_params=params(has_side_effects=True),
        cost_estimate=cost(1000, 1000),
        name="touch",
    )(after, *arrays)


def gram_kernel(ids, *refs):
    all_ref, part_ref = refs[4:]
    for bits, ref in enumerate(refs[:4]):
        for m in range(2):
            at = (ids[0] * 4 + ids[1]) ^ (4 * m + bits)
            all_ref[pl.ds(pl.multiple_of(at * SEQ, SEQ), SEQ), :] = ref[m]
    every = all_ref[:, :TERMS]
    part = lax.dot_general(every, every, (((1,), (1,)), ((), ())), precision=HIGHEST, preferred_element_type=f32)
    mean = jnp.sum(every, axis=0, keepdims=True) / 64.0
    flops = jnp.sum(mean * mean, axis=1, keepdims=True)
    part_ref[...] = jnp.zeros_like(part_ref)
    part_ref[0:64, 0:64] = part
    part_ref[64:72, :] = jnp.broadcast_to(flops, (8, 128))


def gram(ids, groups):
    return pl.pallas_call(
        gram_kernel,
        out_shape=[jax.ShapeDtypeStruct((64, 1024), f32), jax.ShapeDtypeStruct((72, 128), f32)],
        grid_spec=pltpu.PrefetchScalarGridSpec(
            num_scalar_prefetch=1,
            grid=(),
            in_specs=[VMEM] * 4,
            out_specs=[VMEM] * 2,
        ),
        compiler_params=params(),
        name="gram",
    )(ids, *groups)


def contrast(every, parts, scaled_ref, losses_ref):
    sums = (parts[0][...] + parts[1][...]) + (parts[2][...] + parts[3][...])
    scores = sums[0:64, :] * SCORE_SCALE
    row = lax.broadcasted_iota(jnp.int32, (64, 128), 0)
    col = lax.broadcasted_iota(jnp.int32, (64, 128), 1)
    is_query = (row & 7) < 2
    is_passage = ((col & 7) >= 2) & (col < 64)
    tags = every[:, TERMS:]

    def hot(at):
        index = tags[:, at : at + 1]
        group = jnp.floor((index + 0.5) * (1.0 / 6.0))
        place = group * 8.0 + 2.0 + (index - 6.0 * group)
        return (col.astype(f32) == place).astype(f32)

    positive, negatives = hot(0), (hot(1), hot(2))
    highest = jnp.max(jnp.where(is_passage, scores, -3e38), axis=1, keepdims=True)
    shifted = jnp.where(is_passage, jnp.exp(jnp.minimum(scores - highest, 0.0)), 0.0)
    denominator = jnp.sum(shifted, axis=1, keepdims=True)
    log_total = highest + jnp.log(denominator)
    positive_score = jnp.sum(scores * positive, axis=1, keepdims=True)
    query_row = is_query[:, 0:1]
    cross = jnp.sum(jnp.where(query_row, log_total - positive_score, 0.0), axis=0, keepdims=True) / 16.0
    grad = (shifted / denominator - positive) / 16.0
    margin = jnp.zeros((1, 1), f32)
    for negative in negatives:
        gap = jnp.sum(scores * negative, axis=1, keepdims=True) - positive_score
        small = jnp.exp(-jnp.abs(gap))
        soft = jnp.maximum(gap, 0.0) + jnp.log(1.0 + small)
        slope = jnp.where(gap >= 0.0, 1.0, small) / (1.0 + small) / 32.0
        margin = margin + jnp.sum(jnp.where(query_row, soft, 0.0), axis=0, keepdims=True) / 32.0
        grad = grad + slope * negative - slope * positive
    grad = jnp.where(is_query, grad, 0.0)
    square = jnp.concatenate([grad, jnp.zeros((64, 128), f32)], axis=0)
    scaled_ref[...] = (square + square.T) * SCORE_SCALE
    flops = sums[64:65, 0:1] * flops_weight
    lane = lax.broadcasted_iota(jnp.int32, (8, 128), 1)
    losses_ref[...] = jnp.where(lane == 0, cross, jnp.where(lane == 1, margin, flops))


def grad_kernel(
    ids, every, p0, p1, p2, p3, weight, acc, h_ref, ht_ref, dots, losses_ref, rep, scaled, padded
):
    k = pl.program_id(0)

    @pl.when(k == 0)
    def _():
        contrast(every, (p0, p1, p2, p3), scaled, losses_ref)
        dots[...] = jnp.zeros_like(dots)
        padded[0:64, :] = every[:, :TERMS]
        padded[64:128, :] = jnp.zeros((64, TERMS), f32)
        at = pl.multiple_of((ids[0] * 4 + ids[1]) * SEQ, SEQ)
        own = scaled[pl.ds(at, SEQ), :]
        mean = jnp.sum(padded[...], axis=0, keepdims=True) / 64.0
        rep[...] = jnp.dot(own, padded[...], precision=HIGHEST, preferred_element_type=f32) + (
            2.0 * flops_weight / 64.0
        ) * mean

    lines = []
    for s in range(PER):
        rows = slice(s * LEN, (s + 1) * LEN)
        folded = jnp.zeros((LEN, 128), f32)
        for a, b in COLS:
            grad = weight[rows, a:b].astype(f32) * rep[pl.ds(k * PER + s, 1), a:b]
            rounded = grad.astype(bf16)
            h_ref[rows, a:b] = rounded
            turned = grad.T.astype(bf16)
            ht_ref[a:b, rows] = turned
            product = rounded.astype(f32) * acc[rows, a:b].astype(f32)
            wide = b - a
            folded = folded + product[:, :128]
            if wide == 256:
                folded = folded + product[:, 128:]
            else:
                folded = folded + jnp.concatenate([product[:, 128:], jnp.zeros((LEN, 256 - wide), f32)], axis=1)
        lines.append(jnp.sum(folded.T, axis=0, keepdims=True))
    dots[pl.ds((k >> 1) * 8 + (k & 1), 1), :] = jnp.concatenate(lines, axis=1)


def grads(ids, every, parts, weight, acc):
    whole = lambda k, s: (0, 0)
    rows = lambda k, s: (k, 0)
    cols = lambda k, s: (0, k)
    return pl.pallas_call(
        grad_kernel,
        out_shape=[
            jax.ShapeDtypeStruct((TOK, TERMS), bf16),
            jax.ShapeDtypeStruct((TERMS, TOK), bf16),
            jax.ShapeDtypeStruct((16, BLK), f32),
            jax.ShapeDtypeStruct((8, 128), f32),
        ],
        grid_spec=pltpu.PrefetchScalarGridSpec(
            num_scalar_prefetch=1,
            grid=(SEQ // PER,),
            in_specs=[
                pl.BlockSpec((64, 1024), whole),
                *[pl.BlockSpec((72, 128), whole)] * 4,
                pl.BlockSpec((PER * LEN, TERMS), rows),
                pl.BlockSpec((PER * LEN, TERMS), rows),
            ],
            out_specs=[
                pl.BlockSpec((PER * LEN, TERMS), rows),
                pl.BlockSpec((TERMS, PER * LEN), cols),
                pl.BlockSpec((16, BLK), whole),
                pl.BlockSpec((8, 128), whole),
            ],
            scratch_shapes=[pltpu.VMEM((SEQ, TERMS), f32), pltpu.VMEM((128, 128), f32), pltpu.VMEM((128, TERMS), f32)],
        ),
        compiler_params=params(),
        cost_estimate=cost(20 * TOK * TERMS, 12_000_000),
        name="logit_grad",
    )(ids, every, *parts, weight, acc)


def later(count, kernel):
    return lambda ids, *refs: kernel(ids, *refs[count:])


def place_of(steps, n):
    step = steps[0]
    for i in range(1, len(steps)):
        step = jnp.where(n < 2 * i, step, steps[i])
    return step, n & 1


def head_chip(steps, ids, n):
    step, j = place_of(steps, n)
    return (ids[0] ^ j) * 4 + ((ids[1] + step) & 3)


def head_kernel(steps, split, n_add, ids, ht, x, gain, *refs):
    n = pl.program_id(0)
    adds, outs, (keep, send) = refs[:n_add], refs[n_add:-2], refs[-2:]
    block = jnp.concatenate([x[0, 0], x[0, 1]], axis=1)
    chip = head_chip(steps, ids, n)
    row = jnp.concatenate([gain[:, block_at(ids, chip, side)] for side in range(2)], axis=1)
    total = jnp.dot(ht[...], block, preferred_element_type=f32) * row
    sides = [total[:, :BLK], total[:, BLK:]]
    for i in range(len(steps)):

        @pl.when((n >> 1) == i)
        def _(i=i):
            for side in range(2):
                share = sides[side][:ROWS_A]
                if n_add and side == i:
                    share = share + adds[i][0].astype(f32)
                if split:
                    outs[side][0] = share.astype(bf16)
                else:
                    outs[i][0, side] = share.astype(bf16)

    for j, out in enumerate((keep, send)):

        @pl.when((n & 1) == j)
        def _(out=out):
            for side in range(2):
                out[0, side] = sides[side][ROWS_A:].astype(bf16)


def head_part(ids, steps, ht, x, gain, after, split=False, adds=(), weight=0.02):
    count = len(steps)
    at = lambda i: lambda n, s: (jnp.clip(n - 2 * i, 0, 1), 0, 0)
    at4 = lambda i: lambda n, s: (jnp.clip(n - 2 * i, 0, 1), 0, 0, 0)
    one = pl.BlockSpec((1, ROWS_A, BLK), at(0))
    low = pl.BlockSpec((1, 2, ROWS_B, BLK), lambda n, s: (n // 2, 0, 0, 0))
    if split:
        high, specs = [jax.ShapeDtypeStruct((2, ROWS_A, BLK), bf16)] * 2, [one, one]
    else:
        high = [jax.ShapeDtypeStruct((2, 2, ROWS_A, BLK), bf16)] * count
        specs = [pl.BlockSpec((1, 2, ROWS_A, BLK), at4(i)) for i in range(count)]
    return pl.pallas_call(
        later(len(after), functools.partial(head_kernel, steps, split, len(adds))),
        out_shape=high + [jax.ShapeDtypeStruct((count, 2, ROWS_B, BLK), bf16)] * 2,
        grid_spec=pltpu.PrefetchScalarGridSpec(
            num_scalar_prefetch=1,
            grid=(2 * count,),
            in_specs=[ANY] * len(after)
            + [
                pl.BlockSpec((TERMS, TOK), lambda n, s: (0, 0)),
                pl.BlockSpec((1, 2, TOK, BLK), lambda n, s: (head_chip(steps, s, n), 0, 0, 0)),
                pl.BlockSpec((1, D), lambda n, s: (0, 0)),
            ]
            + [pl.BlockSpec((1, ROWS_A, BLK), at(i)) for i in range(len(adds))],
            out_specs=specs + [low, low],
        ),
        compiler_params=params(),
        cost_estimate=cost(2 * TERMS * TOK * 1024 * count, 2 * TERMS * TOK + 2048 * count * (TOK + TERMS), weight),
        name="head_part",
    )(ids, *after, ht, x, gain, *adds)


def gain_rows(gain):
    rows = []
    for m in range(2):
        value = gain[m : m + 1, :]
        high = value.astype(bf16).astype(f32)
        rows += [high, value - high]
    return jnp.concatenate(rows + [jnp.zeros((12, BLK), f32)], axis=0).astype(bf16)


def low_sum_kernel(_, gain, a13, b13, a2, b2, out_1, out_3, out_2):
    for a, b, i, out in ((a13, b13, 0, out_1), (a13, b13, 1, out_3), (a2, b2, 0, out_2)):
        out[0, 0:16, :] = gain_rows(gain)
        out[1, 0:16, :] = jnp.zeros((16, BLK), bf16)
        out[:, 16:, :] = (a[i].astype(f32) + b[i].astype(f32)).astype(bf16)


def low_sum(after, *parts):
    return pl.pallas_call(
        low_sum_kernel,
        out_shape=[jax.ShapeDtypeStruct((2, 16 + ROWS_B, BLK), bf16)] * 3,
        in_specs=[ANY] + [VMEM] * 5,
        out_specs=[VMEM] * 3,
        compiler_params=params(),
        cost_estimate=cost(1000, 4_000_000),
        name="low_sum",
    )(after, *parts)


def gain_kernel(ids, gain, l1, l2, l3, out, held):
    for back, rows in enumerate((gain_rows(gain), l1[0], l2[0], l3[0])):
        values = rows.astype(f32)
        held[(ids[1] - back) & 3] = jnp.concatenate(
            [values[0:1] + values[1:2], values[2:3] + values[3:4], jnp.zeros((6, BLK), f32)], axis=0
        )
    out[...] = (held[0] + held[1]) + (held[2] + held[3])


def gain_along_y(ids, after, gain, *low):
    return pl.pallas_call(
        later(len(after), gain_kernel),
        grid=(1,),
        out_shape=jax.ShapeDtypeStruct((8, BLK), f32),
        in_specs=[SMEM]
        + [ANY] * len(after)
        + [pl.BlockSpec((2, BLK), lambda k: (0, 0))]
        + [pl.BlockSpec((1, 16, BLK), lambda k: (0, 0, 0))] * 3,
        out_specs=pl.BlockSpec((8, BLK), lambda k: (0, 0)),
        scratch_shapes=[pltpu.VMEM((4, 8, BLK), f32)],
        compiler_params=params(),
        cost_estimate=cost(1000, 50_000),
        name="gain_along_y",
    )(ids, *after, gain, *low)


def join_kernel(ids, _, a0, ra, rb, got, keep, swapped, b1, b2, b3, out):
    for side in range(2):
        cols = pl.ds(pl.multiple_of((ids[4] ^ side) * BLK, BLK), BLK)
        total = a0[0, side].astype(f32) + ra[0, side].astype(f32) + rb[0, side].astype(f32) + got[side].astype(f32)
        out[0:ROWS_A, cols] = total.astype(bf16)
        total = keep[0, side].astype(f32) + swapped[0, side].astype(f32)
        for b in (b1, b2, b3):
            total = total + b[side, 16:, :].astype(f32)
        out[ROWS_A:TERMS, cols] = total.astype(bf16)


def join(ids, after, *parts):
    return pl.pallas_call(
        join_kernel,
        out_shape=jax.ShapeDtypeStruct((TERMS, 2 * BLK), bf16),
        in_specs=[SMEM, ANY] + [VMEM] * len(parts),
        out_specs=VMEM,
        compiler_params=params(),
        cost_estimate=cost(1000, 8_000_000),
        name="join",
    )(ids, after, *parts)


ROWS_T = HALF + 16


def term_step(steps, n):
    step = steps[0]
    for i in range(1, len(steps)):
        step = jnp.where(n < i, step, steps[i])
    return step


def term_kernel(n_steps, split, n_adds, ids, h, w0, w1, dots, *refs):
    n = pl.program_id(0)
    crossed, adds, outs = refs[: n_adds[0]], refs[n_adds[0] : sum(n_adds)], refs[sum(n_adds) :]
    weights = jnp.concatenate([w0[...], w1[...]], axis=1)
    for half in range(2):
        total = jnp.dot(h[half * HALF : (half + 1) * HALF, :], weights, preferred_element_type=f32)
        tail = jnp.concatenate([dots[half * 8 : half * 8 + 8, :], jnp.zeros((8, BLK), f32)], axis=0)
        for m in range(2):
            share = jnp.concatenate([total[:, m * BLK : (m + 1) * BLK], tail], axis=0)
            for ref in crossed:
                share = share + ref[0, half, m].astype(f32)
            if adds:
                got = adds[half][m].astype(f32)
                share = share + jnp.where(n == half, got, 0.0)
            if split:
                outs[half][m] = share.astype(bf16)
            elif len(outs) == 1:
                outs[0][0, half, m] = share.astype(bf16)
            else:
                for i in range(n_steps):

                    @pl.when(n == i)
                    def _(i=i, half=half, m=m, share=share):
                        outs[i][half, m] = share.astype(bf16)


def term_part(ids, steps, side, h, wt, dots, after, split=False, apart=False, crossed=(), adds=(), weight=0.02):
    block = pl.BlockSpec((1, 2, 2, ROWS_T, BLK), lambda n, s: (n, 0, 0, 0, 0))
    part = pl.BlockSpec((2, ROWS_T, BLK), lambda n, s: (0, 0, 0))
    sides = [
        pl.BlockSpec(
            (TERMS, BLK), lambda n, s, m=m: (0, ((s[2] ^ m) * 4 + ((s[3] + term_step(steps, n)) & 3)) * 2 + (s[4] ^ side))
        )
        for m in range(2)
    ]
    count = len(steps)
    outs, specs = [jax.ShapeDtypeStruct((count, 2, 2, ROWS_T, BLK), bf16)], [block]
    if split:
        outs, specs = [jax.ShapeDtypeStruct((2, ROWS_T, BLK), bf16)] * 2, [part] * 2
    elif apart:
        outs = [jax.ShapeDtypeStruct((2, 2, ROWS_T, BLK), bf16)] * count
        specs = [pl.BlockSpec((2, 2, ROWS_T, BLK), lambda n, s: (0, 0, 0, 0))] * count
    return pl.pallas_call(
        later(len(after), functools.partial(term_kernel, count, split, (len(crossed), len(adds)))),
        out_shape=outs,
        grid_spec=pltpu.PrefetchScalarGridSpec(
            num_scalar_prefetch=1,
            grid=(count,),
            in_specs=[ANY] * len(after)
            + [pl.BlockSpec((TOK, TERMS), lambda n, s: (0, 0)), *sides]
            + [pl.BlockSpec((16, BLK), lambda n, s: (0, 0))]
            + [block] * len(crossed)
            + [part] * len(adds),
            out_specs=specs,
        ),
        compiler_params=params(),
        cost_estimate=cost(
            4 * count * TOK * BLK * TERMS, 2 * TOK * TERMS + 2 * count * BLK * (2 * TERMS + 4 * TOK), weight
        ),
        name="term_part",
    )(ids, *after, h, wt, wt, dots, *crossed, *adds)


def term_sum_kernel(own, ra, rb, x, x_p, keep, send, dots, gain):
    sums = [jnp.zeros((8, BLK), f32) for _ in range(2)]
    for half in range(2):
        for m, values in ((0, x), (1, x_p)):
            for first in range(0, ROWS_T, 128):
                rows = slice(first, min(first + 128, ROWS_T))
                total = own[half, m, rows, :].astype(f32)
                for ref in (ra, rb):
                    total = total + ref[half, m, rows, :].astype(f32)
                if m:
                    send[half, rows, :] = total.astype(bf16)
                elif first < HALF:
                    keep[half * HALF + first : half * HALF + first + 128, :] = total.astype(bf16)
                else:
                    dots[half * 8 : half * 8 + 8, :] = total[:8]
                if first < HALF:
                    at = half * HALF + first
                    product = total * values[at : at + 128, :].astype(f32)
                    sums[m] = sums[m] + jnp.sum(product.reshape(16, 8, BLK), axis=0)
    for m in range(2):
        gain[m : m + 1, :] = jnp.sum(sums[m], axis=0, keepdims=True)


def term_sum(after, own, ra, rb, x, x_p):
    count = len(after)
    return pl.pallas_call(
        lambda *refs: term_sum_kernel(*refs[count:]),
        out_shape=[
            jax.ShapeDtypeStruct((TOK, BLK), bf16),
            jax.ShapeDtypeStruct((2, ROWS_T, BLK), bf16),
            jax.ShapeDtypeStruct((16, BLK), f32),
            jax.ShapeDtypeStruct((2, BLK), f32),
        ],
        in_specs=[ANY] * count + [VMEM] * 5,
        out_specs=[VMEM] * 4,
        compiler_params=params(),
        cost_estimate=cost(1_000_000, 5_000_000),
        name="term_sum",
    )(*after, own, ra, rb, x, x_p)


def final_kernel(ids, n_ref, got, x_ref, gain, inv_ref, dots, out):
    g = gain[:, block_at(ids, ids[2] * 4 + ids[3], 0)]
    for half in range(2):
        lines = (dots[half * 8 : half * 8 + 8, :] + got[half, HALF:, :].astype(f32)[:8]) / D
        for k in range(4):
            local = slice(k * LEN, (k + 1) * LEN)
            rows = slice(half * HALF + k * LEN, half * HALF + (k + 1) * LEN)
            grad = n_ref[rows, :].astype(f32) + got[half, local, :].astype(f32)
            values = x_ref[rows, :].astype(f32)
            line = lines[k // 2 : k // 2 + 1, (k % 2) * LEN : (k % 2 + 1) * LEN]
            column = jnp.broadcast_to(line, (LEN, LEN)).T[:, 0:1]
            inverse = inv_ref[rows, :]
            out[rows, :] = (grad * g - values * (inverse * inverse * column)).astype(bf16)


def final(ids, after, n, got, x, gain, inv, dots):
    return pl.pallas_call(
        later(len(after), final_kernel),
        out_shape=jax.ShapeDtypeStruct((TOK, BLK), bf16),
        in_specs=[SMEM] + [ANY] * len(after) + [VMEM] * 6,
        out_specs=VMEM,
        compiler_params=params(),
        cost_estimate=cost(1_000_000, 2_000_000),
        name="hidden_grad",
    )(ids, *after, n, got, x, gain, inv, dots)


def shards(hidden, norm_gain, head_weight, lengths, positives, negatives):
    xh, y, xl, z, c = (lax.axis_index(a).astype(jnp.int32) for a in ("xh", "y", "xl", "z", "c"))
    nil = jnp.int32(0)
    ids = jnp.concatenate([jnp.stack([xh, y, xl, z, c, nil, nil, nil]), positives, negatives.reshape(-1)])
    wt = head_weight.T
    gain = norm_gain.reshape(1, D)

    z_m, z_p, x_p = shift(hidden, "z", 1), shift(hidden, "z", -1), swap(hidden, "xl")
    own_c = swap(hidden, "c")
    z_m_c, z_p_c, x_p_c = (swap(a, "c") for a in (z_m, z_p, x_p))
    far, xz_p, xz_m = shift(z_m, "z", 1), shift(x_p, "z", -1), swap(z_m, "xl")
    state = forward(ids, [(0, 0), (0, -1), (1, 0)], [hidden, own_c, z_m, z_m_c, x_p, x_p_c], wt, gain)
    far, xz_p, xz_m = touch(state[1], far, xz_p, xz_m)
    last = swap(far, "xl")
    far_c, xz_p_c, xz_m_c = (swap(a, "c") for a in (far, xz_p, xz_m))
    state = forward(
        ids,
        [(0, 1), (0, 2), (1, 1), (1, -1)],
        [z_p, z_p_c, far, far_c, xz_p, xz_p_c, xz_m, xz_m_c],
        wt,
        gain,
        state,
    )
    (last,) = touch(state[1], last)
    last_c = swap(last, "c")
    acc, x, inv, weight, pooled = forward_last(ids, lengths, (1, 2), (last, last_c), wt, gain, state)

    pair = jnp.stack([pooled, swap(pooled, "xh")])
    every, part = gram(ids, [pair] + [swap(pair, "y", bits) for bits in (1, 2, 3)])
    part = (part + swap(part, "z", 1)) + (swap(part, "z", 2) + swap(part, "z", 3))
    both = lax.ppermute(part, ("xl", "c"), [(i, i ^ 3) for i in range(4)])
    parts = (part, swap(part, "c"), swap(part, "xl"), both)
    h, ht, dots, losses = grads(ids, every, parts, weight, acc)

    (crossing_2,) = term_part(ids, (2,), 1, h, wt, dots, ())
    (crossing,) = term_part(ids, (1, 3, 0), 1, h, wt, dots, (crossing_2,), weight=20)
    crossed_2, crossed = swap(crossing_2, "c"), swap(crossing, "c")
    term_0, term_1 = term_part(ids, (2,), 0, h, wt, dots, (crossing,), split=True, crossed=(crossed_2,))
    far_0, far_1, keep_2, send_2 = head_part(ids, (2,), ht, x, gain, (term_0,), split=True, weight=20)
    swap_2 = swap(send_2, "xh")
    adds = (shift(term_0, "z", 1), shift(term_1, "z", -1))
    t_1, t_3, t_0 = term_part(
        ids, (1, 3, 0), 0, h, wt, dots, (far_0,), apart=True, crossed=(crossed,), adds=adds, weight=20
    )
    adds = (shift(far_0, "y", 1), shift(far_1, "y", -1))
    a_1, a_3, keep_13, send_13 = head_part(ids, (1, 3), ht, x, gain, (t_0, swap_2), adds=adds, weight=20)
    swap_13 = swap(send_13, "xh")
    ra, rb = shift(a_1, "y", 1), shift(a_3, "y", -1)
    keep, send, dots, partial = term_sum((), t_0, shift(t_1, "z", 1), shift(t_3, "z", -1), hidden, x_p)
    a_0, keep_0, send_0 = head_part(ids, (0,), ht, x, gain, (a_1, keep), weight=20)
    swap_0 = swap(send_0, "xh")
    got = swap(a_0[1] + ra[1] + rb[1], "xh")
    low_1, low_3, low_2 = low_sum(swap_0, partial, keep_13, swap_13, keep_2, swap_2)
    low = [shift(low_1, "y", 1), shift(low_2, "y", 2), shift(low_3, "y", 3)]
    hidden_grad = final(ids, (), keep, swap(send, "xl"), hidden, gain, inv, dots)
    gain_grad = gain_along_y(ids, (hidden_grad, swap_0), partial, *low)
    gain_grad = gain_grad + swap(gain_grad, "xh")
    gain_grad = gain_grad[0] + swap(gain_grad[1], "xl")
    head_t = join(ids, hidden_grad, a_0, ra, rb, got, keep_0, swap_0, *low)
    return losses[0, :3], hidden_grad, head_t.T, gain_grad


def solution(mesh):
    fine = Mesh(mesh.devices.reshape(2, 4, 2, 4, 2), ("xh", "y", "xl", "z", "c"))
    dp, vocab = ("xh", "y"), ("xl", "z", "c")
    in_specs = (P(dp, vocab), P(), P(None, vocab), P(dp), P(dp), P(dp, None))
    out_specs = (P(), P(dp, vocab), P(dp, vocab), P(vocab))
    return jax.shard_map(shards, mesh=fine, in_specs=in_specs, out_specs=out_specs, check_vma=False)
```

```python
import functools
import math

import jax
import jax.numpy as jnp
from jax import lax
from jax.experimental import pallas as pl
from jax.experimental.pallas import tpu as pltpu
from jax.sharding import Mesh, PartitionSpec as P

VOCAB = 16000
D = 4096
epsilon = 1e-05
sharpness = 80.0
flops_weight = 0.01

TOK = 1024
SEQ = 8
LEN = 128
TERMS = 1000
BLK = 256
ROWS_A = 688
ROWS_B = TERMS - ROWS_A
HALF = TOK // 2
PER = 2
SCORE_SCALE = 4.0 / math.sqrt(VOCAB)
COLS = ((0, 256), (256, 512), (512, 768), (768, 1000))
SIZES = {"xh": 2, "y": 4, "xl": 2, "z": 4, "c": 2}
VMEM_LIMIT = 67_000_000
HIGHEST = lax.Precision.HIGHEST

f32, bf16 = jnp.float32, jnp.bfloat16


def shift(x, axis, step):
    n = SIZES[axis]
    return lax.ppermute(x, axis, [(i, (i + step) % n) for i in range(n)])


def swap(x, axis, bits=1):
    return lax.ppermute(x, axis, [(i, i ^ bits) for i in range(SIZES[axis])])


def params(**more):
    return pltpu.CompilerParams(vmem_limit_bytes=VMEM_LIMIT, **more)


def cost(flops, moved, weight=0.02):
    return pl.CostEstimate(flops=int(flops * weight), bytes_accessed=int(moved * weight), transcendentals=0)


def tag(ids, pooled_ref):
    lane = lax.broadcasted_iota(jnp.int32, (1, 24), 1)
    for k in range(SEQ):
        tags = jnp.zeros((1, 24), f32)
        if k < 2:
            tags = jnp.where(lane == 0, ids[8 + k].astype(f32), tags)
            tags = jnp.where(lane == 1, ids[10 + 2 * k].astype(f32), tags)
            tags = jnp.where(lane == 2, ids[11 + 2 * k].astype(f32), tags)
        pooled_ref[k : k + 1, TERMS:] = tags


def pool(lengths, first, acc, ssq, inv_ref, weight_ref, pooled_ref):
    for s in range(acc.shape[0] // LEN):
        k = first + s
        rows = slice(s * LEN, (s + 1) * LEN)
        total = jnp.sum(ssq[rows, :], axis=1, keepdims=True)
        inverse = lax.rsqrt(total / D + epsilon)
        inv_ref[rows, :] = inverse
        count = lengths[k]
        for a, b in COLS:
            logits = acc[rows, a:b] * inverse
            valid = lax.broadcasted_iota(jnp.int32, (LEN, b - a), 0) < count
            held = jnp.where(valid, 1.0 + jnp.maximum(logits, 0.0), 1.0)
            top = jnp.max(held, axis=0, keepdims=True)
            down = 1.0 / top
            r1 = held * down
            r2 = r1 * r1
            r4 = r2 * r2
            r8 = r4 * r4
            r16 = r8 * r8
            r32 = r16 * r16
            r79 = (r32 * r32 * r8) * (r4 * (r2 * r1))
            summed = jnp.sum(jnp.where(valid, r79 * r1, 0.0), axis=0, keepdims=True)
            pooled_ref[pl.ds(k, 1), a:b] = jnp.log(top) + jnp.log(summed) / sharpness
            slope = r79 * (down / summed) * inverse
            weight_ref[rows, a:b] = jnp.where(valid & (logits > 0.0), slope, 0.0).astype(bf16)


def chip_of(ids, far_x, step):
    return (ids[2] ^ far_x) * 4 + ((ids[3] + step) & 3)


def block_at(ids, chip, side):
    return pl.ds(pl.multiple_of((chip * 2 + (ids[4] ^ side)) * BLK, BLK), BLK)


def scaled(weights, gain, ids, chip):
    row = jnp.concatenate([gain[:, block_at(ids, chip, side)] for side in range(2)], axis=1)
    return (weights.astype(f32) * row).astype(bf16)


def folded_squares(lefts):
    squares = 0.0
    for left in lefts:
        value = left.astype(f32)
        square = value * value
        squares = squares + square[:, :128] + square[:, 128:]
    return squares


def forward_kernel(places, first, ids, *refs):
    nb = len(places)
    arrays, (weights, gain), refs = refs[: 2 * nb], refs[2 * nb : 2 * nb + 2], refs[2 * nb + 2 :]
    if not first:
        (acc_in, ssq_in, _), refs = refs[:3], refs[3:]
    acc, ssq, kept, held, w_sem, x_sem = refs
    chips = [chip_of(ids, *place) for place in places]
    loads, saves = [], []
    for j in range(nb):
        for side in range(2):
            at = held.at[j, :, side * BLK : (side + 1) * BLK]
            loads.append(pltpu.make_async_copy(weights.at[:, block_at(ids, chips[j], side)], at, w_sem.at[j, side]))
            loads[-1].start()
    for j in range(nb):
        for side in range(2):
            saves.append(pltpu.make_async_copy(arrays[2 * j + side], kept.at[chips[j], side], x_sem.at[j, side]))
            saves[-1].start()
    for j in range(nb):
        loads[2 * j].wait()
        loads[2 * j + 1].wait()
        right = scaled(held[j], gain, ids, chips[j])
        for half in range(2):
            rows = slice(half * HALF, (half + 1) * HALF)
            lefts = [arrays[2 * j + side][rows, :] for side in range(2)]
            squares = folded_squares(lefts)
            product = lax.dot_general(
                jnp.concatenate(lefts, axis=1), right, (((1,), (1,)), ((), ())), preferred_element_type=f32
            )
            if j == 0 and first:
                acc[rows, :] = product
                ssq[rows, :] = squares
            elif j == 0:
                acc[rows, :] = acc_in[rows, :] + product
                ssq[rows, :] = ssq_in[rows, :] + squares
            else:
                acc[rows, :] += product
                ssq[rows, :] += squares
    for copy in saves:
        copy.wait()


SMEM = pl.BlockSpec(memory_space=pltpu.SMEM)
VMEM = pl.BlockSpec(memory_space=pltpu.VMEM)
ANY = pl.BlockSpec(memory_space=pl.ANY)


STATE = [
    jax.ShapeDtypeStruct((TOK, TERMS), f32),
    jax.ShapeDtypeStruct((TOK, 128), f32),
    jax.ShapeDtypeStruct((8, 2, TOK, BLK), bf16),
]


def forward(ids, places, arrays, weights, gain, state=()):
    nb = len(places)
    base = 3 + len(arrays)
    return pl.pallas_call(
        functools.partial(forward_kernel, places, not state),
        out_shape=STATE,
        in_specs=[SMEM] + [VMEM] * len(arrays) + [ANY, VMEM] + [VMEM, VMEM, ANY][: len(state)],
        out_specs=[VMEM, VMEM, ANY],
        scratch_shapes=[
            pltpu.VMEM((nb, TERMS, 2 * BLK), bf16),
            pltpu.SemaphoreType.DMA((nb, 2)),
            pltpu.SemaphoreType.DMA((nb, 2)),
        ],
        input_output_aliases={base + i: i for i in range(len(state))},
        compiler_params=params(),
        cost_estimate=cost(2 * nb * TOK * 512 * TERMS, nb * 3_000_000 + 8_000_000),
        name="forward_part",
    )(ids, *arrays, weights, gain, *state)


STEP = 256


def forward_last_kernel(place, ids, lengths, a0, a1, w0, w1, gain, acc_in, ssq_in, _, *refs):
    product, kept, inv_ref, weight_ref, pooled_ref, acc, right, ssq, sem = refs
    k = pl.program_id(0)
    chip = chip_of(ids, *place)

    @pl.when(k == 0)
    def _():
        right[...] = scaled(jnp.concatenate([w0[...], w1[...]], axis=1), gain, ids, chip)
        tag(ids, pooled_ref)

    rows = pl.ds(pl.multiple_of(k * STEP, STEP), STEP)
    saves = []
    for side, source in enumerate((a0, a1)):
        saves.append(pltpu.make_async_copy(source, kept.at[chip, side, rows, :], sem.at[side]))
        saves[-1].start()
    lefts = [a0[...], a1[...]]
    ssq[...] = ssq_in[...] + folded_squares(lefts)
    acc[...] = acc_in[...] + lax.dot_general(
        jnp.concatenate(lefts, axis=1), right[...], (((1,), (1,)), ((), ())), preferred_element_type=f32
    )
    product[...] = acc[...].astype(bf16)
    pool(lengths, k * (STEP // LEN), acc, ssq, inv_ref, weight_ref, pooled_ref)
    for copy in saves:
        copy.wait()


def forward_last(ids, lengths, place, arrays, weights, gain, state):
    whole = lambda k, *s: (0, 0)
    rows = lambda k, *s: (k, 0)
    sides = [
        pl.BlockSpec((TERMS, BLK), lambda k, s, n, side=side: (0, chip_of(s, *place) * 2 + (s[4] ^ side)))
        for side in range(2)
    ]
    return pl.pallas_call(
        functools.partial(forward_last_kernel, place),
        out_shape=[
            jax.ShapeDtypeStruct((TOK, TERMS), bf16),
            STATE[2],
            jax.ShapeDtypeStruct((TOK, 1), f32),
            jax.ShapeDtypeStruct((TOK, TERMS), bf16),
            jax.ShapeDtypeStruct((SEQ, 1024), f32),
        ],
        grid_spec=pltpu.PrefetchScalarGridSpec(
            num_scalar_prefetch=2,
            grid=(TOK // STEP,),
            in_specs=[pl.BlockSpec((STEP, BLK), rows)] * 2
            + [*sides, pl.BlockSpec((1, D), whole)]
            + [pl.BlockSpec((STEP, TERMS), rows), pl.BlockSpec((STEP, 128), rows), ANY],
            out_specs=[
                pl.BlockSpec((STEP, TERMS), rows),
                ANY,
                pl.BlockSpec((STEP, 1), rows),
                pl.BlockSpec((STEP, TERMS), rows),
                pl.BlockSpec((SEQ, 1024), whole),
            ],
            scratch_shapes=[
                pltpu.VMEM((STEP, TERMS), f32),
                pltpu.VMEM((TERMS, 2 * BLK), bf16),
                pltpu.VMEM((STEP, 128), f32),
                pltpu.SemaphoreType.DMA((2,)),
            ],
        ),
        input_output_aliases={9: 1},
        compiler_params=params(),
        cost_estimate=cost(2 * TOK * 512 * TERMS, 20_000_000),
        name="forward_last",
    )(ids, lengths, *arrays, weights, weights, gain, *state)


def touch_kernel(*refs):
    pass


def touch(after, *arrays):
    n = len(arrays)
    return pl.pallas_call(
        touch_kernel,
        out_shape=[jax.ShapeDtypeStruct(a.shape, a.dtype) for a in arrays],
        in_specs=[ANY] * (n + 1),
        out_specs=[ANY] * n,
        input_output_aliases={i + 1: i for i in range(n)},
        compiler_params=params(has_side_effects=True),
        cost_estimate=cost(1000, 1000),
        name="touch",
    )(after, *arrays)


def gram_kernel(ids, *refs):
    all_ref, part_ref = refs[4:]
    for bits, ref in enumerate(refs[:4]):
        for m in range(2):
            at = (ids[0] * 4 + ids[1]) ^ (4 * m + bits)
            all_ref[pl.ds(pl.multiple_of(at * SEQ, SEQ), SEQ), :] = ref[m]
    every = all_ref[:, :TERMS]
    part = lax.dot_general(every, every, (((1,), (1,)), ((), ())), precision=HIGHEST, preferred_element_type=f32)
    mean = jnp.sum(every, axis=0, keepdims=True) / 64.0
    flops = jnp.sum(mean * mean, axis=1, keepdims=True)
    part_ref[...] = jnp.zeros_like(part_ref)
    part_ref[0:64, 0:64] = part
    part_ref[64:72, :] = jnp.broadcast_to(flops, (8, 128))


def gram(ids, groups):
    return pl.pallas_call(
        gram_kernel,
        out_shape=[jax.ShapeDtypeStruct((64, 1024), f32), jax.ShapeDtypeStruct((72, 128), f32)],
        grid_spec=pltpu.PrefetchScalarGridSpec(
            num_scalar_prefetch=1,
            grid=(),
            in_specs=[VMEM] * 4,
            out_specs=[VMEM] * 2,
        ),
        compiler_params=params(),
        name="gram",
    )(ids, *groups)


def contrast(every, parts, scaled_ref, losses_ref):
    sums = (parts[0][...] + parts[1][...]) + (parts[2][...] + parts[3][...])
    scores = sums[0:64, :] * SCORE_SCALE
    row = lax.broadcasted_iota(jnp.int32, (64, 128), 0)
    col = lax.broadcasted_iota(jnp.int32, (64, 128), 1)
    is_query = (row & 7) < 2
    is_passage = ((col & 7) >= 2) & (col < 64)
    tags = every[:, TERMS:]

    def hot(at):
        index = tags[:, at : at + 1]
        group = jnp.floor((index + 0.5) * (1.0 / 6.0))
        place = group * 8.0 + 2.0 + (index - 6.0 * group)
        return (col.astype(f32) == place).astype(f32)

    positive, negatives = hot(0), (hot(1), hot(2))
    highest = jnp.max(jnp.where(is_passage, scores, -3e38), axis=1, keepdims=True)
    shifted = jnp.where(is_passage, jnp.exp(jnp.minimum(scores - highest, 0.0)), 0.0)
    denominator = jnp.sum(shifted, axis=1, keepdims=True)
    log_total = highest + jnp.log(denominator)
    positive_score = jnp.sum(scores * positive, axis=1, keepdims=True)
    query_row = is_query[:, 0:1]
    cross = jnp.sum(jnp.where(query_row, log_total - positive_score, 0.0), axis=0, keepdims=True) / 16.0
    grad = (shifted / denominator - positive) / 16.0
    margin = jnp.zeros((1, 1), f32)
    for negative in negatives:
        gap = jnp.sum(scores * negative, axis=1, keepdims=True) - positive_score
        small = jnp.exp(-jnp.abs(gap))
        soft = jnp.maximum(gap, 0.0) + jnp.log(1.0 + small)
        slope = jnp.where(gap >= 0.0, 1.0, small) / (1.0 + small) / 32.0
        margin = margin + jnp.sum(jnp.where(query_row, soft, 0.0), axis=0, keepdims=True) / 32.0
        grad = grad + slope * negative - slope * positive
    grad = jnp.where(is_query, grad, 0.0)
    square = jnp.concatenate([grad, jnp.zeros((64, 128), f32)], axis=0)
    scaled_ref[...] = (square + square.T) * SCORE_SCALE
    flops = sums[64:65, 0:1] * flops_weight
    lane = lax.broadcasted_iota(jnp.int32, (8, 128), 1)
    losses_ref[...] = jnp.where(lane == 0, cross, jnp.where(lane == 1, margin, flops))


def grad_kernel(
    ids, every, p0, p1, p2, p3, weight, acc, h_ref, ht_ref, dots, losses_ref, rep, scaled, padded
):
    k = pl.program_id(0)

    @pl.when(k == 0)
    def _():
        contrast(every, (p0, p1, p2, p3), scaled, losses_ref)
        dots[...] = jnp.zeros_like(dots)
        padded[0:64, :] = every[:, :TERMS]
        padded[64:128, :] = jnp.zeros((64, TERMS), f32)
        at = pl.multiple_of((ids[0] * 4 + ids[1]) * SEQ, SEQ)
        own = scaled[pl.ds(at, SEQ), :]
        mean = jnp.sum(padded[...], axis=0, keepdims=True) / 64.0
        rep[...] = jnp.dot(own, padded[...], precision=HIGHEST, preferred_element_type=f32) + (
            2.0 * flops_weight / 64.0
        ) * mean

    lines = []
    for s in range(PER):
        rows = slice(s * LEN, (s + 1) * LEN)
        folded = jnp.zeros((LEN, 128), f32)
        for a, b in COLS:
            grad = weight[rows, a:b].astype(f32) * rep[pl.ds(k * PER + s, 1), a:b]
            rounded = grad.astype(bf16)
            h_ref[rows, a:b] = rounded
            turned = grad.T.astype(bf16)
            ht_ref[a:b, rows] = turned
            product = rounded.astype(f32) * acc[rows, a:b].astype(f32)
            wide = b - a
            folded = folded + product[:, :128]
            if wide == 256:
                folded = folded + product[:, 128:]
            else:
                folded = folded + jnp.concatenate([product[:, 128:], jnp.zeros((LEN, 256 - wide), f32)], axis=1)
        lines.append(jnp.sum(folded.T, axis=0, keepdims=True))
    dots[pl.ds((k >> 1) * 8 + (k & 1), 1), :] = jnp.concatenate(lines, axis=1)


def grads(ids, every, parts, weight, acc):
    whole = lambda k, s: (0, 0)
    rows = lambda k, s: (k, 0)
    cols = lambda k, s: (0, k)
    return pl.pallas_call(
        grad_kernel,
        out_shape=[
            jax.ShapeDtypeStruct((TOK, TERMS), bf16),
            jax.ShapeDtypeStruct((TERMS, TOK), bf16),
            jax.ShapeDtypeStruct((16, BLK), f32),
            jax.ShapeDtypeStruct((8, 128), f32),
        ],
        grid_spec=pltpu.PrefetchScalarGridSpec(
            num_scalar_prefetch=1,
            grid=(SEQ // PER,),
            in_specs=[
                pl.BlockSpec((64, 1024), whole),
                *[pl.BlockSpec((72, 128), whole)] * 4,
                pl.BlockSpec((PER * LEN, TERMS), rows),
                pl.BlockSpec((PER * LEN, TERMS), rows),
            ],
            out_specs=[
                pl.BlockSpec((PER * LEN, TERMS), rows),
                pl.BlockSpec((TERMS, PER * LEN), cols),
                pl.BlockSpec((16, BLK), whole),
                pl.BlockSpec((8, 128), whole),
            ],
            scratch_shapes=[pltpu.VMEM((SEQ, TERMS), f32), pltpu.VMEM((128, 128), f32), pltpu.VMEM((128, TERMS), f32)],
        ),
        compiler_params=params(),
        cost_estimate=cost(20 * TOK * TERMS, 12_000_000),
        name="logit_grad",
    )(ids, every, *parts, weight, acc)


def later(count, kernel):
    return lambda ids, *refs: kernel(ids, *refs[count:])


def place_of(steps, n):
    step = steps[0]
    for i in range(1, len(steps)):
        step = jnp.where(n < 2 * i, step, steps[i])
    return step, n & 1


def head_chip(steps, ids, n):
    step, j = place_of(steps, n)
    return (ids[0] ^ j) * 4 + ((ids[1] + step) & 3)


def head_kernel(steps, split, n_add, ids, ht, x, gain, *refs):
    n = pl.program_id(0)
    adds, outs, (keep, send) = refs[:n_add], refs[n_add:-2], refs[-2:]
    block = jnp.concatenate([x[0, 0], x[0, 1]], axis=1)
    chip = head_chip(steps, ids, n)
    row = jnp.concatenate([gain[:, block_at(ids, chip, side)] for side in range(2)], axis=1)
    total = jnp.dot(ht[...], block, preferred_element_type=f32) * row
    sides = [total[:, :BLK], total[:, BLK:]]
    for i in range(len(steps)):

        @pl.when((n >> 1) == i)
        def _(i=i):
            for side in range(2):
                share = sides[side][:ROWS_A]
                if n_add and side == i:
                    share = share + adds[i][0].astype(f32)
                if split:
                    outs[side][0] = share.astype(bf16)
                else:
                    outs[i][0, side] = share.astype(bf16)

    for j, out in enumerate((keep, send)):

        @pl.when((n & 1) == j)
        def _(out=out):
            for side in range(2):
                out[0, side] = sides[side][ROWS_A:].astype(bf16)


def head_part(ids, steps, ht, x, gain, after, split=False, adds=(), weight=0.02):
    count = len(steps)
    at = lambda i: lambda n, s: (jnp.clip(n - 2 * i, 0, 1), 0, 0)
    at4 = lambda i: lambda n, s: (jnp.clip(n - 2 * i, 0, 1), 0, 0, 0)
    one = pl.BlockSpec((1, ROWS_A, BLK), at(0))
    low = pl.BlockSpec((1, 2, ROWS_B, BLK), lambda n, s: (n // 2, 0, 0, 0))
    if split:
        high, specs = [jax.ShapeDtypeStruct((2, ROWS_A, BLK), bf16)] * 2, [one, one]
    else:
        high = [jax.ShapeDtypeStruct((2, 2, ROWS_A, BLK), bf16)] * count
        specs = [pl.BlockSpec((1, 2, ROWS_A, BLK), at4(i)) for i in range(count)]
    return pl.pallas_call(
        later(len(after), functools.partial(head_kernel, steps, split, len(adds))),
        out_shape=high + [jax.ShapeDtypeStruct((count, 2, ROWS_B, BLK), bf16)] * 2,
        grid_spec=pltpu.PrefetchScalarGridSpec(
            num_scalar_prefetch=1,
            grid=(2 * count,),
            in_specs=[ANY] * len(after)
            + [
                pl.BlockSpec((TERMS, TOK), lambda n, s: (0, 0)),
                pl.BlockSpec((1, 2, TOK, BLK), lambda n, s: (head_chip(steps, s, n), 0, 0, 0)),
                pl.BlockSpec((1, D), lambda n, s: (0, 0)),
            ]
            + [pl.BlockSpec((1, ROWS_A, BLK), at(i)) for i in range(len(adds))],
            out_specs=specs + [low, low],
        ),
        compiler_params=params(),
        cost_estimate=cost(2 * TERMS * TOK * 1024 * count, 2 * TERMS * TOK + 2048 * count * (TOK + TERMS), weight),
        name="head_part",
    )(ids, *after, ht, x, gain, *adds)


def gain_rows(gain):
    rows = []
    for m in range(2):
        value = gain[m : m + 1, :]
        high = value.astype(bf16).astype(f32)
        rows += [high, value - high]
    return jnp.concatenate(rows + [jnp.zeros((12, BLK), f32)], axis=0).astype(bf16)


def low_sum_kernel(_, __, gain, a13, b13, a2, b2, out_1, out_3, out_2):
    for a, b, i, out in ((a13, b13, 0, out_1), (a13, b13, 1, out_3), (a2, b2, 0, out_2)):
        out[0, 0:16, :] = gain_rows(gain)
        out[1, 0:16, :] = jnp.zeros((16, BLK), bf16)
        out[:, 16:, :] = (a[i].astype(f32) + b[i].astype(f32)).astype(bf16)


def low_sum(after, also, *parts):
    return pl.pallas_call(
        low_sum_kernel,
        out_shape=[jax.ShapeDtypeStruct((2, 16 + ROWS_B, BLK), bf16)] * 3,
        in_specs=[ANY] * 2 + [VMEM] * 5,
        out_specs=[VMEM] * 3,
        compiler_params=params(),
        cost_estimate=cost(1000, 4_000_000),
        name="low_sum",
    )(after, also, *parts)


def gain_kernel(ids, gain, l1, l2, l3, out, held):
    for back, rows in enumerate((gain_rows(gain), l1[0], l2[0], l3[0])):
        values = rows.astype(f32)
        held[(ids[1] - back) & 3] = jnp.concatenate(
            [values[0:1] + values[1:2], values[2:3] + values[3:4], jnp.zeros((6, BLK), f32)], axis=0
        )
    out[...] = (held[0] + held[1]) + (held[2] + held[3])


def gain_along_y(ids, after, gain, *low):
    return pl.pallas_call(
        later(len(after), gain_kernel),
        grid=(1,),
        out_shape=jax.ShapeDtypeStruct((8, BLK), f32),
        in_specs=[SMEM]
        + [ANY] * len(after)
        + [pl.BlockSpec((2, BLK), lambda k: (0, 0))]
        + [pl.BlockSpec((1, 16, BLK), lambda k: (0, 0, 0))] * 3,
        out_specs=pl.BlockSpec((8, BLK), lambda k: (0, 0)),
        scratch_shapes=[pltpu.VMEM((4, 8, BLK), f32)],
        compiler_params=params(),
        cost_estimate=cost(1000, 50_000),
        name="gain_along_y",
    )(ids, *after, gain, *low)


def join_kernel(ids, _, a0, ra, rb, got, keep, swapped, b1, b2, b3, out):
    for side in range(2):
        cols = pl.ds(pl.multiple_of((ids[4] ^ side) * BLK, BLK), BLK)
        total = a0[0, side].astype(f32) + ra[0, side].astype(f32) + rb[0, side].astype(f32) + got[side].astype(f32)
        out[0:ROWS_A, cols] = total.astype(bf16)
        total = keep[0, side].astype(f32) + swapped[0, side].astype(f32)
        for b in (b1, b2, b3):
            total = total + b[side, 16:, :].astype(f32)
        out[ROWS_A:TERMS, cols] = total.astype(bf16)


def join(ids, after, *parts):
    return pl.pallas_call(
        join_kernel,
        out_shape=jax.ShapeDtypeStruct((TERMS, 2 * BLK), bf16),
        in_specs=[SMEM, ANY] + [VMEM] * len(parts),
        out_specs=VMEM,
        compiler_params=params(),
        cost_estimate=cost(1000, 8_000_000),
        name="join",
    )(ids, after, *parts)


ROWS_T = HALF + 16


def term_step(steps, n):
    step = steps[0]
    for i in range(1, len(steps)):
        step = jnp.where(n < i, step, steps[i])
    return step


def term_kernel(n_steps, split, n_adds, ids, h, w0, w1, dots, *refs):
    n = pl.program_id(0)
    crossed, adds, outs = refs[: n_adds[0]], refs[n_adds[0] : sum(n_adds)], refs[sum(n_adds) :]
    weights = jnp.concatenate([w0[...], w1[...]], axis=1)
    for half in range(2):
        total = jnp.dot(h[half * HALF : (half + 1) * HALF, :], weights, preferred_element_type=f32)
        tail = jnp.concatenate([dots[half * 8 : half * 8 + 8, :], jnp.zeros((8, BLK), f32)], axis=0)
        for m in range(2):
            share = jnp.concatenate([total[:, m * BLK : (m + 1) * BLK], tail], axis=0)
            for ref in crossed:
                share = share + ref[0, half, m].astype(f32)
            if adds:
                got = adds[half][m].astype(f32)
                share = share + jnp.where(n == half, got, 0.0)
            if split:
                outs[half][m] = share.astype(bf16)
            elif len(outs) == 1:
                outs[0][0, half, m] = share.astype(bf16)
            else:
                for i in range(n_steps):

                    @pl.when(n == i)
                    def _(i=i, half=half, m=m, share=share):
                        outs[i][half, m] = share.astype(bf16)


def term_part(ids, steps, side, h, wt, dots, after, split=False, apart=False, crossed=(), adds=(), weight=0.02):
    block = pl.BlockSpec((1, 2, 2, ROWS_T, BLK), lambda n, s: (n, 0, 0, 0, 0))
    part = pl.BlockSpec((2, ROWS_T, BLK), lambda n, s: (0, 0, 0))
    sides = [
        pl.BlockSpec(
            (TERMS, BLK), lambda n, s, m=m: (0, ((s[2] ^ m) * 4 + ((s[3] + term_step(steps, n)) & 3)) * 2 + (s[4] ^ side))
        )
        for m in range(2)
    ]
    count = len(steps)
    outs, specs = [jax.ShapeDtypeStruct((count, 2, 2, ROWS_T, BLK), bf16)], [block]
    if split:
        outs, specs = [jax.ShapeDtypeStruct((2, ROWS_T, BLK), bf16)] * 2, [part] * 2
    elif apart:
        outs = [jax.ShapeDtypeStruct((2, 2, ROWS_T, BLK), bf16)] * count
        specs = [pl.BlockSpec((2, 2, ROWS_T, BLK), lambda n, s: (0, 0, 0, 0))] * count
    return pl.pallas_call(
        later(len(after), functools.partial(term_kernel, count, split, (len(crossed), len(adds)))),
        out_shape=outs,
        grid_spec=pltpu.PrefetchScalarGridSpec(
            num_scalar_prefetch=1,
            grid=(count,),
            in_specs=[ANY] * len(after)
            + [pl.BlockSpec((TOK, TERMS), lambda n, s: (0, 0)), *sides]
            + [pl.BlockSpec((16, BLK), lambda n, s: (0, 0))]
            + [block] * len(crossed)
            + [part] * len(adds),
            out_specs=specs,
        ),
        compiler_params=params(),
        cost_estimate=cost(
            4 * count * TOK * BLK * TERMS, 2 * TOK * TERMS + 2 * count * BLK * (2 * TERMS + 4 * TOK), weight
        ),
        name="term_part",
    )(ids, *after, h, wt, wt, dots, *crossed, *adds)


def term_sum_kernel(own, ra, rb, x, x_p, keep, send, dots, gain):
    sums = [jnp.zeros((8, BLK), f32) for _ in range(2)]
    for half in range(2):
        for m, values in ((0, x), (1, x_p)):
            for first in range(0, ROWS_T, 128):
                rows = slice(first, min(first + 128, ROWS_T))
                total = own[half, m, rows, :].astype(f32)
                for ref in (ra, rb):
                    total = total + ref[half, m, rows, :].astype(f32)
                if m:
                    send[half, rows, :] = total.astype(bf16)
                elif first < HALF:
                    keep[half * HALF + first : half * HALF + first + 128, :] = total.astype(bf16)
                else:
                    dots[half * 8 : half * 8 + 8, :] = total[:8]
                if first < HALF:
                    at = half * HALF + first
                    product = total * values[at : at + 128, :].astype(f32)
                    sums[m] = sums[m] + jnp.sum(product.reshape(16, 8, BLK), axis=0)
    for m in range(2):
        gain[m : m + 1, :] = jnp.sum(sums[m], axis=0, keepdims=True)


def term_sum(after, own, ra, rb, x, x_p):
    count = len(after)
    return pl.pallas_call(
        lambda *refs: term_sum_kernel(*refs[count:]),
        out_shape=[
            jax.ShapeDtypeStruct((TOK, BLK), bf16),
            jax.ShapeDtypeStruct((2, ROWS_T, BLK), bf16),
            jax.ShapeDtypeStruct((16, BLK), f32),
            jax.ShapeDtypeStruct((2, BLK), f32),
        ],
        in_specs=[ANY] * count + [VMEM] * 5,
        out_specs=[VMEM] * 4,
        compiler_params=params(),
        cost_estimate=cost(1_000_000, 5_000_000),
        name="term_sum",
    )(*after, own, ra, rb, x, x_p)


def final_kernel(ids, n_ref, got, x_ref, gain, inv_ref, dots, out):
    g = gain[:, block_at(ids, ids[2] * 4 + ids[3], 0)]
    for half in range(2):
        lines = (dots[half * 8 : half * 8 + 8, :] + got[half, HALF:, :].astype(f32)[:8]) / D
        for k in range(4):
            local = slice(k * LEN, (k + 1) * LEN)
            rows = slice(half * HALF + k * LEN, half * HALF + (k + 1) * LEN)
            grad = n_ref[rows, :].astype(f32) + got[half, local, :].astype(f32)
            values = x_ref[rows, :].astype(f32)
            line = lines[k // 2 : k // 2 + 1, (k % 2) * LEN : (k % 2 + 1) * LEN]
            column = jnp.broadcast_to(line, (LEN, LEN)).T[:, 0:1]
            inverse = inv_ref[rows, :]
            out[rows, :] = (grad * g - values * (inverse * inverse * column)).astype(bf16)


def final(ids, after, n, got, x, gain, inv, dots):
    return pl.pallas_call(
        later(len(after), final_kernel),
        out_shape=jax.ShapeDtypeStruct((TOK, BLK), bf16),
        in_specs=[SMEM] + [ANY] * len(after) + [VMEM] * 6,
        out_specs=VMEM,
        compiler_params=params(),
        cost_estimate=cost(1_000_000, 2_000_000),
        name="hidden_grad",
    )(ids, *after, n, got, x, gain, inv, dots)


def gain_sum_kernel(_, here, there, other, both, out):
    out[...] = (here[0:1, :] + there[0:1, :]) + (other[1:2, :] + both[1:2, :])


def gain_sum(after, parts):
    return pl.pallas_call(
        gain_sum_kernel,
        out_shape=jax.ShapeDtypeStruct((1, BLK), f32),
        in_specs=[ANY] + [VMEM] * 4,
        out_specs=VMEM,
        compiler_params=params(),
        cost_estimate=cost(1000, 5000),
        name="gain_sum",
    )(after, *parts)


def shards(hidden, norm_gain, head_weight, lengths, positives, negatives):
    xh, y, xl, z, c = (lax.axis_index(a).astype(jnp.int32) for a in ("xh", "y", "xl", "z", "c"))
    nil = jnp.int32(0)
    ids = jnp.concatenate([jnp.stack([xh, y, xl, z, c, nil, nil, nil]), positives, negatives.reshape(-1)])
    wt = head_weight.T
    gain = norm_gain.reshape(1, D)

    z_m, z_p, x_p = shift(hidden, "z", 1), shift(hidden, "z", -1), swap(hidden, "xl")
    own_c = swap(hidden, "c")
    z_m_c, z_p_c, x_p_c = (swap(a, "c") for a in (z_m, z_p, x_p))
    far, xz_p, xz_m = shift(z_m, "z", 1), shift(x_p, "z", -1), swap(z_m, "xl")
    state = forward(ids, [(0, 0), (0, -1), (1, 0)], [hidden, own_c, z_m, z_m_c, x_p, x_p_c], wt, gain)
    far, xz_p, xz_m = touch(state[1], far, xz_p, xz_m)
    last = swap(far, "xl")
    far_c, xz_p_c, xz_m_c = (swap(a, "c") for a in (far, xz_p, xz_m))
    state = forward(
        ids,
        [(0, 1), (0, 2), (1, 1), (1, -1)],
        [z_p, z_p_c, far, far_c, xz_p, xz_p_c, xz_m, xz_m_c],
        wt,
        gain,
        state,
    )
    (last,) = touch(state[1], last)
    last_c = swap(last, "c")
    acc, x, inv, weight, pooled = forward_last(ids, lengths, (1, 2), (last, last_c), wt, gain, state)

    pair = jnp.stack([pooled, swap(pooled, "xh")])
    every, part = gram(ids, [pair] + [swap(pair, "y", bits) for bits in (1, 2, 3)])
    part = (part + swap(part, "z", 1)) + (swap(part, "z", 2) + swap(part, "z", 3))
    both = lax.ppermute(part, ("xl", "c"), [(i, i ^ 3) for i in range(4)])
    parts = (part, swap(part, "c"), swap(part, "xl"), both)
    h, ht, dots, losses = grads(ids, every, parts, weight, acc)

    (crossing_2,) = term_part(ids, (2,), 1, h, wt, dots, ())
    (crossing,) = term_part(ids, (1, 3, 0), 1, h, wt, dots, (crossing_2,), weight=20)
    crossed_2, crossed = swap(crossing_2, "c"), swap(crossing, "c")
    term_0, term_1 = term_part(ids, (2,), 0, h, wt, dots, (crossing,), split=True, crossed=(crossed_2,))
    far_0, far_1, keep_2, send_2 = head_part(ids, (2,), ht, x, gain, (term_0,), split=True, weight=20)
    swap_2 = swap(send_2, "xh")
    adds = (shift(term_0, "z", 1), shift(term_1, "z", -1))
    t_1, t_3, t_0 = term_part(
        ids, (1, 3, 0), 0, h, wt, dots, (far_0,), apart=True, crossed=(crossed,), adds=adds, weight=20
    )
    adds = (shift(far_0, "y", 1), shift(far_1, "y", -1))
    a_1, a_3, keep_13, send_13 = head_part(ids, (1, 3), ht, x, gain, (t_0, swap_2), adds=adds, weight=20)
    swap_13 = swap(send_13, "xh")
    ra, rb = shift(a_1, "y", 1), shift(a_3, "y", -1)
    keep, send, dots, partial = term_sum((), t_0, shift(t_1, "z", 1), shift(t_3, "z", -1), hidden, x_p)
    a_0, keep_0, send_0 = head_part(ids, (0,), ht, x, gain, (a_1, keep), weight=20)
    swap_0 = swap(send_0, "xh")
    mine = a_0[1] + ra[1] + rb[1]
    got = swap(mine, "xh")
    low_1, low_3, low_2 = low_sum(mine, swap_0, partial, keep_13, swap_13, keep_2, swap_2)
    low = [shift(low_1, "y", 1), shift(low_2, "y", 2), shift(low_3, "y", 3)]
    hidden_grad = final(ids, (), keep, swap(send, "xl"), hidden, gain, inv, dots)
    gain_grad = gain_along_y(ids, (hidden_grad, swap_0), partial, *low)
    both = lax.ppermute(gain_grad, ("xh", "xl"), [(i, i ^ 3) for i in range(4)])
    parts = (gain_grad, swap(gain_grad, "xh"), swap(gain_grad, "xl"), both)
    head_t = join(ids, hidden_grad, a_0, ra, rb, got, keep_0, swap_0, *low)
    gain_grad = gain_sum(head_t, parts)
    return losses[0, :3], hidden_grad, head_t.T, gain_grad[0]


def solution(mesh):
    fine = Mesh(mesh.devices.reshape(2, 4, 2, 4, 2), ("xh", "y", "xl", "z", "c"))
    dp, vocab = ("xh", "y"), ("xl", "z", "c")
    in_specs = (P(dp, vocab), P(), P(None, vocab), P(dp), P(dp), P(dp, None))
    out_specs = (P(), P(dp, vocab), P(dp, vocab), P(vocab))
    return jax.shard_map(shards, mesh=fine, in_specs=in_specs, out_specs=out_specs, check_vma=False)
```

```python
import functools
import math

import jax
import jax.numpy as jnp
from jax import lax
from jax.experimental import pallas as pl
from jax.experimental.pallas import tpu as pltpu
from jax.sharding import Mesh, PartitionSpec as P

VOCAB = 16000
D = 4096
epsilon = 1e-05
sharpness = 80.0
flops_weight = 0.01

TOK = 1024
SEQ = 8
LEN = 128
TERMS = 1000
BLK = 256
ROWS_A = 688
ROWS_B = TERMS - ROWS_A
HALF = TOK // 2
PER = 2
SCORE_SCALE = 4.0 / math.sqrt(VOCAB)
COLS = ((0, 256), (256, 512), (512, 768), (768, 1000))
SIZES = {"xh": 2, "y": 4, "xl": 2, "z": 4, "c": 2}
VMEM_LIMIT = 67_000_000
HIGHEST = lax.Precision.HIGHEST

f32, bf16 = jnp.float32, jnp.bfloat16


def shift(x, axis, step):
    n = SIZES[axis]
    return lax.ppermute(x, axis, [(i, (i + step) % n) for i in range(n)])


def swap(x, axis, bits=1):
    return lax.ppermute(x, axis, [(i, i ^ bits) for i in range(SIZES[axis])])


def params(**more):
    return pltpu.CompilerParams(vmem_limit_bytes=VMEM_LIMIT, **more)


def cost(flops, moved, weight=0.02):
    return pl.CostEstimate(flops=int(flops * weight), bytes_accessed=int(moved * weight), transcendentals=0)


def tag(ids, pooled_ref):
    lane = lax.broadcasted_iota(jnp.int32, (1, 24), 1)
    for k in range(SEQ):
        tags = jnp.zeros((1, 24), f32)
        if k < 2:
            tags = jnp.where(lane == 0, ids[8 + k].astype(f32), tags)
            tags = jnp.where(lane == 1, ids[10 + 2 * k].astype(f32), tags)
            tags = jnp.where(lane == 2, ids[11 + 2 * k].astype(f32), tags)
        pooled_ref[k : k + 1, TERMS:] = tags


def pool(lengths, first, acc, ssq, inv_ref, weight_ref, pooled_ref):
    for s in range(acc.shape[0] // LEN):
        k = first + s
        rows = slice(s * LEN, (s + 1) * LEN)
        total = jnp.sum(ssq[rows, :], axis=1, keepdims=True)
        inverse = lax.rsqrt(total / D + epsilon)
        inv_ref[rows, :] = inverse
        count = lengths[k]
        for a, b in COLS:
            logits = acc[rows, a:b] * inverse
            valid = lax.broadcasted_iota(jnp.int32, (LEN, b - a), 0) < count
            held = jnp.where(valid, 1.0 + jnp.maximum(logits, 0.0), 1.0)
            top = jnp.max(held, axis=0, keepdims=True)
            down = 1.0 / top
            r1 = held * down
            r2 = r1 * r1
            r4 = r2 * r2
            r8 = r4 * r4
            r16 = r8 * r8
            r32 = r16 * r16
            r79 = (r32 * r32 * r8) * (r4 * (r2 * r1))
            summed = jnp.sum(jnp.where(valid, r79 * r1, 0.0), axis=0, keepdims=True)
            pooled_ref[pl.ds(k, 1), a:b] = jnp.log(top) + jnp.log(summed) / sharpness
            slope = r79 * (down / summed) * inverse
            weight_ref[rows, a:b] = jnp.where(valid & (logits > 0.0), slope, 0.0).astype(bf16)


def chip_of(ids, far_x, step):
    return (ids[2] ^ far_x) * 4 + ((ids[3] + step) & 3)


def block_at(ids, chip, side):
    return pl.ds(pl.multiple_of((chip * 2 + (ids[4] ^ side)) * BLK, BLK), BLK)


def scaled(weights, gain, ids, chip):
    row = jnp.concatenate([gain[:, block_at(ids, chip, side)] for side in range(2)], axis=1)
    return (weights.astype(f32) * row).astype(bf16)


def folded_squares(lefts):
    squares = 0.0
    for left in lefts:
        value = left.astype(f32)
        square = value * value
        squares = squares + square[:, :128] + square[:, 128:]
    return squares


def forward_kernel(places, first, ids, *refs):
    nb = len(places)
    arrays, (weights, gain), refs = refs[: 2 * nb], refs[2 * nb : 2 * nb + 2], refs[2 * nb + 2 :]
    if not first:
        (acc_in, ssq_in, _), refs = refs[:3], refs[3:]
    acc, ssq, kept, held, w_sem, x_sem = refs
    chips = [chip_of(ids, *place) for place in places]
    loads, saves = [], []
    for j in range(nb):
        for side in range(2):
            at = held.at[j, :, side * BLK : (side + 1) * BLK]
            loads.append(pltpu.make_async_copy(weights.at[:, block_at(ids, chips[j], side)], at, w_sem.at[j, side]))
            loads[-1].start()
    for j in range(nb):
        for side in range(2):
            saves.append(pltpu.make_async_copy(arrays[2 * j + side], kept.at[chips[j], side], x_sem.at[j, side]))
            saves[-1].start()
    for j in range(nb):
        loads[2 * j].wait()
        loads[2 * j + 1].wait()
        right = scaled(held[j], gain, ids, chips[j])
        for half in range(2):
            rows = slice(half * HALF, (half + 1) * HALF)
            lefts = [arrays[2 * j + side][rows, :] for side in range(2)]
            squares = folded_squares(lefts)
            product = lax.dot_general(
                jnp.concatenate(lefts, axis=1), right, (((1,), (1,)), ((), ())), preferred_element_type=f32
            )
            if j == 0 and first:
                acc[rows, :] = product
                ssq[rows, :] = squares
            elif j == 0:
                acc[rows, :] = acc_in[rows, :] + product
                ssq[rows, :] = ssq_in[rows, :] + squares
            else:
                acc[rows, :] += product
                ssq[rows, :] += squares
    for copy in saves:
        copy.wait()


SMEM = pl.BlockSpec(memory_space=pltpu.SMEM)
VMEM = pl.BlockSpec(memory_space=pltpu.VMEM)
ANY = pl.BlockSpec(memory_space=pl.ANY)


STATE = [
    jax.ShapeDtypeStruct((TOK, TERMS), f32),
    jax.ShapeDtypeStruct((TOK, 128), f32),
    jax.ShapeDtypeStruct((8, 2, TOK, BLK), bf16),
]


def forward(ids, places, arrays, weights, gain, state=()):
    nb = len(places)
    base = 3 + len(arrays)
    return pl.pallas_call(
        functools.partial(forward_kernel, places, not state),
        out_shape=STATE,
        in_specs=[SMEM] + [VMEM] * len(arrays) + [ANY, VMEM] + [VMEM, VMEM, ANY][: len(state)],
        out_specs=[VMEM, VMEM, ANY],
        scratch_shapes=[
            pltpu.VMEM((nb, TERMS, 2 * BLK), bf16),
            pltpu.SemaphoreType.DMA((nb, 2)),
            pltpu.SemaphoreType.DMA((nb, 2)),
        ],
        input_output_aliases={base + i: i for i in range(len(state))},
        compiler_params=params(),
        cost_estimate=cost(2 * nb * TOK * 512 * TERMS, nb * 3_000_000 + 8_000_000),
        name="forward_part",
    )(ids, *arrays, weights, gain, *state)


STEP = 256


def forward_last_kernel(place, ids, lengths, a0, a1, w0, w1, gain, acc_in, ssq_in, _, *refs):
    product, kept, inv_ref, weight_ref, pooled_ref, acc, right, ssq, sem = refs
    k = pl.program_id(0)
    chip = chip_of(ids, *place)

    @pl.when(k == 0)
    def _():
        right[...] = scaled(jnp.concatenate([w0[...], w1[...]], axis=1), gain, ids, chip)
        tag(ids, pooled_ref)

    rows = pl.ds(pl.multiple_of(k * STEP, STEP), STEP)
    saves = []
    for side, source in enumerate((a0, a1)):
        saves.append(pltpu.make_async_copy(source, kept.at[chip, side, rows, :], sem.at[side]))
        saves[-1].start()
    lefts = [a0[...], a1[...]]
    ssq[...] = ssq_in[...] + folded_squares(lefts)
    acc[...] = acc_in[...] + lax.dot_general(
        jnp.concatenate(lefts, axis=1), right[...], (((1,), (1,)), ((), ())), preferred_element_type=f32
    )
    product[...] = acc[...].astype(bf16)
    pool(lengths, k * (STEP // LEN), acc, ssq, inv_ref, weight_ref, pooled_ref)
    for copy in saves:
        copy.wait()


def forward_last(ids, lengths, place, arrays, weights, gain, state):
    whole = lambda k, *s: (0, 0)
    rows = lambda k, *s: (k, 0)
    sides = [
        pl.BlockSpec((TERMS, BLK), lambda k, s, n, side=side: (0, chip_of(s, *place) * 2 + (s[4] ^ side)))
        for side in range(2)
    ]
    return pl.pallas_call(
        functools.partial(forward_last_kernel, place),
        out_shape=[
            jax.ShapeDtypeStruct((TOK, TERMS), bf16),
            STATE[2],
            jax.ShapeDtypeStruct((TOK, 1), f32),
            jax.ShapeDtypeStruct((TOK, TERMS), bf16),
            jax.ShapeDtypeStruct((SEQ, 1024), f32),
        ],
        grid_spec=pltpu.PrefetchScalarGridSpec(
            num_scalar_prefetch=2,
            grid=(TOK // STEP,),
            in_specs=[pl.BlockSpec((STEP, BLK), rows)] * 2
            + [*sides, pl.BlockSpec((1, D), whole)]
            + [pl.BlockSpec((STEP, TERMS), rows), pl.BlockSpec((STEP, 128), rows), ANY],
            out_specs=[
                pl.BlockSpec((STEP, TERMS), rows),
                ANY,
                pl.BlockSpec((STEP, 1), rows),
                pl.BlockSpec((STEP, TERMS), rows),
                pl.BlockSpec((SEQ, 1024), whole),
            ],
            scratch_shapes=[
                pltpu.VMEM((STEP, TERMS), f32),
                pltpu.VMEM((TERMS, 2 * BLK), bf16),
                pltpu.VMEM((STEP, 128), f32),
                pltpu.SemaphoreType.DMA((2,)),
            ],
        ),
        input_output_aliases={9: 1},
        compiler_params=params(),
        cost_estimate=cost(2 * TOK * 512 * TERMS, 20_000_000),
        name="forward_last",
    )(ids, lengths, *arrays, weights, weights, gain, *state)


def touch_kernel(*refs):
    pass


def touch(after, *arrays):
    n = len(arrays)
    return pl.pallas_call(
        touch_kernel,
        out_shape=[jax.ShapeDtypeStruct(a.shape, a.dtype) for a in arrays],
        in_specs=[ANY] * (n + 1),
        out_specs=[ANY] * n,
        input_output_aliases={i + 1: i for i in range(n)},
        compiler_params=params(has_side_effects=True),
        cost_estimate=cost(1000, 1000),
        name="touch",
    )(after, *arrays)


def gram_kernel(ids, *refs):
    all_ref, part_ref = refs[4:]
    for bits, ref in enumerate(refs[:4]):
        for m in range(2):
            at = (ids[0] * 4 + ids[1]) ^ (4 * m + bits)
            all_ref[pl.ds(pl.multiple_of(at * SEQ, SEQ), SEQ), :] = ref[m]
    every = all_ref[:, :TERMS]
    part = lax.dot_general(every, every, (((1,), (1,)), ((), ())), precision=HIGHEST, preferred_element_type=f32)
    mean = jnp.sum(every, axis=0, keepdims=True) / 64.0
    flops = jnp.sum(mean * mean, axis=1, keepdims=True)
    part_ref[...] = jnp.zeros_like(part_ref)
    part_ref[0:64, 0:64] = part
    part_ref[64:72, :] = jnp.broadcast_to(flops, (8, 128))


def gram(ids, groups):
    return pl.pallas_call(
        gram_kernel,
        out_shape=[jax.ShapeDtypeStruct((64, 1024), f32), jax.ShapeDtypeStruct((72, 128), f32)],
        grid_spec=pltpu.PrefetchScalarGridSpec(
            num_scalar_prefetch=1,
            grid=(),
            in_specs=[VMEM] * 4,
            out_specs=[VMEM] * 2,
        ),
        compiler_params=params(),
        name="gram",
    )(ids, *groups)


def contrast(every, parts, scaled_ref, losses_ref):
    sums = (parts[0][...] + parts[1][...]) + (parts[2][...] + parts[3][...])
    scores = sums[0:64, :] * SCORE_SCALE
    row = lax.broadcasted_iota(jnp.int32, (64, 128), 0)
    col = lax.broadcasted_iota(jnp.int32, (64, 128), 1)
    is_query = (row & 7) < 2
    is_passage = ((col & 7) >= 2) & (col < 64)
    tags = every[:, TERMS:]

    def hot(at):
        index = tags[:, at : at + 1]
        group = jnp.floor((index + 0.5) * (1.0 / 6.0))
        place = group * 8.0 + 2.0 + (index - 6.0 * group)
        return (col.astype(f32) == place).astype(f32)

    positive, negatives = hot(0), (hot(1), hot(2))
    highest = jnp.max(jnp.where(is_passage, scores, -3e38), axis=1, keepdims=True)
    shifted = jnp.where(is_passage, jnp.exp(jnp.minimum(scores - highest, 0.0)), 0.0)
    denominator = jnp.sum(shifted, axis=1, keepdims=True)
    log_total = highest + jnp.log(denominator)
    positive_score = jnp.sum(scores * positive, axis=1, keepdims=True)
    query_row = is_query[:, 0:1]
    cross = jnp.sum(jnp.where(query_row, log_total - positive_score, 0.0), axis=0, keepdims=True) / 16.0
    grad = (shifted / denominator - positive) / 16.0
    margin = jnp.zeros((1, 1), f32)
    for negative in negatives:
        gap = jnp.sum(scores * negative, axis=1, keepdims=True) - positive_score
        small = jnp.exp(-jnp.abs(gap))
        soft = jnp.maximum(gap, 0.0) + jnp.log(1.0 + small)
        slope = jnp.where(gap >= 0.0, 1.0, small) / (1.0 + small) / 32.0
        margin = margin + jnp.sum(jnp.where(query_row, soft, 0.0), axis=0, keepdims=True) / 32.0
        grad = grad + slope * negative - slope * positive
    grad = jnp.where(is_query, grad, 0.0)
    square = jnp.concatenate([grad, jnp.zeros((64, 128), f32)], axis=0)
    scaled_ref[...] = (square + square.T) * SCORE_SCALE
    flops = sums[64:65, 0:1] * flops_weight
    lane = lax.broadcasted_iota(jnp.int32, (8, 128), 1)
    losses_ref[...] = jnp.where(lane == 0, cross, jnp.where(lane == 1, margin, flops))


def grad_kernel(
    ids, every, p0, p1, p2, p3, weight, acc, h_ref, ht_ref, dots, losses_ref, rep, scaled, padded
):
    k = pl.program_id(0)

    @pl.when(k == 0)
    def _():
        contrast(every, (p0, p1, p2, p3), scaled, losses_ref)
        dots[...] = jnp.zeros_like(dots)
        padded[0:64, :] = every[:, :TERMS]
        padded[64:128, :] = jnp.zeros((64, TERMS), f32)
        at = pl.multiple_of((ids[0] * 4 + ids[1]) * SEQ, SEQ)
        own = scaled[pl.ds(at, SEQ), :]
        mean = jnp.sum(padded[...], axis=0, keepdims=True) / 64.0
        rep[...] = jnp.dot(own, padded[...], precision=HIGHEST, preferred_element_type=f32) + (
            2.0 * flops_weight / 64.0
        ) * mean

    lines = []
    for s in range(PER):
        rows = slice(s * LEN, (s + 1) * LEN)
        folded = jnp.zeros((LEN, 128), f32)
        for a, b in COLS:
            grad = weight[rows, a:b].astype(f32) * rep[pl.ds(k * PER + s, 1), a:b]
            rounded = grad.astype(bf16)
            h_ref[rows, a:b] = rounded
            turned = grad.T.astype(bf16)
            ht_ref[a:b, rows] = turned
            product = rounded.astype(f32) * acc[rows, a:b].astype(f32)
            wide = b - a
            folded = folded + product[:, :128]
            if wide == 256:
                folded = folded + product[:, 128:]
            else:
                folded = folded + jnp.concatenate([product[:, 128:], jnp.zeros((LEN, 256 - wide), f32)], axis=1)
        lines.append(jnp.sum(folded.T, axis=0, keepdims=True))
    dots[pl.ds((k >> 1) * 8 + (k & 1), 1), :] = jnp.concatenate(lines, axis=1)


def grads(ids, every, parts, weight, acc):
    whole = lambda k, s: (0, 0)
    rows = lambda k, s: (k, 0)
    cols = lambda k, s: (0, k)
    return pl.pallas_call(
        grad_kernel,
        out_shape=[
            jax.ShapeDtypeStruct((TOK, TERMS), bf16),
            jax.ShapeDtypeStruct((TERMS, TOK), bf16),
            jax.ShapeDtypeStruct((16, BLK), f32),
            jax.ShapeDtypeStruct((8, 128), f32),
        ],
        grid_spec=pltpu.PrefetchScalarGridSpec(
            num_scalar_prefetch=1,
            grid=(SEQ // PER,),
            in_specs=[
                pl.BlockSpec((64, 1024), whole),
                *[pl.BlockSpec((72, 128), whole)] * 4,
                pl.BlockSpec((PER * LEN, TERMS), rows),
                pl.BlockSpec((PER * LEN, TERMS), rows),
            ],
            out_specs=[
                pl.BlockSpec((PER * LEN, TERMS), rows),
                pl.BlockSpec((TERMS, PER * LEN), cols),
                pl.BlockSpec((16, BLK), whole),
                pl.BlockSpec((8, 128), whole),
            ],
            scratch_shapes=[pltpu.VMEM((SEQ, TERMS), f32), pltpu.VMEM((128, 128), f32), pltpu.VMEM((128, TERMS), f32)],
        ),
        compiler_params=params(),
        cost_estimate=cost(20 * TOK * TERMS, 12_000_000),
        name="logit_grad",
    )(ids, every, *parts, weight, acc)


def later(count, kernel):
    return lambda ids, *refs: kernel(ids, *refs[count:])


def place_of(steps, n):
    step = steps[0]
    for i in range(1, len(steps)):
        step = jnp.where(n < 2 * i, step, steps[i])
    return step, n & 1


def head_chip(steps, ids, n):
    step, j = place_of(steps, n)
    return (ids[0] ^ j) * 4 + ((ids[1] + step) & 3)


def head_kernel(steps, split, n_add, ids, ht, x, gain, *refs):
    n = pl.program_id(0)
    adds, outs, (keep, send) = refs[:n_add], refs[n_add:-2], refs[-2:]
    block = jnp.concatenate([x[0, 0], x[0, 1]], axis=1)
    chip = head_chip(steps, ids, n)
    row = jnp.concatenate([gain[:, block_at(ids, chip, side)] for side in range(2)], axis=1)
    total = jnp.dot(ht[...], block, preferred_element_type=f32) * row
    sides = [total[:, :BLK], total[:, BLK:]]
    for i in range(len(steps)):

        @pl.when((n >> 1) == i)
        def _(i=i):
            for side in range(2):
                share = sides[side][:ROWS_A]
                if n_add and side == i:
                    share = share + adds[i][0].astype(f32)
                if split:
                    outs[side][0] = share.astype(bf16)
                else:
                    outs[i][0, side] = share.astype(bf16)

    for j, out in enumerate((keep, send)):

        @pl.when((n & 1) == j)
        def _(out=out):
            for side in range(2):
                out[0, side] = sides[side][ROWS_A:].astype(bf16)


def head_part(ids, steps, ht, x, gain, after, split=False, adds=(), weight=0.02):
    count = len(steps)
    at = lambda i: lambda n, s: (jnp.clip(n - 2 * i, 0, 1), 0, 0)
    at4 = lambda i: lambda n, s: (jnp.clip(n - 2 * i, 0, 1), 0, 0, 0)
    one = pl.BlockSpec((1, ROWS_A, BLK), at(0))
    low = pl.BlockSpec((1, 2, ROWS_B, BLK), lambda n, s: (n // 2, 0, 0, 0))
    if split:
        high, specs = [jax.ShapeDtypeStruct((2, ROWS_A, BLK), bf16)] * 2, [one, one]
    else:
        high = [jax.ShapeDtypeStruct((2, 2, ROWS_A, BLK), bf16)] * count
        specs = [pl.BlockSpec((1, 2, ROWS_A, BLK), at4(i)) for i in range(count)]
    return pl.pallas_call(
        later(len(after), functools.partial(head_kernel, steps, split, len(adds))),
        out_shape=high + [jax.ShapeDtypeStruct((count, 2, ROWS_B, BLK), bf16)] * 2,
        grid_spec=pltpu.PrefetchScalarGridSpec(
            num_scalar_prefetch=1,
            grid=(2 * count,),
            in_specs=[ANY] * len(after)
            + [
                pl.BlockSpec((TERMS, TOK), lambda n, s: (0, 0)),
                pl.BlockSpec((1, 2, TOK, BLK), lambda n, s: (head_chip(steps, s, n), 0, 0, 0)),
                pl.BlockSpec((1, D), lambda n, s: (0, 0)),
            ]
            + [pl.BlockSpec((1, ROWS_A, BLK), at(i)) for i in range(len(adds))],
            out_specs=specs + [low, low],
        ),
        compiler_params=params(),
        cost_estimate=cost(2 * TERMS * TOK * 1024 * count, 2 * TERMS * TOK + 2048 * count * (TOK + TERMS), weight),
        name="head_part",
    )(ids, *after, ht, x, gain, *adds)


def gain_rows(gain):
    rows = []
    for m in range(2):
        value = gain[m : m + 1, :]
        high = value.astype(bf16).astype(f32)
        rows += [high, value - high]
    return jnp.concatenate(rows + [jnp.zeros((12, BLK), f32)], axis=0).astype(bf16)


def low_sum_kernel(_, gain, a13, b13, a2, b2, out_1, out_3, out_2):
    for a, b, i, out in ((a13, b13, 0, out_1), (a13, b13, 1, out_3), (a2, b2, 0, out_2)):
        out[0, 0:16, :] = gain_rows(gain)
        out[1, 0:16, :] = jnp.zeros((16, BLK), bf16)
        out[:, 16:, :] = (a[i].astype(f32) + b[i].astype(f32)).astype(bf16)


def low_sum(after, *parts):
    return pl.pallas_call(
        low_sum_kernel,
        out_shape=[jax.ShapeDtypeStruct((2, 16 + ROWS_B, BLK), bf16)] * 3,
        in_specs=[ANY] + [VMEM] * 5,
        out_specs=[VMEM] * 3,
        compiler_params=params(),
        cost_estimate=cost(1000, 4_000_000),
        name="low_sum",
    )(after, *parts)


def gain_kernel(ids, gain, l1, l2, l3, out, held):
    for back, rows in enumerate((gain_rows(gain), l1[0], l2[0], l3[0])):
        values = rows.astype(f32)
        held[(ids[1] - back) & 3] = jnp.concatenate(
            [values[0:1] + values[1:2], values[2:3] + values[3:4], jnp.zeros((6, BLK), f32)], axis=0
        )
    out[...] = (held[0] + held[1]) + (held[2] + held[3])


def gain_along_y(ids, after, gain, *low):
    return pl.pallas_call(
        later(len(after), gain_kernel),
        grid=(1,),
        out_shape=jax.ShapeDtypeStruct((8, BLK), f32),
        in_specs=[SMEM]
        + [ANY] * len(after)
        + [pl.BlockSpec((2, BLK), lambda k: (0, 0))]
        + [pl.BlockSpec((1, 16, BLK), lambda k: (0, 0, 0))] * 3,
        out_specs=pl.BlockSpec((8, BLK), lambda k: (0, 0)),
        scratch_shapes=[pltpu.VMEM((4, 8, BLK), f32)],
        compiler_params=params(),
        cost_estimate=cost(1000, 50_000),
        name="gain_along_y",
    )(ids, *after, gain, *low)


def join_kernel(ids, _, a0, ra, rb, got, keep, swapped, b1, b2, b3, out):
    for side in range(2):
        cols = pl.ds(pl.multiple_of((ids[4] ^ side) * BLK, BLK), BLK)
        total = a0[0, side].astype(f32) + ra[0, side].astype(f32) + rb[0, side].astype(f32) + got[side].astype(f32)
        out[0:ROWS_A, cols] = total.astype(bf16)
        total = keep[0, side].astype(f32) + swapped[0, side].astype(f32)
        for b in (b1, b2, b3):
            total = total + b[side, 16:, :].astype(f32)
        out[ROWS_A:TERMS, cols] = total.astype(bf16)


def join(ids, after, *parts):
    return pl.pallas_call(
        join_kernel,
        out_shape=jax.ShapeDtypeStruct((TERMS, 2 * BLK), bf16),
        in_specs=[SMEM, ANY] + [VMEM] * len(parts),
        out_specs=VMEM,
        compiler_params=params(),
        cost_estimate=cost(1000, 8_000_000),
        name="join",
    )(ids, after, *parts)


ROWS_T = HALF + 16


def term_step(steps, n):
    step = steps[0]
    for i in range(1, len(steps)):
        step = jnp.where(n < i, step, steps[i])
    return step


def term_kernel(n_steps, split, n_adds, ids, h, w0, w1, dots, *refs):
    n = pl.program_id(0)
    crossed, adds, outs = refs[: n_adds[0]], refs[n_adds[0] : sum(n_adds)], refs[sum(n_adds) :]
    weights = jnp.concatenate([w0[...], w1[...]], axis=1)
    for half in range(2):
        total = jnp.dot(h[half * HALF : (half + 1) * HALF, :], weights, preferred_element_type=f32)
        tail = jnp.concatenate([dots[half * 8 : half * 8 + 8, :], jnp.zeros((8, BLK), f32)], axis=0)
        for m in range(2):
            share = jnp.concatenate([total[:, m * BLK : (m + 1) * BLK], tail], axis=0)
            for ref in crossed:
                share = share + ref[0, half, m].astype(f32)
            if adds:
                got = adds[half][m].astype(f32)
                share = share + jnp.where(n == half, got, 0.0)
            if split:
                outs[half][m] = share.astype(bf16)
            elif len(outs) == 1:
                outs[0][0, half, m] = share.astype(bf16)
            else:
                for i in range(n_steps):

                    @pl.when(n == i)
                    def _(i=i, half=half, m=m, share=share):
                        outs[i][half, m] = share.astype(bf16)


def term_part(ids, steps, side, h, wt, dots, after, split=False, apart=False, crossed=(), adds=(), weight=0.02):
    block = pl.BlockSpec((1, 2, 2, ROWS_T, BLK), lambda n, s: (n, 0, 0, 0, 0))
    part = pl.BlockSpec((2, ROWS_T, BLK), lambda n, s: (0, 0, 0))
    sides = [
        pl.BlockSpec(
            (TERMS, BLK), lambda n, s, m=m: (0, ((s[2] ^ m) * 4 + ((s[3] + term_step(steps, n)) & 3)) * 2 + (s[4] ^ side))
        )
        for m in range(2)
    ]
    count = len(steps)
    outs, specs = [jax.ShapeDtypeStruct((count, 2, 2, ROWS_T, BLK), bf16)], [block]
    if split:
        outs, specs = [jax.ShapeDtypeStruct((2, ROWS_T, BLK), bf16)] * 2, [part] * 2
    elif apart:
        outs = [jax.ShapeDtypeStruct((2, 2, ROWS_T, BLK), bf16)] * count
        specs = [pl.BlockSpec((2, 2, ROWS_T, BLK), lambda n, s: (0, 0, 0, 0))] * count
    return pl.pallas_call(
        later(len(after), functools.partial(term_kernel, count, split, (len(crossed), len(adds)))),
        out_shape=outs,
        grid_spec=pltpu.PrefetchScalarGridSpec(
            num_scalar_prefetch=1,
            grid=(count,),
            in_specs=[ANY] * len(after)
            + [pl.BlockSpec((TOK, TERMS), lambda n, s: (0, 0)), *sides]
            + [pl.BlockSpec((16, BLK), lambda n, s: (0, 0))]
            + [block] * len(crossed)
            + [part] * len(adds),
            out_specs=specs,
        ),
        compiler_params=params(),
        cost_estimate=cost(
            4 * count * TOK * BLK * TERMS, 2 * TOK * TERMS + 2 * count * BLK * (2 * TERMS + 4 * TOK), weight
        ),
        name="term_part",
    )(ids, *after, h, wt, wt, dots, *crossed, *adds)


def term_sum_kernel(own, ra, rb, x, x_p, keep, send, dots, gain):
    sums = [jnp.zeros((8, BLK), f32) for _ in range(2)]
    for half in range(2):
        for m, values in ((0, x), (1, x_p)):
            for first in range(0, ROWS_T, 128):
                rows = slice(first, min(first + 128, ROWS_T))
                total = own[half, m, rows, :].astype(f32)
                for ref in (ra, rb):
                    total = total + ref[half, m, rows, :].astype(f32)
                if m:
                    send[half, rows, :] = total.astype(bf16)
                elif first < HALF:
                    keep[half * HALF + first : half * HALF + first + 128, :] = total.astype(bf16)
                else:
                    dots[half * 8 : half * 8 + 8, :] = total[:8]
                if first < HALF:
                    at = half * HALF + first
                    product = total * values[at : at + 128, :].astype(f32)
                    sums[m] = sums[m] + jnp.sum(product.reshape(16, 8, BLK), axis=0)
    for m in range(2):
        gain[m : m + 1, :] = jnp.sum(sums[m], axis=0, keepdims=True)


def term_sum(after, own, ra, rb, x, x_p):
    count = len(after)
    return pl.pallas_call(
        lambda *refs: term_sum_kernel(*refs[count:]),
        out_shape=[
            jax.ShapeDtypeStruct((TOK, BLK), bf16),
            jax.ShapeDtypeStruct((2, ROWS_T, BLK), bf16),
            jax.ShapeDtypeStruct((16, BLK), f32),
            jax.ShapeDtypeStruct((2, BLK), f32),
        ],
        in_specs=[ANY] * count + [VMEM] * 5,
        out_specs=[VMEM] * 4,
        compiler_params=params(),
        cost_estimate=cost(1_000_000, 5_000_000),
        name="term_sum",
    )(*after, own, ra, rb, x, x_p)


def final_kernel(ids, n_ref, got, x_ref, gain, inv_ref, dots, out):
    g = gain[:, block_at(ids, ids[2] * 4 + ids[3], 0)]
    for half in range(2):
        lines = (dots[half * 8 : half * 8 + 8, :] + got[half, HALF:, :].astype(f32)[:8]) / D
        for k in range(4):
            local = slice(k * LEN, (k + 1) * LEN)
            rows = slice(half * HALF + k * LEN, half * HALF + (k + 1) * LEN)
            grad = n_ref[rows, :].astype(f32) + got[half, local, :].astype(f32)
            values = x_ref[rows, :].astype(f32)
            line = lines[k // 2 : k // 2 + 1, (k % 2) * LEN : (k % 2 + 1) * LEN]
            column = jnp.broadcast_to(line, (LEN, LEN)).T[:, 0:1]
            inverse = inv_ref[rows, :]
            out[rows, :] = (grad * g - values * (inverse * inverse * column)).astype(bf16)


def final(ids, after, n, got, x, gain, inv, dots):
    return pl.pallas_call(
        later(len(after), final_kernel),
        out_shape=jax.ShapeDtypeStruct((TOK, BLK), bf16),
        in_specs=[SMEM] + [ANY] * len(after) + [VMEM] * 6,
        out_specs=VMEM,
        compiler_params=params(),
        cost_estimate=cost(1_000_000, 2_000_000),
        name="hidden_grad",
    )(ids, *after, n, got, x, gain, inv, dots)


def shards(hidden, norm_gain, head_weight, lengths, positives, negatives):
    xh, y, xl, z, c = (lax.axis_index(a).astype(jnp.int32) for a in ("xh", "y", "xl", "z", "c"))
    nil = jnp.int32(0)
    ids = jnp.concatenate([jnp.stack([xh, y, xl, z, c, nil, nil, nil]), positives, negatives.reshape(-1)])
    wt = head_weight.T
    gain = norm_gain.reshape(1, D)

    z_m, z_p, x_p = shift(hidden, "z", 1), shift(hidden, "z", -1), swap(hidden, "xl")
    own_c = swap(hidden, "c")
    z_m_c, z_p_c, x_p_c = (swap(a, "c") for a in (z_m, z_p, x_p))
    far, xz_p, xz_m = shift(z_m, "z", 1), shift(x_p, "z", -1), swap(z_m, "xl")
    state = forward(ids, [(0, 0), (0, -1), (1, 0)], [hidden, own_c, z_m, z_m_c, x_p, x_p_c], wt, gain)
    far, xz_p, xz_m = touch(state[1], far, xz_p, xz_m)
    last = swap(far, "xl")
    far_c, xz_p_c, xz_m_c = (swap(a, "c") for a in (far, xz_p, xz_m))
    state = forward(
        ids,
        [(0, 1), (0, 2), (1, 1), (1, -1)],
        [z_p, z_p_c, far, far_c, xz_p, xz_p_c, xz_m, xz_m_c],
        wt,
        gain,
        state,
    )
    (last,) = touch(state[1], last)
    last_c = swap(last, "c")
    acc, x, inv, weight, pooled = forward_last(ids, lengths, (1, 2), (last, last_c), wt, gain, state)

    pair = jnp.stack([pooled, swap(pooled, "xh")])
    every, part = gram(ids, [pair] + [swap(pair, "y", bits) for bits in (1, 2, 3)])
    part = (part + swap(part, "z", 1)) + (swap(part, "z", 2) + swap(part, "z", 3))
    both = lax.ppermute(part, ("xl", "c"), [(i, i ^ 3) for i in range(4)])
    parts = (part, swap(part, "c"), swap(part, "xl"), both)
    h, ht, dots, losses = grads(ids, every, parts, weight, acc)

    (crossing_2,) = term_part(ids, (2,), 1, h, wt, dots, ())
    (crossing,) = term_part(ids, (1, 3, 0), 1, h, wt, dots, (crossing_2,), weight=20)
    crossed_2, crossed = swap(crossing_2, "c"), swap(crossing, "c")
    term_0, term_1 = term_part(ids, (2,), 0, h, wt, dots, (crossing,), split=True, crossed=(crossed_2,))
    far_0, far_1, keep_2, send_2 = head_part(ids, (2,), ht, x, gain, (term_0,), split=True, weight=20)
    swap_2 = swap(send_2, "xh")
    adds = (shift(term_0, "z", 1), shift(term_1, "z", -1))
    t_1, t_3, t_0 = term_part(
        ids, (1, 3, 0), 0, h, wt, dots, (far_0,), apart=True, crossed=(crossed,), adds=adds, weight=20
    )
    adds = (shift(far_0, "y", 1), shift(far_1, "y", -1))
    a_1, a_3, keep_13, send_13 = head_part(ids, (1, 3), ht, x, gain, (t_0, swap_2), adds=adds, weight=20)
    swap_13 = swap(send_13, "xh")
    ra, rb = shift(a_1, "y", 1), shift(a_3, "y", -1)
    keep, send, dots, partial = term_sum((), t_0, shift(t_1, "z", 1), shift(t_3, "z", -1), hidden, x_p)
    a_0, keep_0, send_0 = head_part(ids, (0,), ht, x, gain, (a_1, keep), weight=20)
    swap_0 = swap(send_0, "xh")
    got = swap(a_0[1] + ra[1] + rb[1], "xh")
    low_1, low_3, low_2 = low_sum(swap_0, partial, keep_13, swap_13, keep_2, swap_2)
    low = [shift(low_1, "y", 1), shift(low_2, "y", 2), shift(low_3, "y", 3)]
    hidden_grad = final(ids, (), keep, swap(send, "xl"), hidden, gain, inv, dots)
    gain_grad = gain_along_y(ids, (hidden_grad, swap_0), partial, *low)
    both = lax.ppermute(gain_grad, ("xh", "xl"), [(i, i ^ 3) for i in range(4)])
    gain_grad = (gain_grad[0] + swap(gain_grad, "xh")[0]) + (swap(gain_grad, "xl")[1] + both[1])
    head_t = join(ids, hidden_grad, a_0, ra, rb, got, keep_0, swap_0, *low)
    return losses[0, :3], hidden_grad, head_t.T, gain_grad


def solution(mesh):
    fine = Mesh(mesh.devices.reshape(2, 4, 2, 4, 2), ("xh", "y", "xl", "z", "c"))
    dp, vocab = ("xh", "y"), ("xl", "z", "c")
    in_specs = (P(dp, vocab), P(), P(None, vocab), P(dp), P(dp), P(dp, None))
    out_specs = (P(), P(dp, vocab), P(dp, vocab), P(vocab))
    return jax.shard_map(shards, mesh=fine, in_specs=in_specs, out_specs=out_specs, check_vma=False)
```

```python
import functools
import math

import jax
import jax.numpy as jnp
from jax import lax
from jax.experimental import pallas as pl
from jax.experimental.pallas import tpu as pltpu
from jax.sharding import Mesh, PartitionSpec as P

VOCAB = 16000
D = 4096
epsilon = 1e-05
sharpness = 80.0
flops_weight = 0.01

TOK = 1024
SEQ = 8
LEN = 128
TERMS = 1000
BLK = 256
ROWS_A = 752
ROWS_B = TERMS - ROWS_A
HALF = TOK // 2
PER = 2
SCORE_SCALE = 4.0 / math.sqrt(VOCAB)
COLS = ((0, 256), (256, 512), (512, 768), (768, 1000))
SIZES = {"xh": 2, "y": 4, "xl": 2, "z": 4, "c": 2}
VMEM_LIMIT = 67_000_000
HIGHEST = lax.Precision.HIGHEST

f32, bf16 = jnp.float32, jnp.bfloat16


def shift(x, axis, step):
    n = SIZES[axis]
    return lax.ppermute(x, axis, [(i, (i + step) % n) for i in range(n)])


def swap(x, axis, bits=1):
    return lax.ppermute(x, axis, [(i, i ^ bits) for i in range(SIZES[axis])])


def params(**more):
    return pltpu.CompilerParams(vmem_limit_bytes=VMEM_LIMIT, **more)


def cost(flops, moved, weight=0.02):
    return pl.CostEstimate(flops=int(flops * weight), bytes_accessed=int(moved * weight), transcendentals=0)


def tag(ids, pooled_ref):
    lane = lax.broadcasted_iota(jnp.int32, (1, 24), 1)
    for k in range(SEQ):
        tags = jnp.zeros((1, 24), f32)
        if k < 2:
            tags = jnp.where(lane == 0, ids[8 + k].astype(f32), tags)
            tags = jnp.where(lane == 1, ids[10 + 2 * k].astype(f32), tags)
            tags = jnp.where(lane == 2, ids[11 + 2 * k].astype(f32), tags)
        pooled_ref[k : k + 1, TERMS:] = tags


def pool(lengths, first, acc, ssq, inv_ref, weight_ref, pooled_ref):
    for s in range(acc.shape[0] // LEN):
        k = first + s
        rows = slice(s * LEN, (s + 1) * LEN)
        total = jnp.sum(ssq[rows, :], axis=1, keepdims=True)
        inverse = lax.rsqrt(total / D + epsilon)
        inv_ref[rows, :] = inverse
        count = lengths[k]
        for a, b in COLS:
            logits = acc[rows, a:b] * inverse
            valid = lax.broadcasted_iota(jnp.int32, (LEN, b - a), 0) < count
            held = jnp.where(valid, 1.0 + jnp.maximum(logits, 0.0), 1.0)
            top = jnp.max(held, axis=0, keepdims=True)
            down = 1.0 / top
            r1 = held * down
            r2 = r1 * r1
            r4 = r2 * r2
            r8 = r4 * r4
            r16 = r8 * r8
            r32 = r16 * r16
            r79 = (r32 * r32 * r8) * (r4 * (r2 * r1))
            summed = jnp.sum(jnp.where(valid, r79 * r1, 0.0), axis=0, keepdims=True)
            pooled_ref[pl.ds(k, 1), a:b] = jnp.log(top) + jnp.log(summed) / sharpness
            slope = r79 * (down / summed) * inverse
            weight_ref[rows, a:b] = jnp.where(valid & (logits > 0.0), slope, 0.0).astype(bf16)


def chip_of(ids, far_x, step):
    return (ids[2] ^ far_x) * 4 + ((ids[3] + step) & 3)


def block_at(ids, chip, side):
    return pl.ds(pl.multiple_of((chip * 2 + (ids[4] ^ side)) * BLK, BLK), BLK)


def scaled(weights, gain, ids, chip):
    row = jnp.concatenate([gain[:, block_at(ids, chip, side)] for side in range(2)], axis=1)
    return (weights.astype(f32) * row).astype(bf16)


def folded_squares(lefts):
    squares = 0.0
    for left in lefts:
        value = left.astype(f32)
        square = value * value
        squares = squares + square[:, :128] + square[:, 128:]
    return squares


def forward_kernel(places, first, ids, *refs):
    nb = len(places)
    arrays, (weights, gain), refs = refs[: 2 * nb], refs[2 * nb : 2 * nb + 2], refs[2 * nb + 2 :]
    if not first:
        (acc_in, ssq_in, _), refs = refs[:3], refs[3:]
    acc, ssq, kept, held, w_sem, x_sem = refs
    chips = [chip_of(ids, *place) for place in places]
    loads, saves = [], []
    for j in range(nb):
        for side in range(2):
            at = held.at[j, :, side * BLK : (side + 1) * BLK]
            loads.append(pltpu.make_async_copy(weights.at[:, block_at(ids, chips[j], side)], at, w_sem.at[j, side]))
            loads[-1].start()
    for j in range(nb):
        for side in range(2):
            saves.append(pltpu.make_async_copy(arrays[2 * j + side], kept.at[chips[j], side], x_sem.at[j, side]))
            saves[-1].start()
    for j in range(nb):
        loads[2 * j].wait()
        loads[2 * j + 1].wait()
        right = scaled(held[j], gain, ids, chips[j])
        for half in range(2):
            rows = slice(half * HALF, (half + 1) * HALF)
            lefts = [arrays[2 * j + side][rows, :] for side in range(2)]
            squares = folded_squares(lefts)
            product = lax.dot_general(
                jnp.concatenate(lefts, axis=1), right, (((1,), (1,)), ((), ())), preferred_element_type=f32
            )
            if j == 0 and first:
                acc[rows, :] = product
                ssq[rows, :] = squares
            elif j == 0:
                acc[rows, :] = acc_in[rows, :] + product
                ssq[rows, :] = ssq_in[rows, :] + squares
            else:
                acc[rows, :] += product
                ssq[rows, :] += squares
    for copy in saves:
        copy.wait()


SMEM = pl.BlockSpec(memory_space=pltpu.SMEM)
VMEM = pl.BlockSpec(memory_space=pltpu.VMEM)
ANY = pl.BlockSpec(memory_space=pl.ANY)


STATE = [
    jax.ShapeDtypeStruct((TOK, TERMS), f32),
    jax.ShapeDtypeStruct((TOK, 128), f32),
    jax.ShapeDtypeStruct((8, 2, TOK, BLK), bf16),
]


def forward(ids, places, arrays, weights, gain, state=()):
    nb = len(places)
    base = 3 + len(arrays)
    return pl.pallas_call(
        functools.partial(forward_kernel, places, not state),
        out_shape=STATE,
        in_specs=[SMEM] + [VMEM] * len(arrays) + [ANY, VMEM] + [VMEM, VMEM, ANY][: len(state)],
        out_specs=[VMEM, VMEM, ANY],
        scratch_shapes=[
            pltpu.VMEM((nb, TERMS, 2 * BLK), bf16),
            pltpu.SemaphoreType.DMA((nb, 2)),
            pltpu.SemaphoreType.DMA((nb, 2)),
        ],
        input_output_aliases={base + i: i for i in range(len(state))},
        compiler_params=params(),
        cost_estimate=cost(2 * nb * TOK * 512 * TERMS, nb * 3_000_000 + 8_000_000),
        name="forward_part",
    )(ids, *arrays, weights, gain, *state)


STEP = 256


def forward_last_kernel(place, ids, lengths, a0, a1, w0, w1, gain, acc_in, ssq_in, _, *refs):
    product, kept, inv_ref, weight_ref, pooled_ref, acc, right, ssq, sem = refs
    k = pl.program_id(0)
    chip = chip_of(ids, *place)

    @pl.when(k == 0)
    def _():
        right[...] = scaled(jnp.concatenate([w0[...], w1[...]], axis=1), gain, ids, chip)
        tag(ids, pooled_ref)

    rows = pl.ds(pl.multiple_of(k * STEP, STEP), STEP)
    saves = []
    for side, source in enumerate((a0, a1)):
        saves.append(pltpu.make_async_copy(source, kept.at[chip, side, rows, :], sem.at[side]))
        saves[-1].start()
    lefts = [a0[...], a1[...]]
    ssq[...] = ssq_in[...] + folded_squares(lefts)
    acc[...] = acc_in[...] + lax.dot_general(
        jnp.concatenate(lefts, axis=1), right[...], (((1,), (1,)), ((), ())), preferred_element_type=f32
    )
    product[...] = acc[...].astype(bf16)
    pool(lengths, k * (STEP // LEN), acc, ssq, inv_ref, weight_ref, pooled_ref)
    for copy in saves:
        copy.wait()


def forward_last(ids, lengths, place, arrays, weights, gain, state):
    whole = lambda k, *s: (0, 0)
    rows = lambda k, *s: (k, 0)
    sides = [
        pl.BlockSpec((TERMS, BLK), lambda k, s, n, side=side: (0, chip_of(s, *place) * 2 + (s[4] ^ side)))
        for side in range(2)
    ]
    return pl.pallas_call(
        functools.partial(forward_last_kernel, place),
        out_shape=[
            jax.ShapeDtypeStruct((TOK, TERMS), bf16),
            STATE[2],
            jax.ShapeDtypeStruct((TOK, 1), f32),
            jax.ShapeDtypeStruct((TOK, TERMS), bf16),
            jax.ShapeDtypeStruct((SEQ, 1024), f32),
        ],
        grid_spec=pltpu.PrefetchScalarGridSpec(
            num_scalar_prefetch=2,
            grid=(TOK // STEP,),
            in_specs=[pl.BlockSpec((STEP, BLK), rows)] * 2
            + [*sides, pl.BlockSpec((1, D), whole)]
            + [pl.BlockSpec((STEP, TERMS), rows), pl.BlockSpec((STEP, 128), rows), ANY],
            out_specs=[
                pl.BlockSpec((STEP, TERMS), rows),
                ANY,
                pl.BlockSpec((STEP, 1), rows),
                pl.BlockSpec((STEP, TERMS), rows),
                pl.BlockSpec((SEQ, 1024), whole),
            ],
            scratch_shapes=[
                pltpu.VMEM((STEP, TERMS), f32),
                pltpu.VMEM((TERMS, 2 * BLK), bf16),
                pltpu.VMEM((STEP, 128), f32),
                pltpu.SemaphoreType.DMA((2,)),
            ],
        ),
        input_output_aliases={9: 1},
        compiler_params=params(),
        cost_estimate=cost(2 * TOK * 512 * TERMS, 20_000_000),
        name="forward_last",
    )(ids, lengths, *arrays, weights, weights, gain, *state)


def touch_kernel(*refs):
    pass


def touch(after, *arrays):
    n = len(arrays)
    return pl.pallas_call(
        touch_kernel,
        out_shape=[jax.ShapeDtypeStruct(a.shape, a.dtype) for a in arrays],
        in_specs=[ANY] * (n + 1),
        out_specs=[ANY] * n,
        input_output_aliases={i + 1: i for i in range(n)},
        compiler_params=params(has_side_effects=True),
        cost_estimate=cost(1000, 1000),
        name="touch",
    )(after, *arrays)


def gram_kernel(ids, *refs):
    all_ref, part_ref = refs[4:]
    for bits, ref in enumerate(refs[:4]):
        for m in range(2):
            at = (ids[0] * 4 + ids[1]) ^ (4 * m + bits)
            all_ref[pl.ds(pl.multiple_of(at * SEQ, SEQ), SEQ), :] = ref[m]
    every = all_ref[:, :TERMS]
    part = lax.dot_general(every, every, (((1,), (1,)), ((), ())), precision=HIGHEST, preferred_element_type=f32)
    mean = jnp.sum(every, axis=0, keepdims=True) / 64.0
    flops = jnp.sum(mean * mean, axis=1, keepdims=True)
    part_ref[...] = jnp.zeros_like(part_ref)
    part_ref[0:64, 0:64] = part
    part_ref[64:72, :] = jnp.broadcast_to(flops, (8, 128))


def gram(ids, groups):
    return pl.pallas_call(
        gram_kernel,
        out_shape=[jax.ShapeDtypeStruct((64, 1024), f32), jax.ShapeDtypeStruct((72, 128), f32)],
        grid_spec=pltpu.PrefetchScalarGridSpec(
            num_scalar_prefetch=1,
            grid=(),
            in_specs=[VMEM] * 4,
            out_specs=[VMEM] * 2,
        ),
        compiler_params=params(),
        name="gram",
    )(ids, *groups)


def contrast(every, parts, scaled_ref, losses_ref):
    sums = (parts[0][...] + parts[1][...]) + (parts[2][...] + parts[3][...])
    scores = sums[0:64, :] * SCORE_SCALE
    row = lax.broadcasted_iota(jnp.int32, (64, 128), 0)
    col = lax.broadcasted_iota(jnp.int32, (64, 128), 1)
    is_query = (row & 7) < 2
    is_passage = ((col & 7) >= 2) & (col < 64)
    tags = every[:, TERMS:]

    def hot(at):
        index = tags[:, at : at + 1]
        group = jnp.floor((index + 0.5) * (1.0 / 6.0))
        place = group * 8.0 + 2.0 + (index - 6.0 * group)
        return (col.astype(f32) == place).astype(f32)

    positive, negatives = hot(0), (hot(1), hot(2))
    highest = jnp.max(jnp.where(is_passage, scores, -3e38), axis=1, keepdims=True)
    shifted = jnp.where(is_passage, jnp.exp(jnp.minimum(scores - highest, 0.0)), 0.0)
    denominator = jnp.sum(shifted, axis=1, keepdims=True)
    log_total = highest + jnp.log(denominator)
    positive_score = jnp.sum(scores * positive, axis=1, keepdims=True)
    query_row = is_query[:, 0:1]
    cross = jnp.sum(jnp.where(query_row, log_total - positive_score, 0.0), axis=0, keepdims=True) / 16.0
    grad = (shifted / denominator - positive) / 16.0
    margin = jnp.zeros((1, 1), f32)
    for negative in negatives:
        gap = jnp.sum(scores * negative, axis=1, keepdims=True) - positive_score
        small = jnp.exp(-jnp.abs(gap))
        soft = jnp.maximum(gap, 0.0) + jnp.log(1.0 + small)
        slope = jnp.where(gap >= 0.0, 1.0, small) / (1.0 + small) / 32.0
        margin = margin + jnp.sum(jnp.where(query_row, soft, 0.0), axis=0, keepdims=True) / 32.0
        grad = grad + slope * negative - slope * positive
    grad = jnp.where(is_query, grad, 0.0)
    square = jnp.concatenate([grad, jnp.zeros((64, 128), f32)], axis=0)
    scaled_ref[...] = (square + square.T) * SCORE_SCALE
    flops = sums[64:65, 0:1] * flops_weight
    lane = lax.broadcasted_iota(jnp.int32, (8, 128), 1)
    losses_ref[...] = jnp.where(lane == 0, cross, jnp.where(lane == 1, margin, flops))


def grad_kernel(
    ids, every, p0, p1, p2, p3, weight, acc, h_ref, ht_ref, dots, losses_ref, rep, scaled, padded
):
    k = pl.program_id(0)

    @pl.when(k == 0)
    def _():
        contrast(every, (p0, p1, p2, p3), scaled, losses_ref)
        dots[...] = jnp.zeros_like(dots)
        padded[0:64, :] = every[:, :TERMS]
        padded[64:128, :] = jnp.zeros((64, TERMS), f32)
        at = pl.multiple_of((ids[0] * 4 + ids[1]) * SEQ, SEQ)
        own = scaled[pl.ds(at, SEQ), :]
        mean = jnp.sum(padded[...], axis=0, keepdims=True) / 64.0
        rep[...] = jnp.dot(own, padded[...], precision=HIGHEST, preferred_element_type=f32) + (
            2.0 * flops_weight / 64.0
        ) * mean

    lines = []
    for s in range(PER):
        rows = slice(s * LEN, (s + 1) * LEN)
        folded = jnp.zeros((LEN, 128), f32)
        for a, b in COLS:
            grad = weight[rows, a:b].astype(f32) * rep[pl.ds(k * PER + s, 1), a:b]
            rounded = grad.astype(bf16)
            h_ref[rows, a:b] = rounded
            turned = grad.T.astype(bf16)
            ht_ref[a:b, rows] = turned
            product = rounded.astype(f32) * acc[rows, a:b].astype(f32)
            wide = b - a
            folded = folded + product[:, :128]
            if wide == 256:
                folded = folded + product[:, 128:]
            else:
                folded = folded + jnp.concatenate([product[:, 128:], jnp.zeros((LEN, 256 - wide), f32)], axis=1)
        lines.append(jnp.sum(folded.T, axis=0, keepdims=True))
    dots[pl.ds((k >> 1) * 8 + (k & 1), 1), :] = jnp.concatenate(lines, axis=1)


def grads(ids, every, parts, weight, acc):
    whole = lambda k, s: (0, 0)
    rows = lambda k, s: (k, 0)
    cols = lambda k, s: (0, k)
    return pl.pallas_call(
        grad_kernel,
        out_shape=[
            jax.ShapeDtypeStruct((TOK, TERMS), bf16),
            jax.ShapeDtypeStruct((TERMS, TOK), bf16),
            jax.ShapeDtypeStruct((16, BLK), f32),
            jax.ShapeDtypeStruct((8, 128), f32),
        ],
        grid_spec=pltpu.PrefetchScalarGridSpec(
            num_scalar_prefetch=1,
            grid=(SEQ // PER,),
            in_specs=[
                pl.BlockSpec((64, 1024), whole),
                *[pl.BlockSpec((72, 128), whole)] * 4,
                pl.BlockSpec((PER * LEN, TERMS), rows),
                pl.BlockSpec((PER * LEN, TERMS), rows),
            ],
            out_specs=[
                pl.BlockSpec((PER * LEN, TERMS), rows),
                pl.BlockSpec((TERMS, PER * LEN), cols),
                pl.BlockSpec((16, BLK), whole),
                pl.BlockSpec((8, 128), whole),
            ],
            scratch_shapes=[pltpu.VMEM((SEQ, TERMS), f32), pltpu.VMEM((128, 128), f32), pltpu.VMEM((128, TERMS), f32)],
        ),
        compiler_params=params(),
        cost_estimate=cost(20 * TOK * TERMS, 12_000_000),
        name="logit_grad",
    )(ids, every, *parts, weight, acc)


def later(count, kernel):
    return lambda ids, *refs: kernel(ids, *refs[count:])


def place_of(steps, n):
    step = steps[0]
    for i in range(1, len(steps)):
        step = jnp.where(n < 2 * i, step, steps[i])
    return step, n & 1


def head_chip(steps, ids, n):
    step, j = place_of(steps, n)
    return (ids[0] ^ j) * 4 + ((ids[1] + step) & 3)


def head_kernel(steps, split, n_add, ids, ht, x, gain, *refs):
    n = pl.program_id(0)
    adds, outs, (keep, send) = refs[:n_add], refs[n_add:-2], refs[-2:]
    block = jnp.concatenate([x[0, 0], x[0, 1]], axis=1)
    chip = head_chip(steps, ids, n)
    row = jnp.concatenate([gain[:, block_at(ids, chip, side)] for side in range(2)], axis=1)
    total = jnp.dot(ht[...], block, preferred_element_type=f32) * row
    sides = [total[:, :BLK], total[:, BLK:]]
    for i in range(len(steps)):

        @pl.when((n >> 1) == i)
        def _(i=i):
            for side in range(2):
                share = sides[side][:ROWS_A]
                if n_add and side == i:
                    share = share + adds[i][0].astype(f32)
                if split:
                    outs[side][0] = share.astype(bf16)
                else:
                    outs[i][0, side] = share.astype(bf16)

    for j, out in enumerate((keep, send)):

        @pl.when((n & 1) == j)
        def _(out=out):
            for side in range(2):
                out[0, side] = sides[side][ROWS_A:].astype(bf16)


def head_part(ids, steps, ht, x, gain, after, split=False, adds=(), weight=0.02):
    count = len(steps)
    at = lambda i: lambda n, s: (jnp.clip(n - 2 * i, 0, 1), 0, 0)
    at4 = lambda i: lambda n, s: (jnp.clip(n - 2 * i, 0, 1), 0, 0, 0)
    one = pl.BlockSpec((1, ROWS_A, BLK), at(0))
    low = pl.BlockSpec((1, 2, ROWS_B, BLK), lambda n, s: (n // 2, 0, 0, 0))
    if split:
        high, specs = [jax.ShapeDtypeStruct((2, ROWS_A, BLK), bf16)] * 2, [one, one]
    else:
        high = [jax.ShapeDtypeStruct((2, 2, ROWS_A, BLK), bf16)] * count
        specs = [pl.BlockSpec((1, 2, ROWS_A, BLK), at4(i)) for i in range(count)]
    return pl.pallas_call(
        later(len(after), functools.partial(head_kernel, steps, split, len(adds))),
        out_shape=high + [jax.ShapeDtypeStruct((count, 2, ROWS_B, BLK), bf16)] * 2,
        grid_spec=pltpu.PrefetchScalarGridSpec(
            num_scalar_prefetch=1,
            grid=(2 * count,),
            in_specs=[ANY] * len(after)
            + [
                pl.BlockSpec((TERMS, TOK), lambda n, s: (0, 0)),
                pl.BlockSpec((1, 2, TOK, BLK), lambda n, s: (head_chip(steps, s, n), 0, 0, 0)),
                pl.BlockSpec((1, D), lambda n, s: (0, 0)),
            ]
            + [pl.BlockSpec((1, ROWS_A, BLK), at(i)) for i in range(len(adds))],
            out_specs=specs + [low, low],
        ),
        compiler_params=params(),
        cost_estimate=cost(2 * TERMS * TOK * 1024 * count, 2 * TERMS * TOK + 2048 * count * (TOK + TERMS), weight),
        name="head_part",
    )(ids, *after, ht, x, gain, *adds)


def gain_rows(gain):
    rows = []
    for m in range(2):
        value = gain[m : m + 1, :]
        high = value.astype(bf16).astype(f32)
        rows += [high, value - high]
    return jnp.concatenate(rows + [jnp.zeros((12, BLK), f32)], axis=0).astype(bf16)


def low_sum_kernel(_, gain, a13, b13, a2, b2, out_1, out_3, out_2):
    for a, b, i, out in ((a13, b13, 0, out_1), (a13, b13, 1, out_3), (a2, b2, 0, out_2)):
        out[0, 0:16, :] = gain_rows(gain)
        out[1, 0:16, :] = jnp.zeros((16, BLK), bf16)
        out[:, 16:, :] = (a[i].astype(f32) + b[i].astype(f32)).astype(bf16)


def low_sum(after, *parts):
    return pl.pallas_call(
        low_sum_kernel,
        out_shape=[jax.ShapeDtypeStruct((2, 16 + ROWS_B, BLK), bf16)] * 3,
        in_specs=[ANY] + [VMEM] * 5,
        out_specs=[VMEM] * 3,
        compiler_params=params(),
        cost_estimate=cost(1000, 4_000_000),
        name="low_sum",
    )(after, *parts)


def gain_kernel(ids, gain, l1, l2, l3, out, held):
    for back, rows in enumerate((gain_rows(gain), l1[0], l2[0], l3[0])):
        values = rows.astype(f32)
        held[(ids[1] - back) & 3] = jnp.concatenate(
            [values[0:1] + values[1:2], values[2:3] + values[3:4], jnp.zeros((6, BLK), f32)], axis=0
        )
    out[...] = (held[0] + held[1]) + (held[2] + held[3])


def gain_along_y(ids, after, gain, *low):
    return pl.pallas_call(
        later(len(after), gain_kernel),
        grid=(1,),
        out_shape=jax.ShapeDtypeStruct((8, BLK), f32),
        in_specs=[SMEM]
        + [ANY] * len(after)
        + [pl.BlockSpec((2, BLK), lambda k: (0, 0))]
        + [pl.BlockSpec((1, 16, BLK), lambda k: (0, 0, 0))] * 3,
        out_specs=pl.BlockSpec((8, BLK), lambda k: (0, 0)),
        scratch_shapes=[pltpu.VMEM((4, 8, BLK), f32)],
        compiler_params=params(),
        cost_estimate=cost(1000, 50_000),
        name="gain_along_y",
    )(ids, *after, gain, *low)


def join_kernel(ids, _, a0, ra, rb, got, keep, swapped, b1, b2, b3, out):
    for side in range(2):
        cols = pl.ds(pl.multiple_of((ids[4] ^ side) * BLK, BLK), BLK)
        total = a0[0, side].astype(f32) + ra[0, side].astype(f32) + rb[0, side].astype(f32) + got[side].astype(f32)
        out[0:ROWS_A, cols] = total.astype(bf16)
        total = keep[0, side].astype(f32) + swapped[0, side].astype(f32)
        for b in (b1, b2, b3):
            total = total + b[side, 16:, :].astype(f32)
        out[ROWS_A:TERMS, cols] = total.astype(bf16)


def join(ids, after, *parts):
    return pl.pallas_call(
        join_kernel,
        out_shape=jax.ShapeDtypeStruct((TERMS, 2 * BLK), bf16),
        in_specs=[SMEM, ANY] + [VMEM] * len(parts),
        out_specs=VMEM,
        compiler_params=params(),
        cost_estimate=cost(1000, 8_000_000),
        name="join",
    )(ids, after, *parts)


ROWS_T = HALF + 16


def term_step(steps, n):
    step = steps[0]
    for i in range(1, len(steps)):
        step = jnp.where(n < i, step, steps[i])
    return step


def term_kernel(n_steps, split, n_adds, ids, h, w0, w1, dots, *refs):
    n = pl.program_id(0)
    crossed, adds, outs = refs[: n_adds[0]], refs[n_adds[0] : sum(n_adds)], refs[sum(n_adds) :]
    weights = jnp.concatenate([w0[...], w1[...]], axis=1)
    for half in range(2):
        total = jnp.dot(h[half * HALF : (half + 1) * HALF, :], weights, preferred_element_type=f32)
        tail = jnp.concatenate([dots[half * 8 : half * 8 + 8, :], jnp.zeros((8, BLK), f32)], axis=0)
        for m in range(2):
            share = jnp.concatenate([total[:, m * BLK : (m + 1) * BLK], tail], axis=0)
            for ref in crossed:
                share = share + ref[0, half, m].astype(f32)
            if adds:
                got = adds[half][m].astype(f32)
                share = share + jnp.where(n == half, got, 0.0)
            if split:
                outs[half][m] = share.astype(bf16)
            elif len(outs) == 1:
                outs[0][0, half, m] = share.astype(bf16)
            else:
                for i in range(n_steps):

                    @pl.when(n == i)
                    def _(i=i, half=half, m=m, share=share):
                        outs[i][half, m] = share.astype(bf16)


def term_part(ids, steps, side, h, wt, dots, after, split=False, apart=False, crossed=(), adds=(), weight=0.02):
    block = pl.BlockSpec((1, 2, 2, ROWS_T, BLK), lambda n, s: (n, 0, 0, 0, 0))
    part = pl.BlockSpec((2, ROWS_T, BLK), lambda n, s: (0, 0, 0))
    sides = [
        pl.BlockSpec(
            (TERMS, BLK), lambda n, s, m=m: (0, ((s[2] ^ m) * 4 + ((s[3] + term_step(steps, n)) & 3)) * 2 + (s[4] ^ side))
        )
        for m in range(2)
    ]
    count = len(steps)
    outs, specs = [jax.ShapeDtypeStruct((count, 2, 2, ROWS_T, BLK), bf16)], [block]
    if split:
        outs, specs = [jax.ShapeDtypeStruct((2, ROWS_T, BLK), bf16)] * 2, [part] * 2
    elif apart:
        outs = [jax.ShapeDtypeStruct((2, 2, ROWS_T, BLK), bf16)] * count
        specs = [pl.BlockSpec((2, 2, ROWS_T, BLK), lambda n, s: (0, 0, 0, 0))] * count
    return pl.pallas_call(
        later(len(after), functools.partial(term_kernel, count, split, (len(crossed), len(adds)))),
        out_shape=outs,
        grid_spec=pltpu.PrefetchScalarGridSpec(
            num_scalar_prefetch=1,
            grid=(count,),
            in_specs=[ANY] * len(after)
            + [pl.BlockSpec((TOK, TERMS), lambda n, s: (0, 0)), *sides]
            + [pl.BlockSpec((16, BLK), lambda n, s: (0, 0))]
            + [block] * len(crossed)
            + [part] * len(adds),
            out_specs=specs,
        ),
        compiler_params=params(),
        cost_estimate=cost(
            4 * count * TOK * BLK * TERMS, 2 * TOK * TERMS + 2 * count * BLK * (2 * TERMS + 4 * TOK), weight
        ),
        name="term_part",
    )(ids, *after, h, wt, wt, dots, *crossed, *adds)


def term_sum_kernel(own, ra, rb, x, x_p, keep, send, dots, gain):
    sums = [jnp.zeros((8, BLK), f32) for _ in range(2)]
    for half in range(2):
        for m, values in ((0, x), (1, x_p)):
            for first in range(0, ROWS_T, 128):
                rows = slice(first, min(first + 128, ROWS_T))
                total = own[half, m, rows, :].astype(f32)
                for ref in (ra, rb):
                    total = total + ref[half, m, rows, :].astype(f32)
                if m:
                    send[half, rows, :] = total.astype(bf16)
                elif first < HALF:
                    keep[half * HALF + first : half * HALF + first + 128, :] = total.astype(bf16)
                else:
                    dots[half * 8 : half * 8 + 8, :] = total[:8]
                if first < HALF:
                    at = half * HALF + first
                    product = total * values[at : at + 128, :].astype(f32)
                    sums[m] = sums[m] + jnp.sum(product.reshape(16, 8, BLK), axis=0)
    for m in range(2):
        gain[m : m + 1, :] = jnp.sum(sums[m], axis=0, keepdims=True)


def term_sum(after, own, ra, rb, x, x_p):
    count = len(after)
    return pl.pallas_call(
        lambda *refs: term_sum_kernel(*refs[count:]),
        out_shape=[
            jax.ShapeDtypeStruct((TOK, BLK), bf16),
            jax.ShapeDtypeStruct((2, ROWS_T, BLK), bf16),
            jax.ShapeDtypeStruct((16, BLK), f32),
            jax.ShapeDtypeStruct((2, BLK), f32),
        ],
        in_specs=[ANY] * count + [VMEM] * 5,
        out_specs=[VMEM] * 4,
        compiler_params=params(),
        cost_estimate=cost(1_000_000, 5_000_000),
        name="term_sum",
    )(*after, own, ra, rb, x, x_p)


def final_kernel(ids, n_ref, got, x_ref, gain, inv_ref, dots, out):
    g = gain[:, block_at(ids, ids[2] * 4 + ids[3], 0)]
    for half in range(2):
        lines = (dots[half * 8 : half * 8 + 8, :] + got[half, HALF:, :].astype(f32)[:8]) / D
        for k in range(4):
            local = slice(k * LEN, (k + 1) * LEN)
            rows = slice(half * HALF + k * LEN, half * HALF + (k + 1) * LEN)
            grad = n_ref[rows, :].astype(f32) + got[half, local, :].astype(f32)
            values = x_ref[rows, :].astype(f32)
            line = lines[k // 2 : k // 2 + 1, (k % 2) * LEN : (k % 2 + 1) * LEN]
            column = jnp.broadcast_to(line, (LEN, LEN)).T[:, 0:1]
            inverse = inv_ref[rows, :]
            out[rows, :] = (grad * g - values * (inverse * inverse * column)).astype(bf16)


def final(ids, after, n, got, x, gain, inv, dots):
    return pl.pallas_call(
        later(len(after), final_kernel),
        out_shape=jax.ShapeDtypeStruct((TOK, BLK), bf16),
        in_specs=[SMEM] + [ANY] * len(after) + [VMEM] * 6,
        out_specs=VMEM,
        compiler_params=params(),
        cost_estimate=cost(1_000_000, 2_000_000),
        name="hidden_grad",
    )(ids, *after, n, got, x, gain, inv, dots)


def shards(hidden, norm_gain, head_weight, lengths, positives, negatives):
    xh, y, xl, z, c = (lax.axis_index(a).astype(jnp.int32) for a in ("xh", "y", "xl", "z", "c"))
    nil = jnp.int32(0)
    ids = jnp.concatenate([jnp.stack([xh, y, xl, z, c, nil, nil, nil]), positives, negatives.reshape(-1)])
    wt = head_weight.T
    gain = norm_gain.reshape(1, D)

    z_m, z_p, x_p = shift(hidden, "z", 1), shift(hidden, "z", -1), swap(hidden, "xl")
    own_c = swap(hidden, "c")
    z_m_c, z_p_c, x_p_c = (swap(a, "c") for a in (z_m, z_p, x_p))
    far, xz_p, xz_m = shift(z_m, "z", 1), shift(x_p, "z", -1), swap(z_m, "xl")
    state = forward(ids, [(0, 0), (0, -1), (1, 0)], [hidden, own_c, z_m, z_m_c, x_p, x_p_c], wt, gain)
    far, xz_p, xz_m = touch(state[1], far, xz_p, xz_m)
    last = swap(far, "xl")
    far_c, xz_p_c, xz_m_c = (swap(a, "c") for a in (far, xz_p, xz_m))
    state = forward(
        ids,
        [(0, 1), (0, 2), (1, 1), (1, -1)],
        [z_p, z_p_c, far, far_c, xz_p, xz_p_c, xz_m, xz_m_c],
        wt,
        gain,
        state,
    )
    (last,) = touch(state[1], last)
    last_c = swap(last, "c")
    acc, x, inv, weight, pooled = forward_last(ids, lengths, (1, 2), (last, last_c), wt, gain, state)

    pair = jnp.stack([pooled, swap(pooled, "xh")])
    every, part = gram(ids, [pair] + [swap(pair, "y", bits) for bits in (1, 2, 3)])
    part = (part + swap(part, "z", 1)) + (swap(part, "z", 2) + swap(part, "z", 3))
    both = lax.ppermute(part, ("xl", "c"), [(i, i ^ 3) for i in range(4)])
    parts = (part, swap(part, "c"), swap(part, "xl"), both)
    h, ht, dots, losses = grads(ids, every, parts, weight, acc)

    (crossing_2,) = term_part(ids, (2,), 1, h, wt, dots, ())
    (crossing,) = term_part(ids, (1, 3, 0), 1, h, wt, dots, (crossing_2,), weight=20)
    crossed_2, crossed = swap(crossing_2, "c"), swap(crossing, "c")
    term_0, term_1 = term_part(ids, (2,), 0, h, wt, dots, (crossing,), split=True, crossed=(crossed_2,))
    far_0, far_1, keep_2, send_2 = head_part(ids, (2,), ht, x, gain, (term_0,), split=True, weight=20)
    swap_2 = swap(send_2, "xh")
    adds = (shift(term_0, "z", 1), shift(term_1, "z", -1))
    t_1, t_3, t_0 = term_part(
        ids, (1, 3, 0), 0, h, wt, dots, (far_0,), apart=True, crossed=(crossed,), adds=adds, weight=20
    )
    adds = (shift(far_0, "y", 1), shift(far_1, "y", -1))
    a_1, a_3, keep_13, send_13 = head_part(ids, (1, 3), ht, x, gain, (t_0, swap_2), adds=adds, weight=20)
    swap_13 = swap(send_13, "xh")
    ra, rb = shift(a_1, "y", 1), shift(a_3, "y", -1)
    keep, send, dots, partial = term_sum((), t_0, shift(t_1, "z", 1), shift(t_3, "z", -1), hidden, x_p)
    a_0, keep_0, send_0 = head_part(ids, (0,), ht, x, gain, (a_1, keep), weight=20)
    swap_0 = swap(send_0, "xh")
    got = swap(a_0[1] + ra[1] + rb[1], "xh")
    low_1, low_3, low_2 = low_sum(swap_0, partial, keep_13, swap_13, keep_2, swap_2)
    low = [shift(low_1, "y", 1), shift(low_2, "y", 2), shift(low_3, "y", 3)]
    hidden_grad = final(ids, (), keep, swap(send, "xl"), hidden, gain, inv, dots)
    gain_grad = gain_along_y(ids, (hidden_grad, swap_0), partial, *low)
    both = lax.ppermute(gain_grad, ("xh", "xl"), [(i, i ^ 3) for i in range(4)])
    gain_grad = (gain_grad[0] + swap(gain_grad, "xh")[0]) + (swap(gain_grad, "xl")[1] + both[1])
    head_t = join(ids, hidden_grad, a_0, ra, rb, got, keep_0, swap_0, *low)
    return losses[0, :3], hidden_grad, head_t.T, gain_grad


def solution(mesh):
    fine = Mesh(mesh.devices.reshape(2, 4, 2, 4, 2), ("xh", "y", "xl", "z", "c"))
    dp, vocab = ("xh", "y"), ("xl", "z", "c")
    in_specs = (P(dp, vocab), P(), P(None, vocab), P(dp), P(dp), P(dp, None))
    out_specs = (P(), P(dp, vocab), P(dp, vocab), P(vocab))
    return jax.shard_map(shards, mesh=fine, in_specs=in_specs, out_specs=out_specs, check_vma=False)
```
